128 devices in a mesh: wide: 16 (over y_hi, x, core), narrow: 8 (over z, y_lo).
Axes of the slice: x: 4, y: 4 (y_hi: 2, y_lo: 2; y = y_hi * 2 + y_lo), z: 4, core: 2. Of those that a mesh axis runs over, the one named last changes fastest.
Arguments:
- right_side: float32 [3, 128, 512, 256], P(None, 'wide', 'narrow'), may hold values from -6 to 6
- start_guess: float32 [3, 128, 512, 256], P(None, 'wide', 'narrow'), may hold values from -6 to 6
- reaction: float32 [128, 512, 256], P('wide', 'narrow'), may hold values from 2.5 to 5
- coarse_reaction: float32 [64, 256, 128], P('wide'), may hold values from 2.5 to 5
- rest_x: float32 [64, 5], replicated, may hold values from 0.1 to 0.8
- rest_y: float32 [256, 5], replicated, may hold values from 0.1 to 0.8
- rest_z: float32 [128, 5], replicated, may hold values from 0.1 to 0.8
- fine_bounds: float32 [2], replicated, may hold values from 3 to 20, as said below
- coarse_bounds: float32 [2], replicated, may hold values from 0.8 to 20, as said below
Outputs:
- solution: float32 [3, 128, 512, 256], P(None, 'wide', 'narrow')
- coarse_correction: float32 [3, 64, 256, 128], P(None, 'wide')
The draws below stay inside these ranges and needn't reach their ends.
Inputs may be any that keep to these rules, and one draw needn't show every extreme that they name: fine_bounds[1] lies above every eigenvalue of the fine operator and fine_bounds[0] below fine_bounds[1]. coarse_bounds[1] lies above every eigenvalue of the coarse operator and coarse_bounds[0] below coarse_bounds[1].
All inputs are finite; a program needn't handle non-finite values.
Results may differ from the reference program's by a relative error of at most 0.0003.
Values sent between devices are 32-bit elements; how exact they have to be, the bound alone decides.
No kernel may reach another device: no remote copies, remote signals or barrier semaphores. Data moves between devices by JAX's collectives and lax.ppermute only.
A program may use at most 128 MiB of HBM per device.

```python
import math
import jax
import jax.numpy as jnp
from jax import lax

NZ = 256
FINE_STEPS = 2
COARSE_STEPS = 4
NX = 128
NY = 512
NXC = 64
NYC = 256
NZC = 128


def draw_fine_bounds(key, part):
    key = jax.random.fold_in(key, 11)
    first_key, second_key = jax.random.split(key)
    upper = jax.random.uniform(first_key, (), jnp.float32, 18.0, 20.0)
    lower = jax.random.uniform(second_key, (), jnp.float32, 3.0, 5.0)
    return jnp.stack([lower, upper])


def draw_coarse_bounds(key, part):
    key = jax.random.fold_in(key, 23)
    first_key, second_key = jax.random.split(key)
    upper = jax.random.uniform(first_key, (), jnp.float32, 18.0, 20.0)
    lower = jax.random.uniform(second_key, (), jnp.float32, 0.8, 1.6)
    return jnp.stack([lower, upper])


def steps_of(stream_key, shape, cuts, least, largest):
    factor_of, own = 1.0, jax.random.fold_in(stream_key, 6)
    for position, shards_of in cuts:
        heights = jnp.exp(jax.random.uniform(jax.random.fold_in(own, position), (shards_of,), jnp.float32, least / len(cuts), largest / len(cuts)))
        factor_of = factor_of * jnp.repeat(heights, shape[position] // shards_of).reshape([-1 if axis == position else 1 for axis in range(len(shape))])
    return factor_of


def noise(stream_key, dims, width, bound, shards=(), kind=jnp.bfloat16):
    drawn = width * jax.random.normal(stream_key, dims, jnp.float32)
    if shards:
        drawn = drawn * steps_of(stream_key, dims, shards, -0.22, 0.18)
    return jnp.clip(drawn, -bound, bound).astype(kind)


def setup_inputs(seed: int = 0) -> dict:
    seeds = jax.random.split(jax.random.key(seed), 10)
    right_side = noise(seeds[0], (3, NX, NY, NZ), 1.0, 6.0, ((1, 16), (2, 8)), jnp.float32)
    start_guess = noise(seeds[1], (3, NX, NY, NZ), 1.0, 6.0, ((1, 16), (2, 8)), jnp.float32)
    reaction = jnp.clip(2.5 + 2.5 * jax.random.uniform(seeds[2], (NX, NY, NZ), jnp.float32) ** steps_of(seeds[2], (NX, NY, NZ), ((0, 16), (1, 8)), -0.2, 0.2), 2.5, 5.0)
    coarse_reaction = jnp.clip(2.5 + 2.5 * jax.random.uniform(seeds[3], (NXC, NYC, NZC), jnp.float32) ** steps_of(seeds[3], (NXC, NYC, NZC), ((0, 16),), -0.2, 0.2), 2.5, 5.0)
    rest_x = jnp.clip(jnp.exp(jax.random.uniform(seeds[4], (NXC, 5), jnp.float32, math.log(0.1), math.log(0.8))), 0.1, 0.8)
    rest_y = jnp.clip(jnp.exp(jax.random.uniform(seeds[5], (NYC, 5), jnp.float32, math.log(0.1), math.log(0.8))), 0.1, 0.8)
    rest_z = jnp.clip(jnp.exp(jax.random.uniform(seeds[6], (NZC, 5), jnp.float32, math.log(0.1), math.log(0.8))), 0.1, 0.8)
    fine_bounds = draw_fine_bounds(jax.random.fold_in(seeds[9], 71), 0)
    coarse_bounds = draw_coarse_bounds(jax.random.fold_in(seeds[9], 71), 0)
    return dict(right_side=right_side, start_guess=start_guess, reaction=reaction, coarse_reaction=coarse_reaction, rest_x=rest_x, rest_y=rest_y, rest_z=rest_z, fine_bounds=fine_bounds, coarse_bounds=coarse_bounds)


COUPLING = 0.5


def expand(values, which, rank_count):
    new_shape = [1] * rank_count
    new_shape[which] = values.shape[0]
    return values.reshape(new_shape)


def shifted(padded, along_x, along_y, along_z):
    size_x = padded.shape[1] - 2
    size_y = padded.shape[2] - 2
    size_z = padded.shape[3] - 2
    return padded[:, 1 + along_x:1 + along_x + size_x, 1 + along_y:1 + along_y + size_y, 1 + along_z:1 + along_z + size_z]


def stencil(padded, coef):
    centre = shifted(padded, 0, 0, 0)
    neighbours = shifted(padded, 1, 0, 0) + shifted(padded, -1, 0, 0)
    neighbours = neighbours + shifted(padded, 0, 1, 0) + shifted(padded, 0, -1, 0)
    neighbours = neighbours + shifted(padded, 0, 0, 1) + shifted(padded, 0, 0, -1)
    diagonal_part = (6.0 + coef)[None] * centre - neighbours
    cross_xy = 0.25 * (shifted(padded, 1, 1, 0) - shifted(padded, 1, -1, 0) - shifted(padded, -1, 1, 0) + shifted(padded, -1, -1, 0))
    cross_xz = 0.25 * (shifted(padded, 1, 0, 1) - shifted(padded, 1, 0, -1) - shifted(padded, -1, 0, 1) + shifted(padded, -1, 0, -1))
    cross_yz = 0.25 * (shifted(padded, 0, 1, 1) - shifted(padded, 0, 1, -1) - shifted(padded, 0, -1, 1) + shifted(padded, 0, -1, -1))
    first_row = diagonal_part[0] + COUPLING * (cross_xy[1] + cross_xz[2])
    second_row = diagonal_part[1] + COUPLING * (cross_xy[0] + cross_yz[2])
    third_row = diagonal_part[2] + COUPLING * (cross_xz[0] + cross_yz[1])
    return jnp.stack([first_row, second_row, third_row], 0)


def chebyshev(operator, iterate, residual, bounds, sweeps, residual_needed):
    middle = (bounds[1] + bounds[0]) / 2.0
    radius = (bounds[1] - bounds[0]) / 2.0
    stretch = middle / radius
    ratio_now = 1.0 / stretch
    direction = residual / middle
    for iteration in range(sweeps):
        iterate = iterate + direction
        if iteration < sweeps - 1 or residual_needed:
            residual = residual - operator(direction)
        if iteration < sweeps - 1:
            ratio_next = 1.0 / (2.0 * stretch - ratio_now)
            direction = ratio_next * ratio_now * direction + (2.0 * ratio_next / radius) * residual
            ratio_now = ratio_next
    return iterate, residual


def restrict_padded(padded, weights, which):
    coarse_count = weights.shape[0]
    total = None
    for offset in range(5):
        piece = lax.slice_in_dim(padded, offset, offset + 2 * coarse_count - 1, 2, which)
        weighted = expand(weights[:, offset], which, padded.ndim) * piece
        total = weighted if total is None else total + weighted
    return total


def restrict_axis(source, weights, which):
    widths = [(0, 0)] * source.ndim
    widths[which] = (2, 2)
    return restrict_padded(jnp.pad(source, widths), weights, which)


def prolong_axis(source, weights, which):
    weighted = [expand(weights[:, offset], which, source.ndim) * source for offset in range(5)]

    def shifted_pad(piece, before, after):
        widths = [(0, 0)] * piece.ndim
        widths[which] = (before, after)
        return jnp.pad(piece, widths)

    even_part = shifted_pad(weighted[0], 0, 2) + shifted_pad(weighted[2], 1, 1) + shifted_pad(weighted[4], 2, 0)
    odd_part = shifted_pad(weighted[1], 0, 2) + shifted_pad(weighted[3], 1, 1)
    paired = jnp.stack([even_part, odd_part], axis=which + 1)
    new_shape = list(even_part.shape)
    new_shape[which] = new_shape[which] * 2
    return paired.reshape(new_shape)


def pad_all(operand):
    return jnp.pad(operand, ((0, 0), (1, 1), (1, 1), (1, 1)))


def reference(right_side, start_guess, reaction, coarse_reaction, rest_x, rest_y, rest_z, fine_bounds, coarse_bounds):
    def fine_operator(operand):
        return stencil(pad_all(operand), reaction)

    def coarse_operator(operand):
        return stencil(pad_all(operand), coarse_reaction)

    fine_residual = right_side - fine_operator(start_guess)
    smooth, fine_residual = chebyshev(fine_operator, start_guess, fine_residual, fine_bounds, FINE_STEPS, True)
    coarse_rhs = restrict_axis(fine_residual, rest_z, 3)
    coarse_rhs = restrict_axis(coarse_rhs, rest_x, 1)
    coarse_rhs = restrict_axis(coarse_rhs, rest_y, 2)
    correction, unused = chebyshev(coarse_operator, jnp.zeros_like(coarse_rhs), coarse_rhs, coarse_bounds, COARSE_STEPS, False)
    grown_back = prolong_axis(correction, rest_x, 1)[:, 2:2 + NX]
    grown_back = prolong_axis(grown_back, rest_y, 2)[:, :, 2:2 + NY]
    grown_back = prolong_axis(grown_back, rest_z, 3)[:, :, :, 2:2 + NZ]
    return smooth + grown_back, correction
```

```python
import jax
import jax.numpy as jnp
from jax import lax
from jax.experimental import pallas as pl
from jax.experimental.pallas import tpu as pltpu
from jax.sharding import PartitionSpec as P

F32 = jnp.float32
LANES = 128
SUB = 8
RIM = 4
PAD = 8
VMEM_LIMIT = 48 * 1024 * 1024


def params():
    return pltpu.CompilerParams(vmem_limit_bytes=VMEM_LIMIT)


def swap_near(x, axis):
    count = lax.axis_size(axis)
    return lax.ppermute(x, axis, [(i, i ^ 1) for i in range(count)])


def swap_far(x, axis):
    count = lax.axis_size(axis)
    up = [(i, i + 1) for i in range(1, count - 1, 2)]
    return lax.ppermute(x, axis, up + [(j, i) for i, j in up])


def is_even(axis):
    return lax.rem(lax.axis_index(axis), 2) == 0


def lane_index():
    return lax.broadcasted_iota(jnp.int32, (SUB, LANES), 1)


def z_next(parts, last):
    rolled = [pltpu.roll(part, LANES - 1, 1) for part in parts]
    beyond = rolled[1:] + [jnp.zeros_like(parts[0])]
    return [jnp.where(last, b, r) for r, b in zip(rolled, beyond)]


def z_before(parts, first):
    rolled = [pltpu.roll(part, 1, 1) for part in parts]
    beyond = [jnp.zeros_like(parts[0])] + rolled[:-1]
    return [jnp.where(first, b, r) for r, b in zip(rolled, beyond)]


def each(fn, *lists):
    return [fn(*items) for items in zip(*lists)]


def add(a, b):
    return each(lambda p, q: p + q, a, b)


def sub(a, b):
    return each(lambda p, q: p - q, a, b)


def eighth(a):
    return each(lambda p: 0.125 * p, a)


class Plane:
    def __init__(self, load, edges):
        first, last = edges
        v = [load(c, 0) for c in range(3)]
        above = [load(c, 1) for c in range(3)]
        below = [load(c, -1) for c in range(3)]
        dy = [eighth(sub(above[c], below[c])) for c in range(3)]
        next_0, before_0 = z_next(v[0], last), z_before(v[0], first)
        next_2, before_2 = z_next(v[2], last), z_before(v[2], first)
        slope = [
            add(dy[1], eighth(sub(next_2, before_2))),
            dy[0],
            eighth(sub(next_0, before_0)),
        ]
        self.v = v
        self.ahead = [add(v[c], slope[c]) for c in range(3)]
        self.behind = [sub(v[c], slope[c]) for c in range(3)]
        self.parts = (above, below, dy, next_0, before_0, edges)

    def inner(self, diagonal):
        above, below, dy, next_0, before_0, (first, last) = self.parts
        v = self.v
        out = []
        for c in range(3):
            if c == 0:
                along_z = add(next_0, before_0)
            else:
                other = dy[2] if c == 1 else dy[1]
                along_z = add(
                    z_next(sub(v[c], other), last), z_before(add(v[c], other), first)
                )
            total = add(add(above[c], below[c]), along_z)
            out.append(each(lambda d, p, q: d * p - q, diagonal, v[c], total))
        return out


def applied(before, plane, after, diagonal):
    out = plane.inner(diagonal)
    for c in range(3):
        if after is not None:
            out[c] = sub(out[c], after.behind[c])
        if before is not None:
            out[c] = sub(out[c], before.ahead[c])
    return out


def edge_masks():
    lane = lane_index()
    return lane == 0, lane == LANES - 1


def inside_rows(start, own, axis):
    row = start + lax.broadcasted_iota(jnp.int32, (SUB, LANES), 0)
    place = lax.axis_index(axis)
    low = jnp.where(place == 0, RIM, 0)
    high = jnp.where(place == lax.axis_size(axis) - 1, RIM + own, own + 2 * RIM)
    return (row >= low) & (row < high)


def pack_y_kernel(u_lo, u_hi, b_lo, b_hi, s_lo, s_hi, near, far):
    width = u_lo.shape[1]

    def pack(out, u, b, s, low):
        u_rows = slice(0, 3) if low else slice(5, 8)
        two = slice(0, 2) if low else slice(6, 8)
        for h in range(2):
            lanes = slice(h * LANES, (h + 1) * LANES)
            for x in range(width):
                for c in range(3):
                    k = c * width + x
                    out[h, 3 * k : 3 * k + 3, :] = u[c, x, u_rows, lanes]
                    base = 9 * width + 2 * k
                    out[h, base : base + 2, :] = b[c, x, two, lanes]
                base = 15 * width + 2 * x
                out[h, base : base + 2, :] = s[x, two, lanes]

    even = is_even("narrow")

    @pl.when(even)
    def _():
        pack(near, u_hi, b_hi, s_hi, False)
        pack(far, u_lo, b_lo, s_lo, True)

    @pl.when(jnp.logical_not(even))
    def _():
        pack(near, u_lo, b_lo, s_lo, True)
        pack(far, u_hi, b_hi, s_hi, False)


def pack_y(u, b, s):
    _, width, height, depth = u.shape
    last = height // SUB - 1
    block = pl.BlockSpec((3, width, SUB, depth), lambda i: (0, 0, 0, 0))
    block_last = pl.BlockSpec((3, width, SUB, depth), lambda i: (0, 0, last, 0))
    plane = pl.BlockSpec((width, SUB, depth), lambda i: (0, 0, 0))
    plane_last = pl.BlockSpec((width, SUB, depth), lambda i: (0, last, 0))
    rows = 17 * width
    out = jax.ShapeDtypeStruct((2, rows, LANES), F32)
    whole = pl.BlockSpec((2, rows, LANES), lambda i: (0, 0, 0))
    return pl.pallas_call(
        pack_y_kernel,
        grid=(1,),
        in_specs=[block, block_last, block, block_last, plane, plane_last],
        out_specs=[whole, whole],
        out_shape=[out, out],
        compiler_params=params(),
        name="pack_y",
    )(u, u, b, b, s, s)


def residual_kernel(u, b, s, got_near, got_far, r0, s_ext, near, far, ue, be):
    _, width, height, _ = u.shape
    own = PAD + RIM
    tiles = (height + 2 * RIM) // SUB
    for h in range(2):
        lanes = slice(h * LANES, (h + 1) * LANES)

        def fill(t, carry, h=h, lanes=lanes):
            rows = pl.ds(pl.multiple_of(t * SUB, SUB), SUB)
            to = pl.ds(own + t * SUB, SUB)
            for x in range(width):
                for c in range(3):
                    ue[c, x, h, to, :] = u[c, x, rows, lanes]
                    be[c, x, h, to, :] = b[c, x, rows, lanes]
                s_ext[x, h, to, :] = s[x, rows, lanes]
            return carry

        lax.fori_loop(0, height // SUB, fill, 0)

    def place(low, high):
        for h in range(2):
            for x in range(width):
                for c in range(3):
                    k = c * width + x
                    ue[c, x, h, own - 3 : own, :] = low[h, 3 * k : 3 * k + 3, :]
                    ue[c, x, h, own + height : own + height + 3, :] = high[h, 3 * k : 3 * k + 3, :]
                    base = 9 * width + 2 * k
                    be[c, x, h, own - 2 : own, :] = low[h, base : base + 2, :]
                    be[c, x, h, own + height : own + height + 2, :] = high[h, base : base + 2, :]
                base = 15 * width + 2 * x
                s_ext[x, h, own - 2 : own, :] = low[h, base : base + 2, :]
                s_ext[x, h, own + height : own + height + 2, :] = high[h, base : base + 2, :]

    even = is_even("narrow")

    @pl.when(even)
    def _():
        place(got_far, got_near)

    @pl.when(jnp.logical_not(even))
    def _():
        place(got_near, got_far)

    edges = edge_masks()

    def step(t, carry):
        start = PAD + t * SUB
        inside = inside_rows(t * SUB, height, "narrow")

        def plane(x):
            return Plane(
                lambda c, dy: [ue[c, x, h, pl.ds(start + dy, SUB), :] for h in range(2)],
                edges,
            )

        before, here = None, plane(0)
        rows = pl.ds(start, SUB)
        for x in range(width):
            after = plane(x + 1) if x + 1 < width else None
            diagonal = [6.0 + s_ext[x, h, rows, :] for h in range(2)]
            au = applied(before, here, after, diagonal)
            for c in range(3):
                for h in range(2):
                    r0[c, x, h, rows, :] = jnp.where(inside, be[c, x, h, rows, :] - au[c][h], 0.0)
            before, here = here, after
        return carry

    lax.fori_loop(0, tiles, step, 0)

    window = slice(PAD, PAD + height + 2 * RIM)

    def pack(out, edge, second):
        for c in range(3):
            out[c] = r0[c, edge, :, window, :]
            out[3 + c] = r0[c, second, :, window, :]
            out[6 + c] = ue[c, edge, :, window, :]
        out[9] = s_ext[edge, :, window, :]

    even_x = is_even("wide")

    @pl.when(even_x)
    def _():
        pack(near, width - 1, width - 2)
        pack(far, 0, 1)

    @pl.when(jnp.logical_not(even_x))
    def _():
        pack(near, 0, 1)
        pack(far, width - 1, width - 2)


def residual(u, b, s, got_near, got_far):
    _, width, height, _ = u.shape
    padded = height + 2 * (RIM + PAD)
    side = jax.ShapeDtypeStruct((10, 2, height + 2 * RIM, LANES), F32)
    return pl.pallas_call(
        residual_kernel,
        out_shape=[
            jax.ShapeDtypeStruct((3, width, 2, padded, LANES), F32),
            jax.ShapeDtypeStruct((width, 2, padded, LANES), F32),
            side,
            side,
        ],
        scratch_shapes=[
            pltpu.VMEM((3, width, 2, padded, LANES), F32),
            pltpu.VMEM((3, width, 2, padded, LANES), F32),
        ],
        compiler_params=params(),
        name="residual",
    )(u, b, s, got_near, got_far)


def full(value):
    return jnp.full((SUB, LANES), value, F32)


def chebyshev_numbers(bounds, steps):
    low, high = full(bounds[0]), full(bounds[1])
    middle = (high + low) / 2.0
    radius = (high - low) / 2.0
    stretch = middle / radius
    rho = 1.0 / stretch
    factors = []
    for _ in range(steps - 1):
        rho_next = 1.0 / (2.0 * stretch - rho)
        factors.append((rho_next * rho, 2.0 * rho_next / radius))
        rho = rho_next
    return 1.0 / middle, factors


def z_matrix(rest_zt):
    shape = (2 * LANES, LANES)
    offset = lax.broadcasted_iota(jnp.int32, shape, 0) - 2 * lax.broadcasted_iota(jnp.int32, shape, 1) + 2
    out = jnp.zeros(shape, F32)
    for a in range(5):
        out = out + jnp.where(offset == a, rest_zt[a : a + 1, :], 0.0)
    return out


def y_weights(rest_y, a, rows, own):
    start = pl.multiple_of(lax.axis_index("narrow") * own, SUB)
    return jnp.broadcast_to(rest_y[pl.ds(start, rows), a : a + 1], (rows, LANES))


def smooth_kernel(
    bounds, rest_x, r0p, s_ext, got_near, got_far, sent_near, sent_far, u, rest_y, rest_zt,
    smooth, partial, near, far, left, right, u_left, u_right, r0, d1, r1, r2, t_pad, zr,
):
    _, width, height, _ = u.shape
    window = slice(PAD, PAD + height + 2 * RIM)
    tiles = (height + 2 * RIM) // SUB
    even_x = is_even("wide")
    zr[...] = z_matrix(rest_zt)

    def place(from_left, from_right, mine_left, mine_right):
        for k in range(10):
            left[k, :, window, :] = from_left[k]
            right[k, :, window, :] = from_right[k]
        for c in range(3):
            u_left[c, :, window, :] = mine_left[6 + c]
            u_right[c, :, window, :] = mine_right[6 + c]

    @pl.when(even_x)
    def _():
        place(got_far, got_near, sent_far, sent_near)

    @pl.when(jnp.logical_not(even_x))
    def _():
        place(got_near, got_far, sent_near, sent_far)

    edges = edge_masks()
    place_x = lax.axis_index("wide")
    has_left = place_x > 0
    has_right = place_x < lax.axis_size("wide") - 1
    inverse, factors = chebyshev_numbers(bounds, 2)
    factor_d = factors[0][0] * inverse
    factor_r = factors[0][1]

    def fix(t, carry):
        start = PAD + t * SUB
        rows = pl.ds(start, SUB)
        inside = inside_rows(t * SUB, height, "narrow")

        def plane(ref, first):
            return Plane(
                lambda c, dy: [ref[first + c, h, pl.ds(start + dy, SUB), :] for h in range(2)],
                edges,
            )

        out_left = plane(left, 6)
        in_left = plane(u_left, 0)
        in_right = plane(u_right, 0)
        out_right = plane(right, 6)
        inside_left = inside & has_left
        inside_right = inside & has_right
        for c in range(3):
            for h in range(2):
                for x in range(1, width - 1):
                    r0[c, 2 + x, h, rows, :] = r0p[c, x, h, rows, :]
                r0[c, 0, h, rows, :] = left[3 + c, h, rows, :]
                r0[c, 1, h, rows, :] = jnp.where(
                    inside_left, left[c, h, rows, :] + in_left.behind[c][h], 0.0
                )
                r0[c, 2, h, rows, :] = jnp.where(
                    inside, r0p[c, 0, h, rows, :] + out_left.ahead[c][h], 0.0
                )
                r0[c, width + 1, h, rows, :] = jnp.where(
                    inside, r0p[c, width - 1, h, rows, :] + out_right.behind[c][h], 0.0
                )
                r0[c, width + 2, h, rows, :] = jnp.where(
                    inside_right, right[c, h, rows, :] + in_right.ahead[c][h], 0.0
                )
                r0[c, width + 3, h, rows, :] = right[3 + c, h, rows, :]
        return carry

    lax.fori_loop(0, tiles, fix, 0)

    def first_step(t, carry):
        start = PAD + t * SUB
        rows = pl.ds(start, SUB)
        inside = inside_rows(t * SUB, height, "narrow")

        def plane(x):
            return Plane(
                lambda c, dy: [r0[c, x + 2, h, pl.ds(start + dy, SUB), :] for h in range(2)],
                edges,
            )

        before, here = plane(-2), plane(-1)
        for x in range(-1, width + 1):
            after = plane(x + 1)
            keep = inside & has_left if x < 0 else inside & has_right if x == width else inside
            source = left.at[9] if x < 0 else right.at[9] if x == width else s_ext.at[x]
            diagonal = [6.0 + source[h, rows, :] for h in range(2)]
            ar = applied(before, here, after, diagonal)
            for c in range(3):
                for h in range(2):
                    old = here.v[c][h]
                    new = old - inverse * ar[c][h]
                    d1[c, x + 1, h, rows, :] = jnp.where(keep, factor_d * old + factor_r * new, 0.0)
                    if 0 <= x < width:
                        r1[c, x, h, rows, :] = new
            before, here = here, after
        return carry

    lax.fori_loop(0, tiles, first_step, 0)

    def second_step(t, carry):
        start = PAD + RIM + t * SUB
        rows = pl.ds(start, SUB)
        to = pl.ds(pl.multiple_of(t * SUB, SUB), SUB)

        def plane(x):
            return Plane(
                lambda c, dy: [d1[c, x + 1, h, pl.ds(start + dy, SUB), :] for h in range(2)],
                edges,
            )

        before, here = plane(-1), plane(0)
        for x in range(width):
            after = plane(x + 1)
            diagonal = [6.0 + s_ext[x, h, rows, :] for h in range(2)]
            ad = applied(before, here, after, diagonal)
            for c in range(3):
                for h in range(2):
                    lanes = slice(h * LANES, (h + 1) * LANES)
                    r2[c, x, h, to, :] = r1[c, x, h, rows, :] - ad[c][h]
                    step = inverse * r0[c, x + 2, h, rows, :] + here.v[c][h]
                    smooth[c, x, to, lanes] = u[c, x, to, lanes] + step
            before, here = here, after
        return carry

    lax.fori_loop(0, height // SUB, second_step, 0)

    coarse_width = width // 2
    coarse_height = height // 2
    coarse_rows = coarse_height + 2 * RIM
    first_weight = place_x * coarse_width
    lead = 2 * RIM + 2
    for c in range(3):
        for i in range(-1, coarse_width + 1):
            k = c * (coarse_width + 2) + i + 1
            terms = [(a, 2 * i - 2 + a) for a in range(5) if 0 <= 2 * i - 2 + a < width]
            halves = []
            for h in range(2):
                total = None
                for a, x in terms:
                    piece = rest_x[first_weight + i + 1, a] * r2[c, x, h]
                    total = piece if total is None else total + piece
                halves.append(total)
            joined = jnp.concatenate(halves, axis=1)
            t_pad[k, 0:lead, :] = jnp.zeros((lead, LANES), F32)
            t_pad[k, lead + height :, :] = jnp.zeros((t_pad.shape[1] - lead - height, LANES), F32)
            t_pad[k, lead : lead + height, :] = jnp.dot(
                joined, zr[...], precision=lax.Precision.HIGHEST, preferred_element_type=F32
            )
    weights = [y_weights(rest_y, a, coarse_rows, coarse_height) for a in range(5)]
    even_y = is_even("narrow")
    for c in range(3):
        for i in range(coarse_width + 2):
            k = c * (coarse_width + 2) + i
            total = None
            for a in range(5):
                piece = weights[a] * t_pad[k, pl.ds(a, coarse_rows, stride=2), :]
                total = piece if total is None else total + piece
            partial[c, i] = total

    def send(out, first):
        for c in range(3):
            for i in range(coarse_width + 2):
                out[c * (coarse_width + 2) + i] = partial[c, i, first : first + SUB, :]

    @pl.when(even_y)
    def _():
        send(near, coarse_rows - SUB)
        send(far, 0)

    @pl.when(jnp.logical_not(even_y))
    def _():
        send(near, 0)
        send(far, coarse_rows - SUB)


SMEM = pl.BlockSpec(memory_space=pltpu.SMEM)
VMEM = pl.BlockSpec(memory_space=pltpu.VMEM)


def smoothing(bounds, rest_x, r0p, s_ext, got_near, got_far, sent_near, sent_far, u, rest_y, rest_zt):
    _, width, height, depth = u.shape
    padded = height + 2 * (RIM + PAD)
    planes = 3 * (width // 2 + 2)
    coarse_rows = height // 2 + 2 * RIM
    tile = jax.ShapeDtypeStruct((planes, SUB, LANES), F32)

    def field(*lead):
        return pltpu.VMEM((*lead, 2, padded, LANES), F32)

    return pl.pallas_call(
        smooth_kernel,
        in_specs=[SMEM, SMEM] + [VMEM] * 9,
        out_shape=[
            jax.ShapeDtypeStruct((3, width, height, depth), F32),
            jax.ShapeDtypeStruct((3, width // 2 + 2, coarse_rows, LANES), F32),
            tile,
            tile,
        ],
        scratch_shapes=[
            field(10),
            field(10),
            field(3),
            field(3),
            field(3, width + 4),
            field(3, width + 2),
            field(3, width),
            pltpu.VMEM((3, width, 2, height, LANES), F32),
            pltpu.VMEM((planes, 2 * coarse_rows + 2 * SUB, LANES), F32),
            pltpu.VMEM((2 * LANES, LANES), F32),
        ],
        compiler_params=params(),
        name="smoothing",
    )(bounds, rest_x, r0p, s_ext, got_near, got_far, sent_near, sent_far, u, rest_y, rest_zt)


def rows_kernel(partial, got_near, got_far, s, q, s_win, near, far):
    _, planes, rows, _ = partial.shape
    own = rows - 2 * RIM
    coarse_width = planes - 2
    n = lax.axis_index("narrow")
    even_y = is_even("narrow")
    q[:, :, SUB : rows - SUB, :] = partial[:, :, SUB : rows - SUB, :]

    def join(low, high):
        for c in range(3):
            for i in range(planes):
                k = c * planes + i
                q[c, i, 0:SUB, :] = partial[c, i, 0:SUB, :] + low[k]
                q[c, i, rows - SUB :, :] = partial[c, i, rows - SUB :, :] + high[k]

    @pl.when(even_y)
    def _():
        join(got_far, got_near)

    @pl.when(jnp.logical_not(even_y))
    def _():
        join(got_near, got_far)

    total = s.shape[1]
    start = pl.multiple_of(n * own, SUB)
    before = pl.multiple_of(jnp.maximum(start - SUB, 0), SUB)
    after = pl.multiple_of(jnp.minimum(start + own, total - SUB), SUB)
    for x in range(coarse_width):
        s_win[x, RIM : RIM + own, :] = s[x, pl.ds(start, own), :]
        s_win[x, 0:RIM, :] = s[x, pl.ds(before, SUB), :][SUB - RIM :, :]
        s_win[x, RIM + own :, :] = s[x, pl.ds(after, SUB), :][0:RIM, :]

    def pack(out, to_left):
        first = 0 if to_left else 2
        for c in range(3):
            for k in range(coarse_width):
                out[c * coarse_width + k] = q[c, first + k]
        edge = 0 if to_left else coarse_width - 2
        for k in range(2):
            out[3 * coarse_width + k] = s_win[edge + k]

    even_x = is_even("wide")

    @pl.when(even_x)
    def _():
        pack(near, False)
        pack(far, True)

    @pl.when(jnp.logical_not(even_x))
    def _():
        pack(near, True)
        pack(far, False)


def rows(partial, got_near, got_far, s):
    _, planes, height, _ = partial.shape
    width = planes - 2
    side = jax.ShapeDtypeStruct((3 * width + 2, height, LANES), F32)
    return pl.pallas_call(
        rows_kernel,
        out_shape=[
            jax.ShapeDtypeStruct(partial.shape, F32),
            jax.ShapeDtypeStruct((width, height, LANES), F32),
            side,
            side,
        ],
        compiler_params=params(),
        name="coarse_rows",
    )(partial, got_near, got_far, s)


def coarse_kernel(bounds, q, s_win, got_near, got_far, out, own_out, near, far, left, right, r, d, total, sc):
    _, planes, height, _ = q.shape
    width = planes - 2
    own = height - 2 * RIM
    tiles = height // SUB
    window = slice(PAD, PAD + height)
    even_x = is_even("wide")
    place_x = lax.axis_index("wide")
    has_left = place_x > 0
    has_right = place_x < lax.axis_size("wide") - 1
    inverse, factors = chebyshev_numbers(bounds, 4)
    edges = edge_masks()
    reach = 3

    def place(from_left, from_right):
        left[...] = from_left[...]
        right[...] = from_right[...]

    @pl.when(even_x)
    def _():
        place(got_far, got_near)

    @pl.when(jnp.logical_not(even_x))
    def _():
        place(got_near, got_far)

    for k in range(2):
        sc[k] = left[3 * width + k]
        sc[width + 2 + k] = right[3 * width + k]
    for x in range(width):
        sc[x + 2] = s_win[x]

    def start_rows(t, carry):
        rows = pl.ds(pl.multiple_of(t * SUB, SUB), SUB)
        to = pl.ds(pl.multiple_of(PAD + t * SUB, SUB), SUB)
        for c in range(3):
            for i in range(-reach, width + reach):
                value = None
                if -1 <= i <= width:
                    value = q[c, i + 1, rows, :]
                if i <= 0:
                    other = left[c * width + i + reach, rows, :]
                    value = other if value is None else value + other
                if i >= width - 1:
                    other = right[c * width + i - width + 1, rows, :]
                    value = other if value is None else value + other
                r[c, i + reach, to, :] = value
                first = inverse * value
                d[c, i + reach, to, :] = first
                if 0 <= i < width:
                    total[c, i, to, :] = first
        return carry

    lax.fori_loop(0, tiles, start_rows, 0)

    for k in range(3):
        factor_d, factor_r = factors[k]
        rim = reach - 1 - k

        def residual_step(t, carry, rim=rim):
            start = PAD + t * SUB
            rows = pl.ds(start, SUB)
            inside = inside_rows(t * SUB, own, "narrow")

            def plane(x):
                return Plane(lambda c, dy: [d[c, x + reach, pl.ds(start + dy, SUB), :]], edges)

            before, here = plane(-rim - 1), plane(-rim)
            for x in range(-rim, width + rim):
                after = plane(x + 1)
                keep = inside & has_left if x < 0 else inside & has_right if x >= width else inside
                ad = applied(before, here, after, [6.0 + sc[x + 2, pl.ds(t * SUB, SUB), :]])
                for c in range(3):
                    new = r[c, x + reach, rows, :] - ad[c][0]
                    r[c, x + reach, rows, :] = jnp.where(keep, new, 0.0)
                before, here = here, after
            return carry

        lax.fori_loop(0, tiles, residual_step, 0)

        def direction_step(t, carry, rim=rim, factor_d=factor_d, factor_r=factor_r):
            rows = pl.ds(pl.multiple_of(PAD + t * SUB, SUB), SUB)
            for c in range(3):
                for x in range(-rim, width + rim):
                    new = factor_d * d[c, x + reach, rows, :] + factor_r * r[c, x + reach, rows, :]
                    d[c, x + reach, rows, :] = new
                    if 0 <= x < width:
                        total[c, x, rows, :] = total[c, x, rows, :] + new
            return carry

        lax.fori_loop(0, tiles, direction_step, 0)

    for c in range(3):
        for x in range(width):
            out[c, x] = total[c, x, window, :]
            own_out[c, x] = total[c, x, PAD + RIM : PAD + RIM + own, :]

    def send(ref, x):
        for c in range(3):
            ref[c] = total[c, x, window, :]

    @pl.when(even_x)
    def _():
        send(near, width - 1)
        send(far, 0)

    @pl.when(jnp.logical_not(even_x))
    def _():
        send(near, 0)
        send(far, width - 1)


def coarse_solve(bounds, q, s_win, got_near, got_far):
    _, planes, height, _ = q.shape
    width = planes - 2
    side = (3 * width + 2, height, LANES)
    edge = jax.ShapeDtypeStruct((3, height, LANES), F32)

    def field(count):
        return pltpu.VMEM((3, count, height + 2 * PAD, LANES), F32)

    return pl.pallas_call(
        coarse_kernel,
        in_specs=[SMEM] + [VMEM] * 4,
        out_shape=[
            jax.ShapeDtypeStruct((3, width, height, LANES), F32),
            jax.ShapeDtypeStruct((3, width, height - 2 * RIM, LANES), F32),
            edge,
            edge,
        ],
        scratch_shapes=[
            pltpu.VMEM(side, F32),
            pltpu.VMEM(side, F32),
            field(width + 6),
            field(width + 6),
            field(width),
            pltpu.VMEM((width + 4, height, LANES), F32),
        ],
        compiler_params=params(),
        name="coarse_solve",
    )(bounds, q, s_win, got_near, got_far)


def prolong_kernel(rest_x, corr, got_near, got_far, smooth, rest_y, rest_zt, out, left, right, wy, col, grown):
    _, width, height, _ = corr.shape
    own = height - 2 * RIM
    fine_width = 2 * width
    even_x = is_even("wide")
    first_weight = lax.axis_index("wide") * width
    zr = z_matrix(rest_zt)
    for a in range(5):
        wy[a] = y_weights(rest_y, a, height, own)

    def place(from_left, from_right):
        left[...] = from_left[...]
        right[...] = from_right[...]

    @pl.when(even_x)
    def _():
        place(got_far, got_near)

    @pl.when(jnp.logical_not(even_x))
    def _():
        place(got_near, got_far)

    def row(c, i):
        return left[c] if i < 0 else right[c] if i == width else corr[c, i]

    for c in range(3):
        for x in range(fine_width):
            total = None
            for a in range(x % 2, 5, 2):
                i = (x + 2 - a) // 2
                piece = rest_x[first_weight + i + 1, a] * row(c, i)
                total = piece if total is None else total + piece
            col[...] = total

            def at(a, shift):
                rows = pl.ds(RIM + shift, own)
                return wy[a, rows, :] * col[rows, :]

            grown[x, pl.ds(0, own, stride=2), :] = at(0, 1) + at(2, 0) + at(4, -1)
            grown[x, pl.ds(1, own, stride=2), :] = at(1, 1) + at(3, 0)
        flat = grown[...].reshape(fine_width * 2 * own, LANES)
        wide = lax.dot_general(
            flat, zr, (((1,), (1,)), ((), ())), precision=lax.Precision.HIGHEST, preferred_element_type=F32
        )
        out[c] = smooth[c] + wide.reshape(fine_width, 2 * own, 2 * LANES)


def prolong(rest_x, corr, got_near, got_far, smooth, rest_y, rest_zt):
    _, width, height, _ = corr.shape
    own = height - 2 * RIM
    return pl.pallas_call(
        prolong_kernel,
        in_specs=[SMEM] + [VMEM] * 6,
        out_shape=jax.ShapeDtypeStruct(smooth.shape, F32),
        scratch_shapes=[
            pltpu.VMEM((3, height, LANES), F32),
            pltpu.VMEM((3, height, LANES), F32),
            pltpu.VMEM((5, height, LANES), F32),
            pltpu.VMEM((height, LANES), F32),
            pltpu.VMEM((2 * width, 2 * own, LANES), F32),
        ],
        compiler_params=params(),
        name="prolong",
    )(rest_x, corr, got_near, got_far, smooth, rest_y, rest_zt)


def gather(own):
    count = lax.axis_size("narrow")
    n = lax.axis_index("narrow")

    def ring(x, by):
        return lax.ppermute(x, "narrow", [(i, (i + by) % count) for i in range(count)])

    pair = swap_near(own, "narrow")
    low, high = ring(own, 2), ring(own, -2)
    pair_low, pair_high = ring(pair, 2), ring(pair, -2)
    far_own, far_pair = ring(low, 2), ring(pair_high, -2)
    blocks = [own, pair, low, high, pair_low, pair_high, far_own, far_pair]
    return blocks


def assemble_kernel(*refs):
    blocks, out = refs[:-1], refs[-1]
    count = len(blocks)
    n = lax.axis_index("narrow")
    m = n + 1 - 2 * lax.rem(n, 2)
    own = blocks[0].shape[2]
    sources = [n, m, n - 2, n + 2, m - 2, m + 2, n - 4, m + 4]
    for block, source in zip(blocks, sources):
        start = pl.multiple_of(lax.rem(source + count, count) * own, SUB)
        out[:, :, pl.ds(start, own), :] = block[...]


def assemble(blocks):
    three, width, own, lanes = blocks[0].shape
    return pl.pallas_call(
        assemble_kernel,
        out_shape=jax.ShapeDtypeStruct((three, width, own * len(blocks), lanes), F32),
        compiler_params=params(),
        name="assemble",
    )(*blocks)


def body(
    right_side,
    start_guess,
    reaction,
    coarse_reaction,
    rest_x,
    rest_y,
    rest_z,
    fine_bounds,
    coarse_bounds,
):
    x_weights = jnp.pad(rest_x, ((1, 1), (0, 0)))
    y_padded = jnp.pad(rest_y, ((RIM, RIM), (0, 0)))
    z_weights = rest_z.T
    near, far = pack_y(start_guess, right_side, reaction)
    got_far, got_near = swap_far(far, "narrow"), swap_near(near, "narrow")
    r0p, s_ext, near, far = residual(start_guess, right_side, reaction, got_near, got_far)
    got_far, got_near = swap_far(far, "wide"), swap_near(near, "wide")
    smooth, partial, near, far = smoothing(
        fine_bounds, x_weights, r0p, s_ext, got_near, got_far, near, far, start_guess, y_padded, z_weights
    )
    got_far, got_near = swap_far(far, "narrow"), swap_near(near, "narrow")
    q, s_win, near, far = rows(partial, got_near, got_far, coarse_reaction)
    got_far, got_near = swap_far(far, "wide"), swap_near(near, "wide")
    corr, own, near, far = coarse_solve(coarse_bounds, q, s_win, got_near, got_far)
    got_far, got_near = swap_far(far, "wide"), swap_near(near, "wide")
    solution_block = prolong(x_weights, corr, got_near, got_far, smooth, y_padded, z_weights)
    return solution_block, assemble(gather(own))


def solution(mesh):
    return jax.shard_map(
        body,
        mesh=mesh,
        in_specs=(
            P(None, "wide", "narrow", None),
            P(None, "wide", "narrow", None),
            P("wide", "narrow", None),
            P("wide", None, None),
            P(),
            P(),
            P(),
            P(),
            P(),
        ),
        out_specs=(P(None, "wide", "narrow", None), P(None, "wide", None, None)),
        check_vma=False,
    )
```

```python
import jax
import jax.numpy as jnp
from jax import lax
from jax.experimental import pallas as pl
from jax.experimental.pallas import tpu as pltpu
from jax.sharding import PartitionSpec as P

F32 = jnp.float32
LANES = 128
SUB = 8
RIM = 4
PAD = 8
MIB = 1024 * 1024
BYTES_PER_US = 3_690_000


def params(mib=24):
    return pltpu.CompilerParams(vmem_limit_bytes=mib * MIB)


def cost(us):
    return pl.CostEstimate(flops=0, bytes_accessed=int(us * BYTES_PER_US), transcendentals=0)


def swap_near(x, axis):
    count = lax.axis_size(axis)
    return lax.ppermute(x, axis, [(i, i ^ 1) for i in range(count)])


def swap_far(x, axis):
    count = lax.axis_size(axis)
    up = [(i, i + 1) for i in range(1, count - 1, 2)]
    return lax.ppermute(x, axis, up + [(j, i) for i, j in up])


def swap_both(pair, axis):
    return [swap_near(pair[0], axis), swap_far(pair[1], axis)]


def is_even(axis):
    return lax.rem(lax.axis_index(axis), 2) == 0


def lane_index():
    return lax.broadcasted_iota(jnp.int32, (SUB, LANES), 1)


def z_next(parts, last):
    rolled = [pltpu.roll(part, LANES - 1, 1) for part in parts]
    beyond = rolled[1:] + [jnp.zeros_like(parts[0])]
    return [jnp.where(last, b, r) for r, b in zip(rolled, beyond)]


def z_before(parts, first):
    rolled = [pltpu.roll(part, 1, 1) for part in parts]
    beyond = [jnp.zeros_like(parts[0])] + rolled[:-1]
    return [jnp.where(first, b, r) for r, b in zip(rolled, beyond)]


def each(fn, *lists):
    return [fn(*items) for items in zip(*lists)]


def add(a, b):
    return each(lambda p, q: p + q, a, b)


def sub(a, b):
    return each(lambda p, q: p - q, a, b)


def eighth(a):
    return each(lambda p: 0.125 * p, a)


class Plane:
    def __init__(self, load, edges):
        first, last = edges
        v = [load(c, 0) for c in range(3)]
        above = [load(c, 1) for c in range(3)]
        below = [load(c, -1) for c in range(3)]
        dy = [eighth(sub(above[c], below[c])) for c in range(3)]
        next_0, before_0 = z_next(v[0], last), z_before(v[0], first)
        next_2, before_2 = z_next(v[2], last), z_before(v[2], first)
        slope = [
            add(dy[1], eighth(sub(next_2, before_2))),
            dy[0],
            eighth(sub(next_0, before_0)),
        ]
        self.v = v
        self.ahead = [add(v[c], slope[c]) for c in range(3)]
        self.behind = [sub(v[c], slope[c]) for c in range(3)]
        self.parts = (above, below, dy, next_0, before_0, edges)

    def inner(self, diagonal):
        above, below, dy, next_0, before_0, (first, last) = self.parts
        v = self.v
        out = []
        for c in range(3):
            if c == 0:
                along_z = add(next_0, before_0)
            else:
                other = dy[2] if c == 1 else dy[1]
                along_z = add(
                    z_next(sub(v[c], other), last), z_before(add(v[c], other), first)
                )
            total = add(add(above[c], below[c]), along_z)
            out.append(each(lambda d, p, q: d * p - q, diagonal, v[c], total))
        return out


def applied(before, plane, after, diagonal):
    out = plane.inner(diagonal)
    for c in range(3):
        if after is not None:
            out[c] = sub(out[c], after.behind[c])
        if before is not None:
            out[c] = sub(out[c], before.ahead[c])
    return out


def edge_masks():
    lane = lane_index()
    return lane == 0, lane == LANES - 1


def inside_rows(start, own, axis):
    row = start + lax.broadcasted_iota(jnp.int32, (SUB, LANES), 0)
    place = lax.axis_index(axis)
    low = jnp.where(place == 0, RIM, 0)
    high = jnp.where(place == lax.axis_size(axis) - 1, RIM + own, own + 2 * RIM)
    return (row >= low) & (row < high)


def pack_y_kernel(u_lo, u_hi, b_lo, b_hi, s_lo, s_hi, near, far):
    width = u_lo.shape[1]

    def pack(out, u, b, s, low):
        u_rows = slice(0, 3) if low else slice(5, 8)
        two = slice(0, 2) if low else slice(6, 8)
        for h in range(2):
            lanes = slice(h * LANES, (h + 1) * LANES)
            for x in range(width):
                for c in range(3):
                    k = c * width + x
                    out[h, 3 * k : 3 * k + 3, :] = u[c, x, u_rows, lanes]
                    base = 9 * width + 2 * k
                    out[h, base : base + 2, :] = b[c, x, two, lanes]
                base = 15 * width + 2 * x
                out[h, base : base + 2, :] = s[x, two, lanes]

    even = is_even("narrow")

    @pl.when(even)
    def _():
        pack(near, u_hi, b_hi, s_hi, False)
        pack(far, u_lo, b_lo, s_lo, True)

    @pl.when(jnp.logical_not(even))
    def _():
        pack(near, u_lo, b_lo, s_lo, True)
        pack(far, u_hi, b_hi, s_hi, False)


def pack_y(u, b, s):
    _, width, height, depth = u.shape
    last = height // SUB - 1
    block = pl.BlockSpec((3, width, SUB, depth), lambda i: (0, 0, 0, 0))
    block_last = pl.BlockSpec((3, width, SUB, depth), lambda i: (0, 0, last, 0))
    plane = pl.BlockSpec((width, SUB, depth), lambda i: (0, 0, 0))
    plane_last = pl.BlockSpec((width, SUB, depth), lambda i: (0, last, 0))
    rows = 17 * width
    out = jax.ShapeDtypeStruct((2, rows, LANES), F32)
    whole = pl.BlockSpec((2, rows, LANES), lambda i: (0, 0, 0))
    return pl.pallas_call(
        pack_y_kernel,
        grid=(1,),
        in_specs=[block, block_last, block, block_last, plane, plane_last],
        out_specs=[whole, whole],
        out_shape=[out, out],
        compiler_params=params(),
        cost_estimate=cost(1),
        name="pack_y",
    )(u, u, b, b, s, s)


def residual_kernel(u, b, s, r0, near, far, ue):
    _, width, height, _ = u.shape
    for h in range(2):
        lanes = slice(h * LANES, (h + 1) * LANES)
        for x in range(width):
            for c in range(3):
                ue[c, x, h, 0:PAD, :] = jnp.zeros((PAD, LANES), F32)
                ue[c, x, h, PAD + height :, :] = jnp.zeros((PAD, LANES), F32)

        def fill(t, carry, h=h, lanes=lanes):
            rows = pl.ds(pl.multiple_of(t * SUB, SUB), SUB)
            to = pl.ds(pl.multiple_of(PAD + t * SUB, SUB), SUB)
            for x in range(width):
                for c in range(3):
                    ue[c, x, h, to, :] = u[c, x, rows, lanes]
            return carry

        lax.fori_loop(0, height // SUB, fill, 0)

    edges = edge_masks()

    def step(t, carry):
        start = PAD + t * SUB
        rows = pl.ds(pl.multiple_of(t * SUB, SUB), SUB)

        def plane(x):
            return Plane(
                lambda c, dy: [ue[c, x, h, pl.ds(start + dy, SUB), :] for h in range(2)],
                edges,
            )

        before, here = None, plane(0)
        for x in range(width):
            after = plane(x + 1) if x + 1 < width else None
            au = applied(before, here, after, [6.0 + s[x, rows, h * LANES : (h + 1) * LANES] for h in range(2)])
            for c in range(3):
                for h in range(2):
                    r0[c, x, h, rows, :] = b[c, x, rows, h * LANES : (h + 1) * LANES] - au[c][h]
            before, here = here, after
        return carry

    lax.fori_loop(0, height // SUB, step, 0)

    def pack(out, edge, second):
        for c in range(3):
            out[c] = r0[c, edge]
            out[3 + c] = r0[c, second]
            out[6 + c] = ue[c, edge, :, PAD : PAD + height, :]
        for h in range(2):
            out[9, h] = s[edge, :, h * LANES : (h + 1) * LANES]

    even_x = is_even("wide")

    @pl.when(even_x)
    def _():
        pack(near, width - 1, width - 2)
        pack(far, 0, 1)

    @pl.when(jnp.logical_not(even_x))
    def _():
        pack(near, 0, 1)
        pack(far, width - 1, width - 2)


def residual(u, b, s):
    _, width, height, _ = u.shape
    side = jax.ShapeDtypeStruct((10, 2, height, LANES), F32)
    return pl.pallas_call(
        residual_kernel,
        out_shape=[pltpu.HBM((3, width, 2, height, LANES), F32), side, side],
        scratch_shapes=[pltpu.VMEM((3, width, 2, height + 2 * PAD, LANES), F32)],
        compiler_params=params(),
        cost_estimate=cost(3),
        name="residual",
    )(u, b, s)


def ends_kernel(
    u_lo, u_hi, b_lo, b_hi, s_lo, s_hi, got_near, got_far, main_near, main_far,
    r_end, s_end, near, far, ue, be, se, own,
):
    width = u_lo.shape[1]
    begin = (PAD + RIM, PAD - RIM)

    def place(e, u, b, s, halo):
        at = begin[e]
        low = e == 0
        three = slice(at - 3, at) if low else slice(at + SUB, at + SUB + 3)
        two = slice(at - 2, at) if low else slice(at + SUB, at + SUB + 2)
        for h in range(2):
            lanes = slice(h * LANES, (h + 1) * LANES)
            for x in range(width):
                for c in range(3):
                    k = c * width + x
                    ue[e, c, x, h, at : at + SUB, :] = u[c, x, :, lanes]
                    be[e, c, x, h, at : at + SUB, :] = b[c, x, :, lanes]
                    ue[e, c, x, h, three, :] = halo[h, 3 * k : 3 * k + 3, :]
                    base = 9 * width + 2 * k
                    be[e, c, x, h, two, :] = halo[h, base : base + 2, :]
                se[e, x, h, at : at + SUB, :] = s[x, :, lanes]
                base = 15 * width + 2 * x
                se[e, x, h, two, :] = halo[h, base : base + 2, :]

    even = is_even("narrow")

    @pl.when(even)
    def _():
        place(0, u_lo, b_lo, s_lo, got_far)
        place(1, u_hi, b_hi, s_hi, got_near)

    @pl.when(jnp.logical_not(even))
    def _():
        place(0, u_lo, b_lo, s_lo, got_near)
        place(1, u_hi, b_hi, s_hi, got_far)

    edges = edge_masks()

    def step(e, carry):
        inside = inside_rows(e * own + 2 * RIM * e - SUB * e, own, "narrow")

        def plane(x):
            return Plane(
                lambda c, dy: [ue[e, c, x, h, pl.ds(PAD + dy, SUB), :] for h in range(2)],
                edges,
            )

        before, here = None, plane(0)
        tile = pl.ds(PAD, SUB)
        for x in range(width):
            after = plane(x + 1) if x + 1 < width else None
            au = applied(before, here, after, [6.0 + se[e, x, h, tile, :] for h in range(2)])
            for c in range(3):
                for h in range(2):
                    r_end[e, c, x, h] = jnp.where(inside, be[e, c, x, h, tile, :] - au[c][h], 0.0)
            for h in range(2):
                s_end[e, x, h] = se[e, x, h, tile, :]
            before, here = here, after
        return carry

    lax.fori_loop(0, 2, step, 0)

    def pack(out, main, edge, second):
        for k in range(10):
            out[k, :, SUB:own, :] = main[k, :, RIM : own - RIM, :]
        for e in range(2):
            tile = slice(e * own, e * own + SUB)
            for h in range(2):
                for c in range(3):
                    out[c, h, tile, :] = r_end[e, c, edge, h]
                    out[3 + c, h, tile, :] = r_end[e, c, second, h]
                    out[6 + c, h, tile, :] = ue[e, c, edge, h, PAD : PAD + SUB, :]
                out[9, h, tile, :] = s_end[e, edge, h]

    even_x = is_even("wide")

    @pl.when(even_x)
    def _():
        pack(near, main_near, width - 1, width - 2)
        pack(far, main_far, 0, 1)

    @pl.when(jnp.logical_not(even_x))
    def _():
        pack(near, main_near, 0, 1)
        pack(far, main_far, width - 1, width - 2)


def ends(u, b, s, got, main):
    _, width, height, depth = u.shape
    last = height // SUB - 1
    block = pl.BlockSpec((3, width, SUB, depth), lambda i: (0, 0, 0, 0))
    block_last = pl.BlockSpec((3, width, SUB, depth), lambda i: (0, 0, last, 0))
    plane = pl.BlockSpec((width, SUB, depth), lambda i: (0, 0, 0))
    plane_last = pl.BlockSpec((width, SUB, depth), lambda i: (0, last, 0))
    shapes = [(2, 3, width, 2, SUB, LANES), (2, width, 2, SUB, LANES)] + [(10, 2, height + 2 * RIM, LANES)] * 2

    def whole(shape):
        return pl.BlockSpec(shape, lambda i: (0,) * len(shape))

    def field(*lead):
        return pltpu.VMEM((2, *lead, 2, 3 * SUB, LANES), F32)

    def kernel(*refs):
        return ends_kernel(*refs, height)

    return pl.pallas_call(
        kernel,
        grid=(1,),
        in_specs=[block, block_last, block, block_last, plane, plane_last] + [whole(x.shape) for x in (*got, *main)],
        out_specs=[whole(shape) for shape in shapes],
        out_shape=[pltpu.HBM(shape, F32) for shape in shapes[:2]]
        + [jax.ShapeDtypeStruct(shape, F32) for shape in shapes[2:]],
        scratch_shapes=[field(3, width), field(3, width), field(width)],
        compiler_params=params(),
        cost_estimate=cost(40),
        name="ends",
    )(u, u, b, b, s, s, *got, *main)


def full(value):
    return jnp.full((SUB, LANES), value, F32)


def chebyshev_numbers(bounds, steps):
    low, high = full(bounds[0]), full(bounds[1])
    middle = (high + low) / 2.0
    radius = (high - low) / 2.0
    stretch = middle / radius
    rho = 1.0 / stretch
    factors = []
    for _ in range(steps - 1):
        rho_next = 1.0 / (2.0 * stretch - rho)
        factors.append((rho_next * rho, 2.0 * rho_next / radius))
        rho = rho_next
    return 1.0 / middle, factors


def z_matrix(rest_zt):
    shape = (2 * LANES, LANES)
    offset = lax.broadcasted_iota(jnp.int32, shape, 0) - 2 * lax.broadcasted_iota(jnp.int32, shape, 1) + 2
    out = jnp.zeros(shape, F32)
    for a in range(5):
        out = out + jnp.where(offset == a, rest_zt[a : a + 1, :], 0.0)
    return out


def y_weights(rest_y, a, rows, own):
    start = pl.multiple_of(lax.axis_index("narrow") * own, SUB)
    return jnp.broadcast_to(rest_y[pl.ds(start, rows), a : a + 1], (rows, LANES))


def smooth_kernel(
    bounds, rest_x, r0p, r_end, s_end, got_near, got_far, sent_near, sent_far, u, s, rest_y, rest_zt,
    smooth, partial, near, far, left, right, u_left, u_right, s_ext, r0, d1, r1, r2, t_pad, zr,
):
    _, width, height, _ = u.shape
    tiles = (height + 2 * RIM) // SUB
    window = slice(PAD, PAD + height + 2 * RIM)
    middle = slice(PAD + SUB, PAD + height)
    tile_rows = [slice(PAD, PAD + SUB), slice(PAD + height, PAD + height + SUB)]
    even_x = is_even("wide")
    zr[...] = z_matrix(rest_zt)

    def place(from_left, from_right, mine_left, mine_right):
        for k in range(10):
            left[k, :, window, :] = from_left[k]
            right[k, :, window, :] = from_right[k]
        for c in range(3):
            u_left[c, :, window, :] = mine_left[6 + c]
            u_right[c, :, window, :] = mine_right[6 + c]

    @pl.when(even_x)
    def _():
        place(got_far, got_near, sent_far, sent_near)

    @pl.when(jnp.logical_not(even_x))
    def _():
        place(got_near, got_far, sent_near, sent_far)

    for x in range(width):
        for h in range(2):
            s_ext[x, h, middle, :] = s[x, RIM : height - RIM, h * LANES : (h + 1) * LANES]
        for e in range(2):
            s_ext[x, :, tile_rows[e], :] = s_end[e, x]
            for c in range(3):
                r0[c, x + 2, :, tile_rows[e], :] = r_end[e, c, x]
        for c in range(3):
            r0[c, x + 2, :, middle, :] = r0p[c, x, :, RIM : height - RIM, :]

    edges = edge_masks()
    place_x = lax.axis_index("wide")
    has_left = place_x > 0
    has_right = place_x < lax.axis_size("wide") - 1
    inverse, factors = chebyshev_numbers(bounds, 2)
    factor_d = factors[0][0] * inverse
    factor_r = factors[0][1]

    def fix(t, carry):
        start = PAD + t * SUB
        rows = pl.ds(start, SUB)
        inside = inside_rows(t * SUB, height, "narrow")

        def plane(ref, first):
            return Plane(
                lambda c, dy: [ref[first + c, h, pl.ds(start + dy, SUB), :] for h in range(2)],
                edges,
            )

        out_left = plane(left, 6)
        in_left = plane(u_left, 0)
        in_right = plane(u_right, 0)
        out_right = plane(right, 6)
        inside_left = inside & has_left
        inside_right = inside & has_right
        for c in range(3):
            for h in range(2):
                r0[c, 0, h, rows, :] = left[3 + c, h, rows, :]
                r0[c, 1, h, rows, :] = jnp.where(
                    inside_left, left[c, h, rows, :] + in_left.behind[c][h], 0.0
                )
                r0[c, 2, h, rows, :] = jnp.where(
                    inside, r0[c, 2, h, rows, :] + out_left.ahead[c][h], 0.0
                )
                r0[c, width + 1, h, rows, :] = jnp.where(
                    inside, r0[c, width + 1, h, rows, :] + out_right.behind[c][h], 0.0
                )
                r0[c, width + 2, h, rows, :] = jnp.where(
                    inside_right, right[c, h, rows, :] + in_right.ahead[c][h], 0.0
                )
                r0[c, width + 3, h, rows, :] = right[3 + c, h, rows, :]
        return carry

    lax.fori_loop(0, tiles, fix, 0)

    def first_step(t, carry):
        start = PAD + t * SUB
        rows = pl.ds(start, SUB)
        inside = inside_rows(t * SUB, height, "narrow")

        def plane(x):
            return Plane(
                lambda c, dy: [r0[c, x + 2, h, pl.ds(start + dy, SUB), :] for h in range(2)],
                edges,
            )

        before, here = plane(-2), plane(-1)
        for x in range(-1, width + 1):
            after = plane(x + 1)
            keep = inside & has_left if x < 0 else inside & has_right if x == width else inside
            source = left.at[9] if x < 0 else right.at[9] if x == width else s_ext.at[x]
            diagonal = [6.0 + source[h, rows, :] for h in range(2)]
            ar = applied(before, here, after, diagonal)
            for c in range(3):
                for h in range(2):
                    old = here.v[c][h]
                    new = old - inverse * ar[c][h]
                    d1[c, x + 1, h, rows, :] = jnp.where(keep, factor_d * old + factor_r * new, 0.0)
                    if 0 <= x < width:
                        r1[c, x, h, rows, :] = new
            before, here = here, after
        return carry

    lax.fori_loop(0, tiles, first_step, 0)

    def second_step(t, carry):
        start = PAD + RIM + t * SUB
        rows = pl.ds(start, SUB)
        to = pl.ds(pl.multiple_of(t * SUB, SUB), SUB)

        def plane(x):
            return Plane(
                lambda c, dy: [d1[c, x + 1, h, pl.ds(start + dy, SUB), :] for h in range(2)],
                edges,
            )

        before, here = plane(-1), plane(0)
        for x in range(width):
            after = plane(x + 1)
            diagonal = [6.0 + s_ext[x, h, rows, :] for h in range(2)]
            ad = applied(before, here, after, diagonal)
            for c in range(3):
                for h in range(2):
                    lanes = slice(h * LANES, (h + 1) * LANES)
                    r2[c, x, h, to, :] = r1[c, x, h, rows, :] - ad[c][h]
                    step = inverse * r0[c, x + 2, h, rows, :] + here.v[c][h]
                    smooth[c, x, to, lanes] = u[c, x, to, lanes] + step
            before, here = here, after
        return carry

    lax.fori_loop(0, height // SUB, second_step, 0)

    coarse_width = width // 2
    coarse_height = height // 2
    coarse_rows = coarse_height + 2 * RIM
    first_weight = place_x * coarse_width
    lead = 2 * RIM + 2
    for c in range(3):
        for i in range(-1, coarse_width + 1):
            k = c * (coarse_width + 2) + i + 1
            terms = [(a, 2 * i - 2 + a) for a in range(5) if 0 <= 2 * i - 2 + a < width]
            halves = []
            for h in range(2):
                total = None
                for a, x in terms:
                    piece = rest_x[first_weight + i + 1, a] * r2[c, x, h]
                    total = piece if total is None else total + piece
                halves.append(total)
            joined = jnp.concatenate(halves, axis=1)
            t_pad[k, 0:lead, :] = jnp.zeros((lead, LANES), F32)
            t_pad[k, lead + height :, :] = jnp.zeros((t_pad.shape[1] - lead - height, LANES), F32)
            t_pad[k, lead : lead + height, :] = jnp.dot(
                joined, zr[...], precision=lax.Precision.HIGHEST, preferred_element_type=F32
            )
    weights = [y_weights(rest_y, a, coarse_rows, coarse_height) for a in range(5)]
    even_y = is_even("narrow")
    for c in range(3):
        for i in range(coarse_width + 2):
            k = c * (coarse_width + 2) + i
            total = None
            for a in range(5):
                piece = weights[a] * t_pad[k, pl.ds(a, coarse_rows, stride=2), :]
                total = piece if total is None else total + piece
            partial[c, i] = total

    def send(out, first):
        for c in range(3):
            for i in range(coarse_width + 2):
                out[c * (coarse_width + 2) + i] = partial[c, i, first : first + SUB, :]

    @pl.when(even_y)
    def _():
        send(near, coarse_rows - SUB)
        send(far, 0)

    @pl.when(jnp.logical_not(even_y))
    def _():
        send(near, 0)
        send(far, coarse_rows - SUB)


SMEM = pl.BlockSpec(memory_space=pltpu.SMEM)
VMEM = pl.BlockSpec(memory_space=pltpu.VMEM)


def smoothing(bounds, rest_x, r0p, r_end, s_end, got, sent, u, s, rest_y, rest_zt):
    _, width, height, depth = u.shape
    padded = height + 2 * (RIM + PAD)
    planes = 3 * (width // 2 + 2)
    coarse_rows = height // 2 + 2 * RIM
    tile = jax.ShapeDtypeStruct((planes, SUB, LANES), F32)

    def field(*lead):
        return pltpu.VMEM((*lead, 2, padded, LANES), F32)

    return pl.pallas_call(
        smooth_kernel,
        in_specs=[SMEM, SMEM] + [VMEM] * 11,
        out_shape=[
            jax.ShapeDtypeStruct((3, width, height, depth), F32),
            jax.ShapeDtypeStruct((3, width // 2 + 2, coarse_rows, LANES), F32),
            tile,
            tile,
        ],
        scratch_shapes=[
            field(10),
            field(10),
            field(3),
            field(3),
            field(width),
            field(3, width + 4),
            field(3, width + 2),
            field(3, width),
            pltpu.VMEM((3, width, 2, height, LANES), F32),
            pltpu.VMEM((planes, 2 * coarse_rows + 2 * SUB, LANES), F32),
            pltpu.VMEM((2 * LANES, LANES), F32),
        ],
        compiler_params=params(),
        cost_estimate=cost(10),
        name="smoothing",
    )(bounds, rest_x, r0p, r_end, s_end, *got, *sent, u, s, rest_y, rest_zt)


def rows_kernel(partial, got_near, got_far, s, q, s_win, near, far):
    _, planes, rows, _ = partial.shape
    own = rows - 2 * RIM
    coarse_width = planes - 2
    n = lax.axis_index("narrow")
    even_y = is_even("narrow")
    q[:, :, SUB : rows - SUB, :] = partial[:, :, SUB : rows - SUB, :]

    def join(low, high):
        for c in range(3):
            for i in range(planes):
                k = c * planes + i
                q[c, i, 0:SUB, :] = partial[c, i, 0:SUB, :] + low[k]
                q[c, i, rows - SUB :, :] = partial[c, i, rows - SUB :, :] + high[k]

    @pl.when(even_y)
    def _():
        join(got_far, got_near)

    @pl.when(jnp.logical_not(even_y))
    def _():
        join(got_near, got_far)

    total = s.shape[1]
    start = pl.multiple_of(n * own, SUB)
    before = pl.multiple_of(jnp.maximum(start - SUB, 0), SUB)
    after = pl.multiple_of(jnp.minimum(start + own, total - SUB), SUB)
    for x in range(coarse_width):
        s_win[x, RIM : RIM + own, :] = s[x, pl.ds(start, own), :]
        s_win[x, 0:RIM, :] = s[x, pl.ds(before, SUB), :][SUB - RIM :, :]
        s_win[x, RIM + own :, :] = s[x, pl.ds(after, SUB), :][0:RIM, :]

    def pack(out, to_left):
        first = 0 if to_left else 2
        for c in range(3):
            for k in range(coarse_width):
                out[c * coarse_width + k] = q[c, first + k]
        edge = 0 if to_left else coarse_width - 2
        for k in range(2):
            out[3 * coarse_width + k] = s_win[edge + k]

    even_x = is_even("wide")

    @pl.when(even_x)
    def _():
        pack(near, False)
        pack(far, True)

    @pl.when(jnp.logical_not(even_x))
    def _():
        pack(near, True)
        pack(far, False)


def rows(partial, got_near, got_far, s):
    _, planes, height, _ = partial.shape
    width = planes - 2
    side = jax.ShapeDtypeStruct((3 * width + 2, height, LANES), F32)
    return pl.pallas_call(
        rows_kernel,
        out_shape=[
            jax.ShapeDtypeStruct(partial.shape, F32),
            jax.ShapeDtypeStruct((width, height, LANES), F32),
            side,
            side,
        ],
        compiler_params=params(),
        cost_estimate=cost(1),
        name="coarse_rows",
    )(partial, got_near, got_far, s)


def coarse_kernel(bounds, q, s_win, got_near, got_far, out, own_out, near, far, left, right, r, d, total, sc):
    _, planes, height, _ = q.shape
    width = planes - 2
    own = height - 2 * RIM
    tiles = height // SUB
    window = slice(PAD, PAD + height)
    even_x = is_even("wide")
    place_x = lax.axis_index("wide")
    has_left = place_x > 0
    has_right = place_x < lax.axis_size("wide") - 1
    inverse, factors = chebyshev_numbers(bounds, 4)
    edges = edge_masks()
    reach = 3

    def place(from_left, from_right):
        left[...] = from_left[...]
        right[...] = from_right[...]

    @pl.when(even_x)
    def _():
        place(got_far, got_near)

    @pl.when(jnp.logical_not(even_x))
    def _():
        place(got_near, got_far)

    for k in range(2):
        sc[k] = left[3 * width + k]
        sc[width + 2 + k] = right[3 * width + k]
    for x in range(width):
        sc[x + 2] = s_win[x]

    def start_rows(t, carry):
        rows = pl.ds(pl.multiple_of(t * SUB, SUB), SUB)
        to = pl.ds(pl.multiple_of(PAD + t * SUB, SUB), SUB)
        for c in range(3):
            for i in range(-reach, width + reach):
                value = None
                if -1 <= i <= width:
                    value = q[c, i + 1, rows, :]
                if i <= 0:
                    other = left[c * width + i + reach, rows, :]
                    value = other if value is None else value + other
                if i >= width - 1:
                    other = right[c * width + i - width + 1, rows, :]
                    value = other if value is None else value + other
                r[c, i + reach, to, :] = value
                first = inverse * value
                d[c, i + reach, to, :] = first
                if 0 <= i < width:
                    total[c, i, to, :] = first
        return carry

    lax.fori_loop(0, tiles, start_rows, 0)

    for k in range(3):
        factor_d, factor_r = factors[k]
        rim = reach - 1 - k

        def residual_step(t, carry, rim=rim):
            start = PAD + t * SUB
            rows = pl.ds(start, SUB)
            inside = inside_rows(t * SUB, own, "narrow")

            def plane(x):
                return Plane(lambda c, dy: [d[c, x + reach, pl.ds(start + dy, SUB), :]], edges)

            before, here = plane(-rim - 1), plane(-rim)
            for x in range(-rim, width + rim):
                after = plane(x + 1)
                keep = inside & has_left if x < 0 else inside & has_right if x >= width else inside
                ad = applied(before, here, after, [6.0 + sc[x + 2, pl.ds(t * SUB, SUB), :]])
                for c in range(3):
                    new = r[c, x + reach, rows, :] - ad[c][0]
                    r[c, x + reach, rows, :] = jnp.where(keep, new, 0.0)
                before, here = here, after
            return carry

        lax.fori_loop(0, tiles, residual_step, 0)

        def direction_step(t, carry, rim=rim, factor_d=factor_d, factor_r=factor_r):
            rows = pl.ds(pl.multiple_of(PAD + t * SUB, SUB), SUB)
            for c in range(3):
                for x in range(-rim, width + rim):
                    new = factor_d * d[c, x + reach, rows, :] + factor_r * r[c, x + reach, rows, :]
                    d[c, x + reach, rows, :] = new
                    if 0 <= x < width:
                        total[c, x, rows, :] = total[c, x, rows, :] + new
            return carry

        lax.fori_loop(0, tiles, direction_step, 0)

    for c in range(3):
        for x in range(width):
            out[c, x] = total[c, x, window, :]
            own_out[c, x] = total[c, x, PAD + RIM : PAD + RIM + own, :]

    def send(ref, x):
        for c in range(3):
            ref[c] = total[c, x, window, :]

    @pl.when(even_x)
    def _():
        send(near, width - 1)
        send(far, 0)

    @pl.when(jnp.logical_not(even_x))
    def _():
        send(near, 0)
        send(far, width - 1)


def coarse_solve(bounds, q, s_win, got_near, got_far):
    _, planes, height, _ = q.shape
    width = planes - 2
    side = (3 * width + 2, height, LANES)
    edge = jax.ShapeDtypeStruct((3, height, LANES), F32)

    def field(count):
        return pltpu.VMEM((3, count, height + 2 * PAD, LANES), F32)

    return pl.pallas_call(
        coarse_kernel,
        in_specs=[SMEM] + [VMEM] * 4,
        out_shape=[
            jax.ShapeDtypeStruct((3, width, height, LANES), F32),
            jax.ShapeDtypeStruct((3, width, height - 2 * RIM, LANES), F32),
            edge,
            edge,
        ],
        scratch_shapes=[
            pltpu.VMEM(side, F32),
            pltpu.VMEM(side, F32),
            field(width + 6),
            field(width + 6),
            field(width),
            pltpu.VMEM((width + 4, height, LANES), F32),
        ],
        compiler_params=params(),
        cost_estimate=cost(3),
        name="coarse_solve",
    )(bounds, q, s_win, got_near, got_far)


def prolong_kernel(rest_x, corr, got_near, got_far, smooth, rest_y, rest_zt, out, left, right, wy, col, grown):
    _, width, height, _ = corr.shape
    own = height - 2 * RIM
    fine_width = 2 * width
    even_x = is_even("wide")
    first_weight = lax.axis_index("wide") * width
    zr = z_matrix(rest_zt)
    for a in range(5):
        wy[a] = y_weights(rest_y, a, height, own)

    def place(from_left, from_right):
        left[...] = from_left[...]
        right[...] = from_right[...]

    @pl.when(even_x)
    def _():
        place(got_far, got_near)

    @pl.when(jnp.logical_not(even_x))
    def _():
        place(got_near, got_far)

    def row(c, i):
        return left[c] if i < 0 else right[c] if i == width else corr[c, i]

    for c in range(3):
        for x in range(fine_width):
            total = None
            for a in range(x % 2, 5, 2):
                i = (x + 2 - a) // 2
                piece = rest_x[first_weight + i + 1, a] * row(c, i)
                total = piece if total is None else total + piece
            col[...] = total

            def at(a, shift):
                rows = pl.ds(RIM + shift, own)
                return wy[a, rows, :] * col[rows, :]

            grown[x, pl.ds(0, own, stride=2), :] = at(0, 1) + at(2, 0) + at(4, -1)
            grown[x, pl.ds(1, own, stride=2), :] = at(1, 1) + at(3, 0)
        flat = grown[...].reshape(fine_width * 2 * own, LANES)
        wide = lax.dot_general(
            flat, zr, (((1,), (1,)), ((), ())), precision=lax.Precision.HIGHEST, preferred_element_type=F32
        )
        out[c] = smooth[c] + wide.reshape(fine_width, 2 * own, 2 * LANES)


def prolong(rest_x, corr, got_near, got_far, smooth, rest_y, rest_zt):
    _, width, height, _ = corr.shape
    own = height - 2 * RIM
    return pl.pallas_call(
        prolong_kernel,
        in_specs=[SMEM] + [VMEM] * 6,
        out_shape=jax.ShapeDtypeStruct(smooth.shape, F32),
        scratch_shapes=[
            pltpu.VMEM((3, height, LANES), F32),
            pltpu.VMEM((3, height, LANES), F32),
            pltpu.VMEM((5, height, LANES), F32),
            pltpu.VMEM((height, LANES), F32),
            pltpu.VMEM((2 * width, 2 * own, LANES), F32),
        ],
        compiler_params=params(),
        cost_estimate=cost(12),
        name="prolong",
    )(rest_x, corr, got_near, got_far, smooth, rest_y, rest_zt)


def gather(own, edges):
    count = lax.axis_size("narrow")
    n = lax.axis_index("narrow")

    def ring(x, by):
        return lax.ppermute(x, "narrow", [(i, (i + by) % count) for i in range(count)])

    pair = swap_near(own, "narrow")
    low, high = ring(own, 2), ring(own, -2)
    pair, low, high = lax.optimization_barrier((pair, low, high))
    pair_low, pair_high = ring(pair, 2), ring(pair, -2)
    pair_high, edges = lax.optimization_barrier((pair_high, edges))
    far_own, far_pair = ring(low, 2), ring(pair_high, -2)
    blocks = [own, pair, low, high, pair_low, pair_high, far_own, far_pair]
    return blocks, edges


def assemble_kernel(*refs):
    blocks, out = refs[:-1], refs[-1]
    count = len(blocks)
    n = lax.axis_index("narrow")
    m = n + 1 - 2 * lax.rem(n, 2)
    own = blocks[0].shape[2]
    sources = [n, m, n - 2, n + 2, m - 2, m + 2, n - 4, m + 4]
    for block, source in zip(blocks, sources):
        start = pl.multiple_of(lax.rem(source + count, count) * own, SUB)
        out[:, :, pl.ds(start, own), :] = block[...]


def assemble(blocks):
    three, width, own, lanes = blocks[0].shape
    return pl.pallas_call(
        assemble_kernel,
        out_shape=jax.ShapeDtypeStruct((three, width, own * len(blocks), lanes), F32),
        compiler_params=params(),
        cost_estimate=cost(1),
        name="assemble",
    )(*blocks)


def body(
    right_side,
    start_guess,
    reaction,
    coarse_reaction,
    rest_x,
    rest_y,
    rest_z,
    fine_bounds,
    coarse_bounds,
):
    x_weights = jnp.pad(rest_x, ((1, 1), (0, 0)))
    y_padded = jnp.pad(rest_y, ((RIM, RIM), (0, 0)))
    z_weights = rest_z.T
    from_hbm = [pltpu.with_memory_space_constraint(x, pltpu.HBM) for x in (start_guess, right_side, reaction)]
    got = swap_both(pack_y(*from_hbm), "narrow")
    r0p, *main = residual(start_guess, right_side, reaction)
    r_end, s_end, *sent = ends(start_guess, right_side, reaction, got, main)
    got = swap_both(sent, "wide")
    r0p, r_end, s_end = (pltpu.with_memory_space_constraint(x, pltpu.HBM) for x in (r0p, r_end, s_end))
    smooth, partial, *sent = smoothing(
        fine_bounds, x_weights, r0p, r_end, s_end, got, sent, start_guess, reaction, y_padded, z_weights
    )
    got = swap_both(sent, "narrow")
    q, s_win, *sent = rows(partial, *got, coarse_reaction)
    got = swap_both(sent, "wide")
    corr, own, *sent = coarse_solve(coarse_bounds, q, s_win, *got)
    got_near, got_far = swap_both(sent, "wide")
    blocks, (got_near, got_far) = gather(own, (got_near, got_far))
    solution_block = prolong(x_weights, corr, got_near, got_far, smooth, y_padded, z_weights)
    return solution_block, assemble(blocks)


def solution(mesh):
    return jax.shard_map(
        body,
        mesh=mesh,
        in_specs=(
            P(None, "wide", "narrow", None),
            P(None, "wide", "narrow", None),
            P("wide", "narrow", None),
            P("wide", None, None),
            P(),
            P(),
            P(),
            P(),
            P(),
        ),
        out_specs=(P(None, "wide", "narrow", None), P(None, "wide", None, None)),
        check_vma=False,
    )
```

```python
import jax
import jax.numpy as jnp
from jax import lax
from jax.experimental import pallas as pl
from jax.experimental.pallas import tpu as pltpu
from jax.sharding import PartitionSpec as P

F32 = jnp.float32
LANES = 128
SUB = 8
RIM = 4
PAD = 8
MIB = 1024 * 1024
BYTES_PER_US = 3_690_000


def params(mib=24):
    return pltpu.CompilerParams(vmem_limit_bytes=mib * MIB)


def cost(us):
    return pl.CostEstimate(flops=0, bytes_accessed=int(us * BYTES_PER_US), transcendentals=0)


def swap_near(x, axis):
    count = lax.axis_size(axis)
    return lax.ppermute(x, axis, [(i, i ^ 1) for i in range(count)])


def swap_far(x, axis):
    count = lax.axis_size(axis)
    up = [(i, i + 1) for i in range(1, count - 1, 2)]
    return lax.ppermute(x, axis, up + [(j, i) for i, j in up])


def swap_both(pair, axis):
    return [swap_near(pair[0], axis), swap_far(pair[1], axis)]


def is_even(axis):
    return lax.rem(lax.axis_index(axis), 2) == 0


def lane_index():
    return lax.broadcasted_iota(jnp.int32, (SUB, LANES), 1)


def z_next(parts, last):
    rolled = [pltpu.roll(part, LANES - 1, 1) for part in parts]
    beyond = rolled[1:] + [jnp.zeros_like(parts[0])]
    return [jnp.where(last, b, r) for r, b in zip(rolled, beyond)]


def z_before(parts, first):
    rolled = [pltpu.roll(part, 1, 1) for part in parts]
    beyond = [jnp.zeros_like(parts[0])] + rolled[:-1]
    return [jnp.where(first, b, r) for r, b in zip(rolled, beyond)]


def each(fn, *lists):
    return [fn(*items) for items in zip(*lists)]


def add(a, b):
    return each(lambda p, q: p + q, a, b)


def sub(a, b):
    return each(lambda p, q: p - q, a, b)


def eighth(a):
    return each(lambda p: 0.125 * p, a)


class Plane:
    def __init__(self, load):
        self.v = [load(c, 0) for c in range(3)]
        above = [load(c, 1) for c in range(3)]
        below = [load(c, -1) for c in range(3)]
        self.along_y = [add(above[c], below[c]) for c in range(3)]
        self.dy = [eighth(sub(above[c], below[c])) for c in range(3)]


def applied(before, plane, after, diagonal, edges):
    first, last = edges
    v, dy = plane.v, plane.dy

    def difference(pick):
        if before is None:
            return pick(after)
        if after is None:
            return each(lambda p: -p, pick(before))
        return sub(pick(after), pick(before))

    slope = [
        eighth(difference(lambda q: q.v[2])),
        dy[2],
        add(eighth(difference(lambda q: q.v[0])), dy[1]),
    ]
    cross = [difference(lambda q: q.dy[1]), difference(lambda q: q.dy[0]), None]
    out = []
    for c in range(3):
        near = plane.along_y[c]
        for other in (before, after):
            if other is not None:
                near = add(near, other.v[c])
        total = each(lambda d, p, q: d * p - q, diagonal, v[c], near)
        if cross[c] is not None:
            total = add(total, cross[c])
        total = add(total, z_next(sub(slope[c], v[c]), last))
        out.append(sub(total, z_before(add(slope[c], v[c]), first)))
    return out


def shares(load, edges):
    first, last = edges
    plane = Plane(load)
    v, dy = plane.v, plane.dy
    along_z = [sub(z_next(v[c], last), z_before(v[c], first)) for c in (0, 2)]
    slope = [add(dy[1], eighth(along_z[1])), dy[0], eighth(along_z[0])]
    return [add(v[c], slope[c]) for c in range(3)], [sub(v[c], slope[c]) for c in range(3)]


def edge_masks():
    lane = lane_index()
    return lane == 0, lane == LANES - 1


def inside_rows(start, own, axis):
    row = start + lax.broadcasted_iota(jnp.int32, (SUB, LANES), 0)
    place = lax.axis_index(axis)
    low = jnp.where(place == 0, RIM, 0)
    high = jnp.where(place == lax.axis_size(axis) - 1, RIM + own, own + 2 * RIM)
    return (row >= low) & (row < high)


def pack_y_kernel(u_lo, u_hi, b_lo, b_hi, s_lo, s_hi, near, far):
    width = u_lo.shape[1]

    def pack(out, u, b, s, low):
        u_rows = slice(0, 3) if low else slice(5, 8)
        two = slice(0, 2) if low else slice(6, 8)
        for h in range(2):
            lanes = slice(h * LANES, (h + 1) * LANES)
            for x in range(width):
                for c in range(3):
                    k = c * width + x
                    out[h, 3 * k : 3 * k + 3, :] = u[c, x, u_rows, lanes]
                    base = 9 * width + 2 * k
                    out[h, base : base + 2, :] = b[c, x, two, lanes]
                base = 15 * width + 2 * x
                out[h, base : base + 2, :] = s[x, two, lanes]

    even = is_even("narrow")

    @pl.when(even)
    def _():
        pack(near, u_hi, b_hi, s_hi, False)
        pack(far, u_lo, b_lo, s_lo, True)

    @pl.when(jnp.logical_not(even))
    def _():
        pack(near, u_lo, b_lo, s_lo, True)
        pack(far, u_hi, b_hi, s_hi, False)


def pack_y(u, b, s):
    _, width, height, depth = u.shape
    last = height // SUB - 1
    block = pl.BlockSpec((3, width, SUB, depth), lambda i: (0, 0, 0, 0))
    block_last = pl.BlockSpec((3, width, SUB, depth), lambda i: (0, 0, last, 0))
    plane = pl.BlockSpec((width, SUB, depth), lambda i: (0, 0, 0))
    plane_last = pl.BlockSpec((width, SUB, depth), lambda i: (0, last, 0))
    rows = 17 * width
    out = jax.ShapeDtypeStruct((2, rows, LANES), F32)
    whole = pl.BlockSpec((2, rows, LANES), lambda i: (0, 0, 0))
    return pl.pallas_call(
        pack_y_kernel,
        grid=(1,),
        in_specs=[block, block_last, block, block_last, plane, plane_last],
        out_specs=[whole, whole],
        out_shape=[out, out],
        compiler_params=params(),
        cost_estimate=cost(1),
        name="pack_y",
    )(u, u, b, b, s, s)


def residual_kernel(u, b, s, r0, near, far, ue):
    _, width, height, _ = u.shape
    for h in range(2):
        lanes = slice(h * LANES, (h + 1) * LANES)
        for x in range(width):
            for c in range(3):
                ue[c, x, h, 0:PAD, :] = jnp.zeros((PAD, LANES), F32)
                ue[c, x, h, PAD + height :, :] = jnp.zeros((PAD, LANES), F32)

        def fill(t, carry, h=h, lanes=lanes):
            rows = pl.ds(pl.multiple_of(t * SUB, SUB), SUB)
            to = pl.ds(pl.multiple_of(PAD + t * SUB, SUB), SUB)
            for x in range(width):
                for c in range(3):
                    ue[c, x, h, to, :] = u[c, x, rows, lanes]
            return carry

        lax.fori_loop(0, height // SUB, fill, 0)

    edges = edge_masks()

    def step(t, carry):
        start = PAD + t * SUB
        rows = pl.ds(pl.multiple_of(t * SUB, SUB), SUB)

        def plane(x):
            return Plane(lambda c, dy: [ue[c, x, h, pl.ds(start + dy, SUB), :] for h in range(2)])

        before, here = None, plane(0)
        for x in range(width):
            after = plane(x + 1) if x + 1 < width else None
            au = applied(before, here, after, [6.0 + s[x, rows, h * LANES : (h + 1) * LANES] for h in range(2)], edges)
            for c in range(3):
                for h in range(2):
                    r0[c, x, h, rows, :] = b[c, x, rows, h * LANES : (h + 1) * LANES] - au[c][h]
            before, here = here, after
        return carry

    lax.fori_loop(0, height // SUB, step, 0, unroll=2)

    def pack(out, edge, second):
        for c in range(3):
            out[c] = r0[c, edge]
            out[3 + c] = r0[c, second]
            out[6 + c] = ue[c, edge, :, PAD : PAD + height, :]
        for h in range(2):
            out[9, h] = s[edge, :, h * LANES : (h + 1) * LANES]

    even_x = is_even("wide")

    @pl.when(even_x)
    def _():
        pack(near, width - 1, width - 2)
        pack(far, 0, 1)

    @pl.when(jnp.logical_not(even_x))
    def _():
        pack(near, 0, 1)
        pack(far, width - 1, width - 2)


def residual(u, b, s):
    _, width, height, _ = u.shape
    side = jax.ShapeDtypeStruct((10, 2, height, LANES), F32)
    return pl.pallas_call(
        residual_kernel,
        out_shape=[pltpu.HBM((3, width, 2, height, LANES), F32), side, side],
        scratch_shapes=[pltpu.VMEM((3, width, 2, height + 2 * PAD, LANES), F32)],
        compiler_params=params(),
        cost_estimate=cost(3),
        name="residual",
    )(u, b, s)


def ends_kernel(
    u_lo, u_hi, b_lo, b_hi, s_lo, s_hi, got_near, got_far, main_near, main_far,
    r_end, s_end, near, far, ue, be, se, own,
):
    width = u_lo.shape[1]
    begin = (PAD + RIM, PAD - RIM)

    def place(e, u, b, s, halo):
        at = begin[e]
        low = e == 0
        three = slice(at - 3, at) if low else slice(at + SUB, at + SUB + 3)
        two = slice(at - 2, at) if low else slice(at + SUB, at + SUB + 2)
        for h in range(2):
            lanes = slice(h * LANES, (h + 1) * LANES)
            for x in range(width):
                for c in range(3):
                    k = c * width + x
                    ue[e, c, x, h, at : at + SUB, :] = u[c, x, :, lanes]
                    be[e, c, x, h, at : at + SUB, :] = b[c, x, :, lanes]
                    ue[e, c, x, h, three, :] = halo[h, 3 * k : 3 * k + 3, :]
                    base = 9 * width + 2 * k
                    be[e, c, x, h, two, :] = halo[h, base : base + 2, :]
                se[e, x, h, at : at + SUB, :] = s[x, :, lanes]
                base = 15 * width + 2 * x
                se[e, x, h, two, :] = halo[h, base : base + 2, :]

    even = is_even("narrow")

    @pl.when(even)
    def _():
        place(0, u_lo, b_lo, s_lo, got_far)
        place(1, u_hi, b_hi, s_hi, got_near)

    @pl.when(jnp.logical_not(even))
    def _():
        place(0, u_lo, b_lo, s_lo, got_near)
        place(1, u_hi, b_hi, s_hi, got_far)

    edges = edge_masks()

    def step(e, carry):
        inside = inside_rows(e * own + 2 * RIM * e - SUB * e, own, "narrow")

        def plane(x):
            return Plane(lambda c, dy: [ue[e, c, x, h, pl.ds(PAD + dy, SUB), :] for h in range(2)])

        before, here = None, plane(0)
        tile = pl.ds(PAD, SUB)
        for x in range(width):
            after = plane(x + 1) if x + 1 < width else None
            au = applied(before, here, after, [6.0 + se[e, x, h, tile, :] for h in range(2)], edges)
            for c in range(3):
                for h in range(2):
                    r_end[e, c, x, h] = jnp.where(inside, be[e, c, x, h, tile, :] - au[c][h], 0.0)
            for h in range(2):
                s_end[e, x, h] = se[e, x, h, tile, :]
            before, here = here, after
        return carry

    lax.fori_loop(0, 2, step, 0, unroll=2)

    def pack(out, main, edge, second):
        for k in range(10):
            out[k, :, SUB:own, :] = main[k, :, RIM : own - RIM, :]
        for e in range(2):
            tile = slice(e * own, e * own + SUB)
            for h in range(2):
                for c in range(3):
                    out[c, h, tile, :] = r_end[e, c, edge, h]
                    out[3 + c, h, tile, :] = r_end[e, c, second, h]
                    out[6 + c, h, tile, :] = ue[e, c, edge, h, PAD : PAD + SUB, :]
                out[9, h, tile, :] = s_end[e, edge, h]

    even_x = is_even("wide")

    @pl.when(even_x)
    def _():
        pack(near, main_near, width - 1, width - 2)
        pack(far, main_far, 0, 1)

    @pl.when(jnp.logical_not(even_x))
    def _():
        pack(near, main_near, 0, 1)
        pack(far, main_far, width - 1, width - 2)


def ends(u, b, s, got, main):
    _, width, height, depth = u.shape
    last = height // SUB - 1
    block = pl.BlockSpec((3, width, SUB, depth), lambda i: (0, 0, 0, 0))
    block_last = pl.BlockSpec((3, width, SUB, depth), lambda i: (0, 0, last, 0))
    plane = pl.BlockSpec((width, SUB, depth), lambda i: (0, 0, 0))
    plane_last = pl.BlockSpec((width, SUB, depth), lambda i: (0, last, 0))
    shapes = [(2, 3, width, 2, SUB, LANES), (2, width, 2, SUB, LANES)] + [(10, 2, height + 2 * RIM, LANES)] * 2

    def whole(shape):
        return pl.BlockSpec(shape, lambda i: (0,) * len(shape))

    def field(*lead):
        return pltpu.VMEM((2, *lead, 2, 3 * SUB, LANES), F32)

    def kernel(*refs):
        return ends_kernel(*refs, height)

    return pl.pallas_call(
        kernel,
        grid=(1,),
        in_specs=[block, block_last, block, block_last, plane, plane_last] + [whole(x.shape) for x in (*got, *main)],
        out_specs=[whole(shape) for shape in shapes],
        out_shape=[pltpu.HBM(shape, F32) for shape in shapes[:2]]
        + [jax.ShapeDtypeStruct(shape, F32) for shape in shapes[2:]],
        scratch_shapes=[field(3, width), field(3, width), field(width)],
        compiler_params=params(),
        cost_estimate=cost(40),
        name="ends",
    )(u, u, b, b, s, s, *got, *main)


def full(value):
    return jnp.full((SUB, LANES), value, F32)


def chebyshev_numbers(bounds, steps):
    low, high = full(bounds[0]), full(bounds[1])
    middle = (high + low) / 2.0
    radius = (high - low) / 2.0
    stretch = middle / radius
    rho = 1.0 / stretch
    factors = []
    for _ in range(steps - 1):
        rho_next = 1.0 / (2.0 * stretch - rho)
        factors.append((rho_next * rho, 2.0 * rho_next / radius))
        rho = rho_next
    return 1.0 / middle, factors


def z_matrix(rest_zt):
    shape = (2 * LANES, LANES)
    offset = lax.broadcasted_iota(jnp.int32, shape, 0) - 2 * lax.broadcasted_iota(jnp.int32, shape, 1) + 2
    out = jnp.zeros(shape, F32)
    for a in range(5):
        out = out + jnp.where(offset == a, rest_zt[a : a + 1, :], 0.0)
    return out


def y_weights(rest_y, a, rows, own):
    start = pl.multiple_of(lax.axis_index("narrow") * own, SUB)
    return jnp.broadcast_to(rest_y[pl.ds(start, rows), a : a + 1], (rows, LANES))


def smooth_kernel(
    bounds, rest_x, r0p, r_end, s_end, got_near, got_far, sent_near, sent_far, u, s, rest_y, rest_zt,
    smooth, partial, near, far, left, right, u_left, u_right, s_ext, r0, d1, r1, r2, t_pad, zr,
):
    _, width, height, _ = u.shape
    tiles = (height + 2 * RIM) // SUB
    window = slice(PAD, PAD + height + 2 * RIM)
    middle = slice(PAD + SUB, PAD + height)
    tile_rows = [slice(PAD, PAD + SUB), slice(PAD + height, PAD + height + SUB)]
    even_x = is_even("wide")
    zr[0], zr[1] = split(z_matrix(rest_zt))

    def place(from_left, from_right, mine_left, mine_right):
        for k in range(10):
            left[k, :, window, :] = from_left[k]
            right[k, :, window, :] = from_right[k]
        for c in range(3):
            u_left[c, :, window, :] = mine_left[6 + c]
            u_right[c, :, window, :] = mine_right[6 + c]

    @pl.when(even_x)
    def _():
        place(got_far, got_near, sent_far, sent_near)

    @pl.when(jnp.logical_not(even_x))
    def _():
        place(got_near, got_far, sent_near, sent_far)

    for x in range(width):
        for h in range(2):
            s_ext[x, h, middle, :] = s[x, RIM : height - RIM, h * LANES : (h + 1) * LANES]
        for e in range(2):
            s_ext[x, :, tile_rows[e], :] = s_end[e, x]
            for c in range(3):
                r0[c, x + 2, :, tile_rows[e], :] = r_end[e, c, x]
        for c in range(3):
            r0[c, x + 2, :, middle, :] = r0p[c, x, :, RIM : height - RIM, :]

    edges = edge_masks()
    place_x = lax.axis_index("wide")
    has_left = place_x > 0
    has_right = place_x < lax.axis_size("wide") - 1
    inverse, factors = chebyshev_numbers(bounds, 2)
    factor_d = factors[0][0] * inverse
    factor_r = factors[0][1]

    def fix(t, carry):
        start = PAD + t * SUB
        rows = pl.ds(start, SUB)
        inside = inside_rows(t * SUB, height, "narrow")

        def of(ref, first):
            return shares(lambda c, dy: [ref[first + c, h, pl.ds(start + dy, SUB), :] for h in range(2)], edges)

        out_left, _ = of(left, 6)
        _, in_left = of(u_left, 0)
        in_right, _ = of(u_right, 0)
        _, out_right = of(right, 6)
        inside_left = inside & has_left
        inside_right = inside & has_right
        for c in range(3):
            for h in range(2):
                r0[c, 0, h, rows, :] = left[3 + c, h, rows, :]
                r0[c, 1, h, rows, :] = jnp.where(
                    inside_left, left[c, h, rows, :] + in_left[c][h], 0.0
                )
                r0[c, 2, h, rows, :] = jnp.where(
                    inside, r0[c, 2, h, rows, :] + out_left[c][h], 0.0
                )
                r0[c, width + 1, h, rows, :] = jnp.where(
                    inside, r0[c, width + 1, h, rows, :] + out_right[c][h], 0.0
                )
                r0[c, width + 2, h, rows, :] = jnp.where(
                    inside_right, right[c, h, rows, :] + in_right[c][h], 0.0
                )
                r0[c, width + 3, h, rows, :] = right[3 + c, h, rows, :]
        return carry

    lax.fori_loop(0, tiles, fix, 0, unroll=3)

    def first_step(t, carry):
        start = PAD + t * SUB
        rows = pl.ds(start, SUB)
        inside = inside_rows(t * SUB, height, "narrow")

        def plane(x):
            return Plane(lambda c, dy: [r0[c, x + 2, h, pl.ds(start + dy, SUB), :] for h in range(2)])

        before, here = plane(-2), plane(-1)
        for x in range(-1, width + 1):
            after = plane(x + 1)
            keep = inside & has_left if x < 0 else inside & has_right if x == width else inside
            source = left.at[9] if x < 0 else right.at[9] if x == width else s_ext.at[x]
            diagonal = [6.0 + source[h, rows, :] for h in range(2)]
            ar = applied(before, here, after, diagonal, edges)
            for c in range(3):
                for h in range(2):
                    old = here.v[c][h]
                    new = old - inverse * ar[c][h]
                    d1[c, x + 1, h, rows, :] = jnp.where(keep, factor_d * old + factor_r * new, 0.0)
                    if 0 <= x < width:
                        r1[c, x, h, rows, :] = new
            before, here = here, after
        return carry

    lax.fori_loop(0, tiles, first_step, 0, unroll=3)

    def second_step(t, carry):
        start = PAD + RIM + t * SUB
        rows = pl.ds(start, SUB)
        to = pl.ds(pl.multiple_of(t * SUB, SUB), SUB)

        def plane(x):
            return Plane(lambda c, dy: [d1[c, x + 1, h, pl.ds(start + dy, SUB), :] for h in range(2)])

        before, here = plane(-1), plane(0)
        for x in range(width):
            after = plane(x + 1)
            diagonal = [6.0 + s_ext[x, h, rows, :] for h in range(2)]
            ad = applied(before, here, after, diagonal, edges)
            for c in range(3):
                for h in range(2):
                    lanes = slice(h * LANES, (h + 1) * LANES)
                    r2[c, x, h, to, :] = r1[c, x, h, rows, :] - ad[c][h]
                    step = inverse * r0[c, x + 2, h, rows, :] + here.v[c][h]
                    smooth[c, x, to, lanes] = u[c, x, to, lanes] + step
            before, here = here, after
        return carry

    lax.fori_loop(0, height // SUB, second_step, 0, unroll=2)

    coarse_width = width // 2
    coarse_height = height // 2
    coarse_rows = coarse_height + 2 * RIM
    first_weight = place_x * coarse_width
    lead = 2 * RIM + 2
    zr_halves = zr[0], zr[1]
    for c in range(3):
        for i in range(-1, coarse_width + 1):
            k = c * (coarse_width + 2) + i + 1
            terms = [(a, 2 * i - 2 + a) for a in range(5) if 0 <= 2 * i - 2 + a < width]
            halves = []
            for h in range(2):
                total = None
                for a, x in terms:
                    piece = rest_x[first_weight + i + 1, a] * r2[c, x, h]
                    total = piece if total is None else total + piece
                halves.append(total)
            joined = jnp.concatenate(halves, axis=1)
            t_pad[k, 0:lead, :] = jnp.zeros((lead, LANES), F32)
            t_pad[k, lead + height :, :] = jnp.zeros((t_pad.shape[1] - lead - height, LANES), F32)
            t_pad[k, lead : lead + height, :] = product(joined, zr_halves, 0)
    weights = [y_weights(rest_y, a, coarse_rows, coarse_height) for a in range(5)]
    even_y = is_even("narrow")
    for c in range(3):
        for i in range(coarse_width + 2):
            k = c * (coarse_width + 2) + i
            total = None
            for a in range(5):
                piece = weights[a] * t_pad[k, pl.ds(a, coarse_rows, stride=2), :]
                total = piece if total is None else total + piece
            partial[c, i] = total

    def send(out, first):
        for c in range(3):
            for i in range(coarse_width + 2):
                out[c * (coarse_width + 2) + i] = partial[c, i, first : first + SUB, :]

    @pl.when(even_y)
    def _():
        send(near, coarse_rows - SUB)
        send(far, 0)

    @pl.when(jnp.logical_not(even_y))
    def _():
        send(near, 0)
        send(far, coarse_rows - SUB)


def split(x):
    high = x.astype(jnp.bfloat16)
    return high, (x - high.astype(F32)).astype(jnp.bfloat16)


def product(x, halves, contract):
    high, low = split(x)
    dims = (((1,), (contract,)), ((), ()))

    def dot(p, q):
        return lax.dot_general(p, q, dims, preferred_element_type=F32)

    return dot(high, halves[0]) + (dot(high, halves[1]) + dot(low, halves[0]))


SMEM = pl.BlockSpec(memory_space=pltpu.SMEM)
VMEM = pl.BlockSpec(memory_space=pltpu.VMEM)


def smoothing(bounds, rest_x, r0p, r_end, s_end, got, sent, u, s, rest_y, rest_zt):
    _, width, height, depth = u.shape
    padded = height + 2 * (RIM + PAD)
    planes = 3 * (width // 2 + 2)
    coarse_rows = height // 2 + 2 * RIM
    tile = jax.ShapeDtypeStruct((planes, SUB, LANES), F32)

    def field(*lead):
        return pltpu.VMEM((*lead, 2, padded, LANES), F32)

    return pl.pallas_call(
        smooth_kernel,
        in_specs=[SMEM, SMEM] + [VMEM] * 11,
        out_shape=[
            jax.ShapeDtypeStruct((3, width, height, depth), F32),
            jax.ShapeDtypeStruct((3, width // 2 + 2, coarse_rows, LANES), F32),
            tile,
            tile,
        ],
        scratch_shapes=[
            field(10),
            field(10),
            field(3),
            field(3),
            field(width),
            field(3, width + 4),
            field(3, width + 2),
            field(3, width),
            pltpu.VMEM((3, width, 2, height, LANES), F32),
            pltpu.VMEM((planes, 2 * coarse_rows + 2 * SUB, LANES), F32),
            pltpu.VMEM((2, 2 * LANES, LANES), jnp.bfloat16),
        ],
        compiler_params=params(),
        cost_estimate=cost(10),
        name="smoothing",
    )(bounds, rest_x, r0p, r_end, s_end, *got, *sent, u, s, rest_y, rest_zt)


def rows_kernel(partial, got_near, got_far, s, q, s_win, near, far):
    _, planes, rows, _ = partial.shape
    own = rows - 2 * RIM
    coarse_width = planes - 2
    n = lax.axis_index("narrow")
    even_y = is_even("narrow")
    q[:, :, SUB : rows - SUB, :] = partial[:, :, SUB : rows - SUB, :]

    def join(low, high):
        for c in range(3):
            for i in range(planes):
                k = c * planes + i
                q[c, i, 0:SUB, :] = partial[c, i, 0:SUB, :] + low[k]
                q[c, i, rows - SUB :, :] = partial[c, i, rows - SUB :, :] + high[k]

    @pl.when(even_y)
    def _():
        join(got_far, got_near)

    @pl.when(jnp.logical_not(even_y))
    def _():
        join(got_near, got_far)

    total = s.shape[1]
    start = pl.multiple_of(n * own, SUB)
    before = pl.multiple_of(jnp.maximum(start - SUB, 0), SUB)
    after = pl.multiple_of(jnp.minimum(start + own, total - SUB), SUB)
    for x in range(coarse_width):
        s_win[x, RIM : RIM + own, :] = s[x, pl.ds(start, own), :]
        s_win[x, 0:RIM, :] = s[x, pl.ds(before, SUB), :][SUB - RIM :, :]
        s_win[x, RIM + own :, :] = s[x, pl.ds(after, SUB), :][0:RIM, :]

    def pack(out, to_left):
        first = 0 if to_left else 2
        for c in range(3):
            for k in range(coarse_width):
                out[c * coarse_width + k] = q[c, first + k]
        edge = 0 if to_left else coarse_width - 2
        for k in range(2):
            out[3 * coarse_width + k] = s_win[edge + k]

    even_x = is_even("wide")

    @pl.when(even_x)
    def _():
        pack(near, False)
        pack(far, True)

    @pl.when(jnp.logical_not(even_x))
    def _():
        pack(near, True)
        pack(far, False)


def rows(partial, got_near, got_far, s):
    _, planes, height, _ = partial.shape
    width = planes - 2
    side = jax.ShapeDtypeStruct((3 * width + 2, height, LANES), F32)
    return pl.pallas_call(
        rows_kernel,
        out_shape=[
            jax.ShapeDtypeStruct(partial.shape, F32),
            jax.ShapeDtypeStruct((width, height, LANES), F32),
            side,
            side,
        ],
        compiler_params=params(),
        cost_estimate=cost(1),
        name="coarse_rows",
    )(partial, got_near, got_far, s)


def coarse_kernel(bounds, q, s_win, got_near, got_far, out, own_out, near, far, left, right, r, d, total, sc):
    _, planes, height, _ = q.shape
    width = planes - 2
    own = height - 2 * RIM
    tiles = height // SUB
    window = slice(PAD, PAD + height)
    even_x = is_even("wide")
    place_x = lax.axis_index("wide")
    has_left = place_x > 0
    has_right = place_x < lax.axis_size("wide") - 1
    inverse, factors = chebyshev_numbers(bounds, 4)
    edges = edge_masks()
    reach = 3

    def place(from_left, from_right):
        left[...] = from_left[...]
        right[...] = from_right[...]

    @pl.when(even_x)
    def _():
        place(got_far, got_near)

    @pl.when(jnp.logical_not(even_x))
    def _():
        place(got_near, got_far)

    for k in range(2):
        sc[k] = left[3 * width + k]
        sc[width + 2 + k] = right[3 * width + k]
    for x in range(width):
        sc[x + 2] = s_win[x]

    def start_rows(t, carry):
        rows = pl.ds(pl.multiple_of(t * SUB, SUB), SUB)
        to = pl.ds(pl.multiple_of(PAD + t * SUB, SUB), SUB)
        for c in range(3):
            for i in range(-reach, width + reach):
                value = None
                if -1 <= i <= width:
                    value = q[c, i + 1, rows, :]
                if i <= 0:
                    other = left[c * width + i + reach, rows, :]
                    value = other if value is None else value + other
                if i >= width - 1:
                    other = right[c * width + i - width + 1, rows, :]
                    value = other if value is None else value + other
                r[c, i + reach, to, :] = value
                first = inverse * value
                d[c, i + reach, to, :] = first
                if 0 <= i < width:
                    total[c, i, to, :] = first
        return carry

    lax.fori_loop(0, tiles, start_rows, 0, unroll=5)

    for k in range(3):
        factor_d, factor_r = factors[k]
        rim = reach - 1 - k

        def residual_step(t, carry, rim=rim):
            start = PAD + t * SUB
            rows = pl.ds(start, SUB)
            inside = inside_rows(t * SUB, own, "narrow")

            def plane(x):
                return Plane(lambda c, dy: [d[c, x + reach, pl.ds(start + dy, SUB), :]])

            before, here = plane(-rim - 1), plane(-rim)
            for x in range(-rim, width + rim):
                after = plane(x + 1)
                keep = inside & has_left if x < 0 else inside & has_right if x >= width else inside
                ad = applied(before, here, after, [6.0 + sc[x + 2, pl.ds(t * SUB, SUB), :]], edges)
                for c in range(3):
                    new = r[c, x + reach, rows, :] - ad[c][0]
                    r[c, x + reach, rows, :] = jnp.where(keep, new, 0.0)
                before, here = here, after
            return carry

        lax.fori_loop(0, tiles, residual_step, 0, unroll=5)

        def direction_step(t, carry, rim=rim, factor_d=factor_d, factor_r=factor_r):
            rows = pl.ds(pl.multiple_of(PAD + t * SUB, SUB), SUB)
            for c in range(3):
                for x in range(-rim, width + rim):
                    new = factor_d * d[c, x + reach, rows, :] + factor_r * r[c, x + reach, rows, :]
                    d[c, x + reach, rows, :] = new
                    if 0 <= x < width:
                        total[c, x, rows, :] = total[c, x, rows, :] + new
            return carry

        lax.fori_loop(0, tiles, direction_step, 0, unroll=5)

    for c in range(3):
        for x in range(width):
            out[c, x] = total[c, x, window, :]
            own_out[c, x] = total[c, x, PAD + RIM : PAD + RIM + own, :]

    def send(ref, x):
        for c in range(3):
            ref[c] = total[c, x, window, :]

    @pl.when(even_x)
    def _():
        send(near, width - 1)
        send(far, 0)

    @pl.when(jnp.logical_not(even_x))
    def _():
        send(near, 0)
        send(far, width - 1)


def coarse_solve(bounds, q, s_win, got_near, got_far):
    _, planes, height, _ = q.shape
    width = planes - 2
    side = (3 * width + 2, height, LANES)
    edge = jax.ShapeDtypeStruct((3, height, LANES), F32)

    def field(count):
        return pltpu.VMEM((3, count, height + 2 * PAD, LANES), F32)

    return pl.pallas_call(
        coarse_kernel,
        in_specs=[SMEM] + [VMEM] * 4,
        out_shape=[
            jax.ShapeDtypeStruct((3, width, height, LANES), F32),
            jax.ShapeDtypeStruct((3, width, height - 2 * RIM, LANES), F32),
            edge,
            edge,
        ],
        scratch_shapes=[
            pltpu.VMEM(side, F32),
            pltpu.VMEM(side, F32),
            field(width + 6),
            field(width + 6),
            field(width),
            pltpu.VMEM((width + 4, height, LANES), F32),
        ],
        compiler_params=params(),
        cost_estimate=cost(3),
        name="coarse_solve",
    )(bounds, q, s_win, got_near, got_far)


def prolong_kernel(rest_x, corr, got_near, got_far, smooth, rest_y, rest_zt, out, left, right, wy, col, grown):
    _, width, height, _ = corr.shape
    own = height - 2 * RIM
    fine_width = 2 * width
    even_x = is_even("wide")
    first_weight = lax.axis_index("wide") * width
    zr = split(z_matrix(rest_zt))
    for a in range(5):
        wy[a] = y_weights(rest_y, a, height, own)

    def place(from_left, from_right):
        left[...] = from_left[...]
        right[...] = from_right[...]

    @pl.when(even_x)
    def _():
        place(got_far, got_near)

    @pl.when(jnp.logical_not(even_x))
    def _():
        place(got_near, got_far)

    def row(c, i):
        return left[c] if i < 0 else right[c] if i == width else corr[c, i]

    for c in range(3):
        for x in range(fine_width):
            total = None
            for a in range(x % 2, 5, 2):
                i = (x + 2 - a) // 2
                piece = rest_x[first_weight + i + 1, a] * row(c, i)
                total = piece if total is None else total + piece
            col[...] = total

            def at(a, shift):
                rows = pl.ds(RIM + shift, own)
                return wy[a, rows, :] * col[rows, :]

            grown[x, pl.ds(0, own, stride=2), :] = at(0, 1) + at(2, 0) + at(4, -1)
            grown[x, pl.ds(1, own, stride=2), :] = at(1, 1) + at(3, 0)
        flat = grown[...].reshape(fine_width * 2 * own, LANES)
        wide = product(flat, zr, 1)
        out[c] = smooth[c] + wide.reshape(fine_width, 2 * own, 2 * LANES)


def prolong(rest_x, corr, got_near, got_far, smooth, rest_y, rest_zt):
    _, width, height, _ = corr.shape
    own = height - 2 * RIM
    return pl.pallas_call(
        prolong_kernel,
        in_specs=[SMEM] + [VMEM] * 6,
        out_shape=jax.ShapeDtypeStruct(smooth.shape, F32),
        scratch_shapes=[
            pltpu.VMEM((3, height, LANES), F32),
            pltpu.VMEM((3, height, LANES), F32),
            pltpu.VMEM((5, height, LANES), F32),
            pltpu.VMEM((height, LANES), F32),
            pltpu.VMEM((2 * width, 2 * own, LANES), F32),
        ],
        compiler_params=params(),
        cost_estimate=cost(12),
        name="prolong",
    )(rest_x, corr, got_near, got_far, smooth, rest_y, rest_zt)


def gather(own, edges, prolonged):
    count = lax.axis_size("narrow")

    def ring(x, by):
        return lax.ppermute(x, "narrow", [(i, (i + by) % count) for i in range(count)])

    after = lax.optimization_barrier
    pair = swap_near(own, "narrow")
    low, high = ring(own, 2), ring(own, -2)
    def across(x, by):
        return lax.ppermute(x, "narrow", [(i, ((i + by) % count) ^ 1) for i in range(count)])

    pair_low, pair_high = across(own, 2), across(own, -2)
    first, second, edges = after((low, pair_high, edges))
    far_own, far_pair = ring(first, 2), ring(second, -2)
    result = prolonged(edges)
    return [own, pair, low, high, pair_low, pair_high, far_own, far_pair], result


def assemble_kernel(*refs):
    blocks, out = refs[:-1], refs[-1]
    count = len(blocks)
    n = lax.axis_index("narrow")
    m = n + 1 - 2 * lax.rem(n, 2)
    own = blocks[0].shape[2]
    sources = [n, m, n - 2, n + 2, m - 2, m + 2, n - 4, m + 4]
    for block, source in zip(blocks, sources):
        start = pl.multiple_of(lax.rem(source + count, count) * own, SUB)
        out[:, :, pl.ds(start, own), :] = block[...]


def assemble(blocks):
    three, width, own, lanes = blocks[0].shape
    return pl.pallas_call(
        assemble_kernel,
        out_shape=jax.ShapeDtypeStruct((three, width, own * len(blocks), lanes), F32),
        compiler_params=params(),
        cost_estimate=cost(1),
        name="assemble",
    )(*blocks)


def body(
    right_side,
    start_guess,
    reaction,
    coarse_reaction,
    rest_x,
    rest_y,
    rest_z,
    fine_bounds,
    coarse_bounds,
):
    x_weights = jnp.pad(rest_x, ((1, 1), (0, 0)))
    y_padded = jnp.pad(rest_y, ((RIM, RIM), (0, 0)))
    z_weights = rest_z.T
    from_hbm = [pltpu.with_memory_space_constraint(x, pltpu.HBM) for x in (start_guess, right_side, reaction)]
    got = swap_both(pack_y(*from_hbm), "narrow")
    r0p, *main = residual(start_guess, right_side, reaction)
    r_end, s_end, *sent = ends(start_guess, right_side, reaction, got, main)
    got = swap_both(sent, "wide")
    r0p, r_end, s_end = (pltpu.with_memory_space_constraint(x, pltpu.HBM) for x in (r0p, r_end, s_end))
    smooth, partial, *sent = smoothing(
        fine_bounds, x_weights, r0p, r_end, s_end, got, sent, start_guess, reaction, y_padded, z_weights
    )
    got = swap_both(sent, "narrow")
    q, s_win, *sent = rows(partial, *got, coarse_reaction)
    got = swap_both(sent, "wide")
    corr, own, *sent = coarse_solve(coarse_bounds, q, s_win, *got)
    edges = swap_both(sent, "wide")
    blocks, solution_block = gather(
        own, edges, lambda edges: prolong(x_weights, corr, *edges, smooth, y_padded, z_weights)
    )
    return solution_block, assemble(blocks)


def solution(mesh):
    return jax.shard_map(
        body,
        mesh=mesh,
        in_specs=(
            P(None, "wide", "narrow", None),
            P(None, "wide", "narrow", None),
            P("wide", "narrow", None),
            P("wide", None, None),
            P(),
            P(),
            P(),
            P(),
            P(),
        ),
        out_specs=(P(None, "wide", "narrow", None), P(None, "wide", None, None)),
        check_vma=False,
    )
```

```python
import jax
import jax.numpy as jnp
from jax import lax
from jax.experimental import pallas as pl
from jax.experimental.pallas import tpu as pltpu
from jax.sharding import PartitionSpec as P

F32 = jnp.float32
LANES = 128
SUB = 8
RIM = 4
PAD = 8
MIB = 1024 * 1024
BYTES_PER_US = 3_690_000


def params(mib=24):
    return pltpu.CompilerParams(vmem_limit_bytes=mib * MIB)


def cost(us):
    return pl.CostEstimate(flops=0, bytes_accessed=int(us * BYTES_PER_US), transcendentals=0)


def swap_near(x, axis):
    count = lax.axis_size(axis)
    return lax.ppermute(x, axis, [(i, i ^ 1) for i in range(count)])


def swap_far(x, axis):
    count = lax.axis_size(axis)
    up = [(i, i + 1) for i in range(1, count - 1, 2)]
    return lax.ppermute(x, axis, up + [(j, i) for i, j in up])


def swap_both(pair, axis):
    return [swap_near(pair[0], axis), swap_far(pair[1], axis)]


def is_even(axis):
    return lax.rem(lax.axis_index(axis), 2) == 0


def lane_index():
    return lax.broadcasted_iota(jnp.int32, (SUB, LANES), 1)


def z_next(parts, last):
    rolled = [pltpu.roll(part, LANES - 1, 1) for part in parts]
    beyond = rolled[1:] + [jnp.zeros_like(parts[0])]
    return [jnp.where(last, b, r) for r, b in zip(rolled, beyond)]


def z_before(parts, first):
    rolled = [pltpu.roll(part, 1, 1) for part in parts]
    beyond = [jnp.zeros_like(parts[0])] + rolled[:-1]
    return [jnp.where(first, b, r) for r, b in zip(rolled, beyond)]


def each(fn, *lists):
    return [fn(*items) for items in zip(*lists)]


def add(a, b):
    return each(lambda p, q: p + q, a, b)


def sub(a, b):
    return each(lambda p, q: p - q, a, b)


def eighth(a):
    return each(lambda p: 0.125 * p, a)


class Plane:
    def __init__(self, load):
        self.v = [load(c, 0) for c in range(3)]
        above = [load(c, 1) for c in range(3)]
        below = [load(c, -1) for c in range(3)]
        self.along_y = [add(above[c], below[c]) for c in range(3)]
        self.dy = [eighth(sub(above[c], below[c])) for c in range(3)]


def applied(before, plane, after, diagonal, edges):
    first, last = edges
    v, dy = plane.v, plane.dy

    def difference(pick):
        if before is None:
            return pick(after)
        if after is None:
            return each(lambda p: -p, pick(before))
        return sub(pick(after), pick(before))

    slope = [
        eighth(difference(lambda q: q.v[2])),
        dy[2],
        add(eighth(difference(lambda q: q.v[0])), dy[1]),
    ]
    cross = [difference(lambda q: q.dy[1]), difference(lambda q: q.dy[0]), None]
    out = []
    for c in range(3):
        near = plane.along_y[c]
        for other in (before, after):
            if other is not None:
                near = add(near, other.v[c])
        total = each(lambda d, p, q: d * p - q, diagonal, v[c], near)
        if cross[c] is not None:
            total = add(total, cross[c])
        total = add(total, z_next(sub(slope[c], v[c]), last))
        out.append(sub(total, z_before(add(slope[c], v[c]), first)))
    return out


def shares(load, edges):
    first, last = edges
    plane = Plane(load)
    v, dy = plane.v, plane.dy
    along_z = [sub(z_next(v[c], last), z_before(v[c], first)) for c in (0, 2)]
    slope = [add(dy[1], eighth(along_z[1])), dy[0], eighth(along_z[0])]
    return [add(v[c], slope[c]) for c in range(3)], [sub(v[c], slope[c]) for c in range(3)]


def edge_masks():
    lane = lane_index()
    return lane == 0, lane == LANES - 1


def inside_rows(start, own, axis):
    row = start + lax.broadcasted_iota(jnp.int32, (SUB, LANES), 0)
    place = lax.axis_index(axis)
    low = jnp.where(place == 0, RIM, 0)
    high = jnp.where(place == lax.axis_size(axis) - 1, RIM + own, own + 2 * RIM)
    return (row >= low) & (row < high)


def pack_y_kernel(u_lo, u_hi, b_lo, b_hi, s_lo, s_hi, near, far):
    width = u_lo.shape[1]

    def pack(out, u, b, s, low):
        u_rows = slice(0, 3) if low else slice(5, 8)
        two = slice(0, 2) if low else slice(6, 8)
        for h in range(2):
            lanes = slice(h * LANES, (h + 1) * LANES)
            for x in range(width):
                for c in range(3):
                    k = c * width + x
                    out[h, 3 * k : 3 * k + 3, :] = u[c, x, u_rows, lanes]
                    base = 9 * width + 2 * k
                    out[h, base : base + 2, :] = b[c, x, two, lanes]
                base = 15 * width + 2 * x
                out[h, base : base + 2, :] = s[x, two, lanes]

    even = is_even("narrow")

    @pl.when(even)
    def _():
        pack(near, u_hi, b_hi, s_hi, False)
        pack(far, u_lo, b_lo, s_lo, True)

    @pl.when(jnp.logical_not(even))
    def _():
        pack(near, u_lo, b_lo, s_lo, True)
        pack(far, u_hi, b_hi, s_hi, False)


def pack_y(u, b, s):
    _, width, height, depth = u.shape
    last = height // SUB - 1
    block = pl.BlockSpec((3, width, SUB, depth), lambda i: (0, 0, 0, 0))
    block_last = pl.BlockSpec((3, width, SUB, depth), lambda i: (0, 0, last, 0))
    plane = pl.BlockSpec((width, SUB, depth), lambda i: (0, 0, 0))
    plane_last = pl.BlockSpec((width, SUB, depth), lambda i: (0, last, 0))
    rows = 17 * width
    out = jax.ShapeDtypeStruct((2, rows, LANES), F32)
    whole = pl.BlockSpec((2, rows, LANES), lambda i: (0, 0, 0))
    return pl.pallas_call(
        pack_y_kernel,
        grid=(1,),
        in_specs=[block, block_last, block, block_last, plane, plane_last],
        out_specs=[whole, whole],
        out_shape=[out, out],
        compiler_params=params(),
        cost_estimate=cost(1),
        name="pack_y",
    )(u, u, b, b, s, s)


def residual_kernel(u, b, s, r0, s_out, near, far, ue):
    _, width, height, _ = u.shape
    for h in range(2):
        lanes = slice(h * LANES, (h + 1) * LANES)
        for x in range(width):
            for c in range(3):
                ue[c, x, h, 0:PAD, :] = jnp.zeros((PAD, LANES), F32)
                ue[c, x, h, PAD + height :, :] = jnp.zeros((PAD, LANES), F32)

        def fill(t, carry, h=h, lanes=lanes):
            rows = pl.ds(pl.multiple_of(t * SUB, SUB), SUB)
            to = pl.ds(pl.multiple_of(PAD + t * SUB, SUB), SUB)
            for x in range(width):
                for c in range(3):
                    ue[c, x, h, to, :] = u[c, x, rows, lanes]
            return carry

        lax.fori_loop(0, height // SUB, fill, 0)

    edges = edge_masks()

    def step(t, carry):
        start = PAD + t * SUB
        rows = pl.ds(pl.multiple_of(t * SUB, SUB), SUB)
        to = pl.ds(RIM + t * SUB, SUB)

        def plane(x):
            return Plane(lambda c, dy: [ue[c, x, h, pl.ds(start + dy, SUB), :] for h in range(2)])

        before, here = None, plane(0)
        for x in range(width):
            after = plane(x + 1) if x + 1 < width else None
            au = applied(before, here, after, [6.0 + s[x, rows, h * LANES : (h + 1) * LANES] for h in range(2)], edges)
            for c in range(3):
                for h in range(2):
                    r0[c, x, h, to, :] = b[c, x, rows, h * LANES : (h + 1) * LANES] - au[c][h]
            for h in range(2):
                s_out[x, h, to, :] = s[x, rows, h * LANES : (h + 1) * LANES]
            before, here = here, after
        return carry

    lax.fori_loop(0, height // SUB, step, 0, unroll=2)
    own = slice(RIM, RIM + height)

    def pack(out, edge, second):
        for c in range(3):
            out[c] = r0[c, edge, :, own, :]
            out[3 + c] = r0[c, second, :, own, :]
            out[6 + c] = ue[c, edge, :, PAD : PAD + height, :]
        for h in range(2):
            out[9, h] = s[edge, :, h * LANES : (h + 1) * LANES]

    even_x = is_even("wide")

    @pl.when(even_x)
    def _():
        pack(near, width - 1, width - 2)
        pack(far, 0, 1)

    @pl.when(jnp.logical_not(even_x))
    def _():
        pack(near, 0, 1)
        pack(far, width - 1, width - 2)


def residual(u, b, s):
    _, width, height, _ = u.shape
    side = jax.ShapeDtypeStruct((10, 2, height, LANES), F32)
    return pl.pallas_call(
        residual_kernel,
        out_shape=[
            pltpu.HBM((3, width, 2, height + 2 * RIM, LANES), F32),
            pltpu.HBM((width, 2, height + 2 * RIM, LANES), F32),
            side,
            side,
        ],
        scratch_shapes=[pltpu.VMEM((3, width, 2, height + 2 * PAD, LANES), F32)],
        compiler_params=params(),
        cost_estimate=cost(3),
        name="residual",
    )(u, b, s)


def ends_kernel(
    u_lo, u_hi, b_lo, b_hi, s_lo, s_hi, got_near, got_far, main_near, main_far,
    r_end, s_end, near, far, ue, be, se, own,
):
    width = u_lo.shape[1]
    begin = (PAD + RIM, PAD - RIM)

    def place(e, u, b, s, halo):
        at = begin[e]
        low = e == 0
        three = slice(at - 3, at) if low else slice(at + SUB, at + SUB + 3)
        two = slice(at - 2, at) if low else slice(at + SUB, at + SUB + 2)
        for h in range(2):
            lanes = slice(h * LANES, (h + 1) * LANES)
            for x in range(width):
                for c in range(3):
                    k = c * width + x
                    ue[e, c, x, h, at : at + SUB, :] = u[c, x, :, lanes]
                    be[e, c, x, h, at : at + SUB, :] = b[c, x, :, lanes]
                    ue[e, c, x, h, three, :] = halo[h, 3 * k : 3 * k + 3, :]
                    base = 9 * width + 2 * k
                    be[e, c, x, h, two, :] = halo[h, base : base + 2, :]
                se[e, x, h, at : at + SUB, :] = s[x, :, lanes]
                base = 15 * width + 2 * x
                se[e, x, h, two, :] = halo[h, base : base + 2, :]

    even = is_even("narrow")

    @pl.when(even)
    def _():
        place(0, u_lo, b_lo, s_lo, got_far)
        place(1, u_hi, b_hi, s_hi, got_near)

    @pl.when(jnp.logical_not(even))
    def _():
        place(0, u_lo, b_lo, s_lo, got_near)
        place(1, u_hi, b_hi, s_hi, got_far)

    edges = edge_masks()

    def step(e, carry):
        inside = inside_rows(e * own + 2 * RIM * e - SUB * e, own, "narrow")

        def plane(x):
            return Plane(lambda c, dy: [ue[e, c, x, h, pl.ds(PAD + dy, SUB), :] for h in range(2)])

        before, here = None, plane(0)
        tile = pl.ds(PAD, SUB)
        for x in range(width):
            after = plane(x + 1) if x + 1 < width else None
            au = applied(before, here, after, [6.0 + se[e, x, h, tile, :] for h in range(2)], edges)
            for c in range(3):
                for h in range(2):
                    r_end[e, c, x, h] = jnp.where(inside, be[e, c, x, h, tile, :] - au[c][h], 0.0)
            for h in range(2):
                s_end[e, x, h] = se[e, x, h, tile, :]
            before, here = here, after
        return carry

    lax.fori_loop(0, 2, step, 0, unroll=2)

    def pack(out, main, edge, second):
        for k in range(10):
            out[k, :, SUB:own, :] = main[k, :, RIM : own - RIM, :]
        for e in range(2):
            tile = slice(e * own, e * own + SUB)
            for h in range(2):
                for c in range(3):
                    out[c, h, tile, :] = r_end[e, c, edge, h]
                    out[3 + c, h, tile, :] = r_end[e, c, second, h]
                    out[6 + c, h, tile, :] = ue[e, c, edge, h, PAD : PAD + SUB, :]
                out[9, h, tile, :] = s_end[e, edge, h]

    even_x = is_even("wide")

    @pl.when(even_x)
    def _():
        pack(near, main_near, width - 1, width - 2)
        pack(far, main_far, 0, 1)

    @pl.when(jnp.logical_not(even_x))
    def _():
        pack(near, main_near, 0, 1)
        pack(far, main_far, width - 1, width - 2)


def ends(u, b, s, got, main):
    _, width, height, depth = u.shape
    last = height // SUB - 1
    block = pl.BlockSpec((3, width, SUB, depth), lambda i: (0, 0, 0, 0))
    block_last = pl.BlockSpec((3, width, SUB, depth), lambda i: (0, 0, last, 0))
    plane = pl.BlockSpec((width, SUB, depth), lambda i: (0, 0, 0))
    plane_last = pl.BlockSpec((width, SUB, depth), lambda i: (0, last, 0))
    shapes = [(2, 3, width, 2, SUB, LANES), (2, width, 2, SUB, LANES)] + [(10, 2, height + 2 * RIM, LANES)] * 2

    def whole(shape):
        return pl.BlockSpec(shape, lambda i: (0,) * len(shape))

    def field(*lead):
        return pltpu.VMEM((2, *lead, 2, 3 * SUB, LANES), F32)

    def kernel(*refs):
        return ends_kernel(*refs, height)

    return pl.pallas_call(
        kernel,
        grid=(1,),
        in_specs=[block, block_last, block, block_last, plane, plane_last] + [whole(x.shape) for x in (*got, *main)],
        out_specs=[whole(shape) for shape in shapes],
        out_shape=[pltpu.HBM(shape, F32) for shape in shapes[:2]]
        + [jax.ShapeDtypeStruct(shape, F32) for shape in shapes[2:]],
        scratch_shapes=[field(3, width), field(3, width), field(width)],
        compiler_params=params(),
        cost_estimate=cost(40),
        name="ends",
    )(u, u, b, b, s, s, *got, *main)


def full(value):
    return jnp.full((SUB, LANES), value, F32)


def chebyshev_numbers(bounds, steps):
    low, high = full(bounds[0]), full(bounds[1])
    middle = (high + low) / 2.0
    radius = (high - low) / 2.0
    stretch = middle / radius
    rho = 1.0 / stretch
    factors = []
    for _ in range(steps - 1):
        rho_next = 1.0 / (2.0 * stretch - rho)
        factors.append((rho_next * rho, 2.0 * rho_next / radius))
        rho = rho_next
    return 1.0 / middle, factors


def z_matrix(rest_zt):
    shape = (2 * LANES, LANES)
    offset = lax.broadcasted_iota(jnp.int32, shape, 0) - 2 * lax.broadcasted_iota(jnp.int32, shape, 1) + 2
    out = jnp.zeros(shape, F32)
    for a in range(5):
        out = out + jnp.where(offset == a, rest_zt[a : a + 1, :], 0.0)
    return out


def y_weights(rest_y, a, rows, own):
    start = pl.multiple_of(lax.axis_index("narrow") * own, SUB)
    return jnp.broadcast_to(rest_y[pl.ds(start, rows), a : a + 1], (rows, LANES))


def field_shape(height, *lead):
    return (*lead, 2, height + 2 * (RIM + PAD), LANES)


def start_copies(moves, sems):
    copies = [pltpu.make_async_copy(source, to, sems.at[k]) for k, (source, to) in enumerate(moves)]
    for copy in copies:
        copy.start()
    return copies


def inner_kernel(bounds, r0p, s_win, r_end, s_end, r0, s_ext, d1, r1, r2, sems):
    _, width, _, rows, _ = r0p.shape
    height = rows - 2 * RIM
    middle, to_middle = pl.ds(SUB, height - SUB), pl.ds(PAD + SUB, height - SUB)
    to_tile = [pl.ds(PAD, SUB), pl.ds(PAD + height, SUB)]
    moves = [
        (r0p.at[:, :, :, middle, :], r0.at[:, :, :, to_middle, :]),
        (s_win.at[:, :, middle, :], s_ext.at[:, :, to_middle, :]),
    ]
    for e in range(2):
        moves.append((r_end.at[e], r0.at[:, :, :, to_tile[e], :]))
        moves.append((s_end.at[e], s_ext.at[:, :, to_tile[e], :]))
    for copy in start_copies(moves, sems):
        copy.wait()
    edges = edge_masks()
    inverse, factors = chebyshev_numbers(bounds, 2)
    factor_d = factors[0][0] * inverse
    factor_r = factors[0][1]

    def first_step(t, carry):
        start = PAD + t * SUB
        rows = pl.ds(start, SUB)
        inside = inside_rows(t * SUB, height, "narrow")

        def plane(x):
            return Plane(lambda c, dy: [r0[c, x, h, pl.ds(start + dy, SUB), :] for h in range(2)])

        before, here = plane(1), plane(2)
        for x in range(2, width - 2):
            after = plane(x + 1)
            diagonal = [6.0 + s_ext[x, h, rows, :] for h in range(2)]
            ar = applied(before, here, after, diagonal, edges)
            for c in range(3):
                for h in range(2):
                    old = here.v[c][h]
                    new = old - inverse * ar[c][h]
                    d1[c, x - 2, h, rows, :] = jnp.where(inside, factor_d * old + factor_r * new, 0.0)
                    r1[c, x - 2, h, rows, :] = new
            before, here = here, after
        return carry

    lax.fori_loop(0, (height + 2 * RIM) // SUB, first_step, 0, unroll=3)

    def second_step(t, carry):
        start = PAD + RIM + t * SUB
        rows = pl.ds(start, SUB)
        to = pl.ds(pl.multiple_of(t * SUB, SUB), SUB)

        def plane(x):
            return Plane(lambda c, dy: [d1[c, x - 2, h, pl.ds(start + dy, SUB), :] for h in range(2)])

        before, here = plane(2), plane(3)
        for x in range(3, width - 3):
            after = plane(x + 1)
            ad = applied(before, here, after, [6.0 + s_ext[x, h, rows, :] for h in range(2)], edges)
            for c in range(3):
                for h in range(2):
                    r2[c, x - 3, h, to, :] = r1[c, x - 2, h, rows, :] - ad[c][h]
            before, here = here, after
        return carry

    lax.fori_loop(0, height // SUB, second_step, 0, unroll=2)


def inner(bounds, r0p, s_win, r_end, s_end):
    _, width, _, rows, _ = r0p.shape
    height = rows - 2 * RIM
    shapes = [field_shape(height, *lead) for lead in ((3, width), (width,), (3, width - 4), (3, width - 4))]
    shapes.append((3, width - 6, 2, height, LANES))
    return pl.pallas_call(
        inner_kernel,
        in_specs=[SMEM] + [ANY] * 4,
        out_shape=[jax.ShapeDtypeStruct(shape, F32) for shape in shapes],
        scratch_shapes=[pltpu.SemaphoreType.DMA((6,))],
        compiler_params=params(),
        cost_estimate=cost(5),
        name="inner",
    )(bounds, r0p, s_win, r_end, s_end)


def smooth_kernel(
    bounds, rest_x, guess, r0_own, s_ext, d1_own, r1_own, r2_own, got_near, got_far, sent_near, sent_far, rest_y, rest_zt,
    smooth, partial, near, far, left, right, u_left, u_right, r0_rim, d1_rim, r1_rim, r2_rim, t_pad, zr, u, sems,
):
    _, width, height, _ = u.shape
    tiles = (height + 2 * RIM) // SUB
    window = slice(PAD, PAD + height + 2 * RIM)
    even_x = is_even("wide")
    (guess_copy,) = start_copies([(guess, u)], sems)
    zr[0], zr[1] = split(z_matrix(rest_zt))

    def place(from_left, from_right, mine_left, mine_right):
        for k in range(10):
            left[k, :, window, :] = from_left[k]
            right[k, :, window, :] = from_right[k]
        for c in range(3):
            u_left[c, :, window, :] = mine_left[6 + c]
            u_right[c, :, window, :] = mine_right[6 + c]

    @pl.when(even_x)
    def _():
        place(got_far, got_near, sent_far, sent_near)

    @pl.when(jnp.logical_not(even_x))
    def _():
        place(got_near, got_far, sent_near, sent_far)

    def rim(own_ref, first, last, rim_ref, low):
        def pick(c, x):
            if first <= x < last:
                return own_ref.at[c, x - first]
            return rim_ref.at[c, x - low if x < first else x - low - (last - first)]

        return pick

    r0 = rim(r0_own.at[:, 1 : width - 1], 1, width - 1, r0_rim, -2)
    d1 = rim(d1_own, 2, width - 2, d1_rim, -1)
    r1 = rim(r1_own, 2, width - 2, r1_rim, 0)
    r2 = rim(r2_own, 3, width - 3, r2_rim, 0)

    edges = edge_masks()
    place_x = lax.axis_index("wide")
    has_left = place_x > 0
    has_right = place_x < lax.axis_size("wide") - 1
    inverse, factors = chebyshev_numbers(bounds, 2)
    factor_d = factors[0][0] * inverse
    factor_r = factors[0][1]

    def fix(t, carry):
        start = PAD + t * SUB
        rows = pl.ds(start, SUB)
        inside = inside_rows(t * SUB, height, "narrow")

        def of(ref, first):
            return shares(lambda c, dy: [ref[first + c, h, pl.ds(start + dy, SUB), :] for h in range(2)], edges)

        out_left, _ = of(left, 6)
        _, in_left = of(u_left, 0)
        in_right, _ = of(u_right, 0)
        _, out_right = of(right, 6)
        inside_left = inside & has_left
        inside_right = inside & has_right
        for c in range(3):
            for h in range(2):
                r0(c, -2)[h, rows, :] = left[3 + c, h, rows, :]
                r0(c, -1)[h, rows, :] = jnp.where(
                    inside_left, left[c, h, rows, :] + in_left[c][h], 0.0
                )
                r0(c, 0)[h, rows, :] = jnp.where(
                    inside, r0_own[c, 0, h, rows, :] + out_left[c][h], 0.0
                )
                r0(c, width - 1)[h, rows, :] = jnp.where(
                    inside, r0_own[c, width - 1, h, rows, :] + out_right[c][h], 0.0
                )
                r0(c, width)[h, rows, :] = jnp.where(
                    inside_right, right[c, h, rows, :] + in_right[c][h], 0.0
                )
                r0(c, width + 1)[h, rows, :] = right[3 + c, h, rows, :]
        return carry

    lax.fori_loop(0, tiles, fix, 0, unroll=3)

    def first_step(t, carry):
        start = PAD + t * SUB
        rows = pl.ds(start, SUB)
        inside = inside_rows(t * SUB, height, "narrow")

        def plane(x):
            return Plane(lambda c, dy: [r0(c, x)[h, pl.ds(start + dy, SUB), :] for h in range(2)])

        for first in (-1, width - 2):
            before, here = plane(first - 1), plane(first)
            for x in range(first, first + 3):
                after = plane(x + 1)
                keep = inside & has_left if x < 0 else inside & has_right if x == width else inside
                source = left.at[9] if x < 0 else right.at[9] if x == width else s_ext.at[x]
                diagonal = [6.0 + source[h, rows, :] for h in range(2)]
                ar = applied(before, here, after, diagonal, edges)
                for c in range(3):
                    for h in range(2):
                        old = here.v[c][h]
                        new = old - inverse * ar[c][h]
                        d1(c, x)[h, rows, :] = jnp.where(keep, factor_d * old + factor_r * new, 0.0)
                        if 0 <= x < width:
                            r1(c, x)[h, rows, :] = new
                before, here = here, after
        return carry

    lax.fori_loop(0, tiles, first_step, 0, unroll=3)

    def second_step(t, carry):
        start = PAD + RIM + t * SUB
        rows = pl.ds(start, SUB)
        to = pl.ds(pl.multiple_of(t * SUB, SUB), SUB)

        def plane(x):
            return Plane(lambda c, dy: [d1(c, x)[h, pl.ds(start + dy, SUB), :] for h in range(2)])

        for first in (0, width - 3):
            before, here = plane(first - 1), plane(first)
            for x in range(first, first + 3):
                after = plane(x + 1)
                diagonal = [6.0 + s_ext[x, h, rows, :] for h in range(2)]
                ad = applied(before, here, after, diagonal, edges)
                for c in range(3):
                    for h in range(2):
                        r2(c, x)[h, to, :] = r1(c, x)[h, rows, :] - ad[c][h]
                before, here = here, after
        for x in range(width):
            for c in range(3):
                for h in range(2):
                    lanes = slice(h * LANES, (h + 1) * LANES)
                    step = inverse * r0(c, x)[h, rows, :] + d1(c, x)[h, rows, :]
                    smooth[c, x, to, lanes] = u[c, x, to, lanes] + step
        return carry

    guess_copy.wait()
    lax.fori_loop(0, height // SUB, second_step, 0, unroll=2)

    coarse_width = width // 2
    coarse_height = height // 2
    coarse_rows = coarse_height + 2 * RIM
    first_weight = place_x * coarse_width
    lead = 2 * RIM + 2
    zr_halves = zr[0], zr[1]
    for c in range(3):
        for i in range(-1, coarse_width + 1):
            k = c * (coarse_width + 2) + i + 1
            terms = [(a, 2 * i - 2 + a) for a in range(5) if 0 <= 2 * i - 2 + a < width]
            halves = []
            for h in range(2):
                total = None
                for a, x in terms:
                    piece = rest_x[first_weight + i + 1, a] * r2(c, x)[h]
                    total = piece if total is None else total + piece
                halves.append(total)
            joined = jnp.concatenate(halves, axis=1)
            t_pad[k, 0:lead, :] = jnp.zeros((lead, LANES), F32)
            t_pad[k, lead + height :, :] = jnp.zeros((t_pad.shape[1] - lead - height, LANES), F32)
            t_pad[k, lead : lead + height, :] = product(joined, zr_halves, 0)
    weights = [y_weights(rest_y, a, coarse_rows, coarse_height) for a in range(5)]
    even_y = is_even("narrow")
    for c in range(3):
        for i in range(coarse_width + 2):
            k = c * (coarse_width + 2) + i
            total = None
            for a in range(5):
                piece = weights[a] * t_pad[k, pl.ds(a, coarse_rows, stride=2), :]
                total = piece if total is None else total + piece
            partial[c, i] = total

    def send(out, first):
        for c in range(3):
            for i in range(coarse_width + 2):
                k = 5 * (c * (coarse_width + 2) + i)
                out[k : k + 5, :] = partial[c, i, first : first + 5, :]

    @pl.when(even_y)
    def _():
        send(near, coarse_rows - 8)
        send(far, 3)

    @pl.when(jnp.logical_not(even_y))
    def _():
        send(near, 3)
        send(far, coarse_rows - 8)


def split(x):
    high = x.astype(jnp.bfloat16)
    return high, (x - high.astype(F32)).astype(jnp.bfloat16)


def product(x, halves, contract):
    high, low = split(x)
    dims = (((1,), (contract,)), ((), ()))

    def dot(p, q):
        return lax.dot_general(p, q, dims, preferred_element_type=F32)

    return dot(high, halves[0]) + (dot(high, halves[1]) + dot(low, halves[0]))


SMEM = pl.BlockSpec(memory_space=pltpu.SMEM)
VMEM = pl.BlockSpec(memory_space=pltpu.VMEM)
ANY = pl.BlockSpec(memory_space=pl.ANY)


def smoothing(bounds, rest_x, u, own, got, sent, rest_y, rest_zt):
    _, width, height, depth = u.shape
    planes = 3 * (width // 2 + 2)
    coarse_rows = height // 2 + 2 * RIM
    tile = jax.ShapeDtypeStruct((-(-5 * planes // SUB) * SUB, LANES), F32)

    def field(*lead):
        return pltpu.VMEM(field_shape(height, *lead), F32)

    return pl.pallas_call(
        smooth_kernel,
        in_specs=[SMEM, SMEM, ANY] + [VMEM] * 11,
        out_shape=[
            jax.ShapeDtypeStruct((3, width, height, depth), F32),
            jax.ShapeDtypeStruct((3, width // 2 + 2, coarse_rows, LANES), F32),
            tile,
            tile,
        ],
        scratch_shapes=[
            field(10),
            field(10),
            field(3),
            field(3),
            field(3, 6),
            field(3, 6),
            field(3, 4),
            pltpu.VMEM((3, 6, 2, height, LANES), F32),
            pltpu.VMEM((planes, 2 * coarse_rows + 2 * SUB, LANES), F32),
            pltpu.VMEM((2, 2 * LANES, LANES), jnp.bfloat16),
            pltpu.VMEM((3, width, height, depth), F32),
            pltpu.SemaphoreType.DMA((1,)),
        ],
        compiler_params=params(),
        cost_estimate=cost(10),
        name="smoothing",
    )(bounds, rest_x, u, *own, *got, *sent, rest_y, rest_zt)


def rows_kernel(partial, got_near, got_far, s, q, s_win, near, far):
    _, planes, rows, _ = partial.shape
    own = rows - 2 * RIM
    coarse_width = planes - 2
    n = lax.axis_index("narrow")
    even_y = is_even("narrow")
    q[...] = partial[...]

    def join(low, high):
        for c in range(3):
            for i in range(planes):
                k = 5 * (c * planes + i)
                q[c, i, 0:5, :] = partial[c, i, 0:5, :] + low[k : k + 5, :]
                q[c, i, rows - 5 :, :] = partial[c, i, rows - 5 :, :] + high[k : k + 5, :]

    @pl.when(even_y)
    def _():
        join(got_far, got_near)

    @pl.when(jnp.logical_not(even_y))
    def _():
        join(got_near, got_far)

    total = s.shape[1]
    start = pl.multiple_of(n * own, SUB)
    before = pl.multiple_of(jnp.maximum(start - SUB, 0), SUB)
    after = pl.multiple_of(jnp.minimum(start + own, total - SUB), SUB)
    for x in range(coarse_width):
        s_win[x, RIM : RIM + own, :] = s[x, pl.ds(start, own), :]
        s_win[x, 0:RIM, :] = s[x, pl.ds(before, SUB), :][SUB - RIM :, :]
        s_win[x, RIM + own :, :] = s[x, pl.ds(after, SUB), :][0:RIM, :]

    def pack(out, to_left):
        first = 0 if to_left else 2
        for c in range(3):
            for k in range(coarse_width):
                out[c * coarse_width + k] = q[c, first + k]
        edge = 0 if to_left else coarse_width - 2
        for k in range(2):
            out[3 * coarse_width + k] = s_win[edge + k]

    even_x = is_even("wide")

    @pl.when(even_x)
    def _():
        pack(near, False)
        pack(far, True)

    @pl.when(jnp.logical_not(even_x))
    def _():
        pack(near, True)
        pack(far, False)


def rows(partial, got_near, got_far, s):
    _, planes, height, _ = partial.shape
    width = planes - 2
    side = jax.ShapeDtypeStruct((3 * width + 2, height, LANES), F32)
    return pl.pallas_call(
        rows_kernel,
        out_shape=[
            jax.ShapeDtypeStruct(partial.shape, F32),
            jax.ShapeDtypeStruct((width, height, LANES), F32),
            side,
            side,
        ],
        compiler_params=params(),
        cost_estimate=cost(1),
        name="coarse_rows",
    )(partial, got_near, got_far, s)


def coarse_kernel(bounds, q, s_win, got_near, got_far, out, own_out, near, far, left, right, r, d, total, sc):
    _, planes, height, _ = q.shape
    width = planes - 2
    own = height - 2 * RIM
    tiles = height // SUB
    window = slice(PAD, PAD + height)
    even_x = is_even("wide")
    place_x = lax.axis_index("wide")
    has_left = place_x > 0
    has_right = place_x < lax.axis_size("wide") - 1
    inverse, factors = chebyshev_numbers(bounds, 4)
    edges = edge_masks()
    reach = 3

    def place(from_left, from_right):
        left[...] = from_left[...]
        right[...] = from_right[...]

    @pl.when(even_x)
    def _():
        place(got_far, got_near)

    @pl.when(jnp.logical_not(even_x))
    def _():
        place(got_near, got_far)

    for k in range(2):
        sc[k] = left[3 * width + k]
        sc[width + 2 + k] = right[3 * width + k]
    for x in range(width):
        sc[x + 2] = s_win[x]

    def start_rows(t, carry):
        rows = pl.ds(pl.multiple_of(t * SUB, SUB), SUB)
        to = pl.ds(pl.multiple_of(PAD + t * SUB, SUB), SUB)
        for c in range(3):
            for i in range(-reach, width + reach):
                value = None
                if -1 <= i <= width:
                    value = q[c, i + 1, rows, :]
                if i <= 0:
                    other = left[c * width + i + reach, rows, :]
                    value = other if value is None else value + other
                if i >= width - 1:
                    other = right[c * width + i - width + 1, rows, :]
                    value = other if value is None else value + other
                r[c, i + reach, to, :] = value
                first = inverse * value
                d[c, i + reach, to, :] = first
                if 0 <= i < width:
                    total[c, i, to, :] = first
        return carry

    lax.fori_loop(0, tiles, start_rows, 0, unroll=5)

    for k in range(3):
        factor_d, factor_r = factors[k]
        rim = reach - 1 - k

        def residual_step(t, carry, rim=rim):
            start = PAD + t * SUB
            rows = pl.ds(start, SUB)
            inside = inside_rows(t * SUB, own, "narrow")

            def plane(x):
                return Plane(lambda c, dy: [d[c, x + reach, pl.ds(start + dy, SUB), :]])

            before, here = plane(-rim - 1), plane(-rim)
            for x in range(-rim, width + rim):
                after = plane(x + 1)
                keep = inside & has_left if x < 0 else inside & has_right if x >= width else inside
                ad = applied(before, here, after, [6.0 + sc[x + 2, pl.ds(t * SUB, SUB), :]], edges)
                for c in range(3):
                    new = r[c, x + reach, rows, :] - ad[c][0]
                    r[c, x + reach, rows, :] = jnp.where(keep, new, 0.0)
                before, here = here, after
            return carry

        lax.fori_loop(0, tiles, residual_step, 0, unroll=5)

        def direction_step(t, carry, rim=rim, factor_d=factor_d, factor_r=factor_r):
            rows = pl.ds(pl.multiple_of(PAD + t * SUB, SUB), SUB)
            for c in range(3):
                for x in range(-rim, width + rim):
                    new = factor_d * d[c, x + reach, rows, :] + factor_r * r[c, x + reach, rows, :]
                    d[c, x + reach, rows, :] = new
                    if 0 <= x < width:
                        total[c, x, rows, :] = total[c, x, rows, :] + new
            return carry

        lax.fori_loop(0, tiles, direction_step, 0, unroll=5)

    for c in range(3):
        for x in range(width):
            out[c, x] = total[c, x, window, :]
            own_out[c, x] = total[c, x, PAD + RIM : PAD + RIM + own, :]

    def send(ref, x):
        for c in range(3):
            ref[c] = total[c, x, window, :]

    @pl.when(even_x)
    def _():
        send(near, width - 1)
        send(far, 0)

    @pl.when(jnp.logical_not(even_x))
    def _():
        send(near, 0)
        send(far, width - 1)


def coarse_solve(bounds, q, s_win, got_near, got_far):
    _, planes, height, _ = q.shape
    width = planes - 2
    side = (3 * width + 2, height, LANES)
    edge = jax.ShapeDtypeStruct((3, height, LANES), F32)

    def field(count):
        return pltpu.VMEM((3, count, height + 2 * PAD, LANES), F32)

    return pl.pallas_call(
        coarse_kernel,
        in_specs=[SMEM] + [VMEM] * 4,
        out_shape=[
            jax.ShapeDtypeStruct((3, width, height, LANES), F32),
            jax.ShapeDtypeStruct((3, width, height - 2 * RIM, LANES), F32),
            edge,
            edge,
        ],
        scratch_shapes=[
            pltpu.VMEM(side, F32),
            pltpu.VMEM(side, F32),
            field(width + 6),
            field(width + 6),
            field(width),
            pltpu.VMEM((width + 4, height, LANES), F32),
        ],
        compiler_params=params(),
        cost_estimate=cost(3),
        name="coarse_solve",
    )(bounds, q, s_win, got_near, got_far)


def prolong_kernel(rest_x, corr, got_far, got_near, smooth, rest_y, rest_zt, out, left, right, wy, col, grown):
    _, width, height, _ = corr.shape
    own = height - 2 * RIM
    fine_width = 2 * width
    even_x = is_even("wide")
    first_weight = lax.axis_index("wide") * width
    zr = split(z_matrix(rest_zt))
    for a in range(5):
        wy[a] = y_weights(rest_y, a, height, own)

    def place(from_left, from_right):
        left[...] = from_left[...]
        right[...] = from_right[...]

    @pl.when(even_x)
    def _():
        place(got_far, got_near)

    @pl.when(jnp.logical_not(even_x))
    def _():
        place(got_near, got_far)

    def row(c, i):
        return left[c] if i < 0 else right[c] if i == width else corr[c, i]

    for c in range(3):
        for x in range(fine_width):
            total = None
            for a in range(x % 2, 5, 2):
                i = (x + 2 - a) // 2
                piece = rest_x[first_weight + i + 1, a] * row(c, i)
                total = piece if total is None else total + piece
            col[...] = total

            def at(a, shift):
                rows = pl.ds(RIM + shift, own)
                return wy[a, rows, :] * col[rows, :]

            grown[x, pl.ds(0, own, stride=2), :] = at(0, 1) + at(2, 0) + at(4, -1)
            grown[x, pl.ds(1, own, stride=2), :] = at(1, 1) + at(3, 0)
        flat = grown[...].reshape(fine_width * 2 * own, LANES)
        wide = product(flat, zr, 1)
        out[c] = smooth[c] + wide.reshape(fine_width, 2 * own, 2 * LANES)


def prolong(rest_x, corr, got_near, got_far, smooth, rest_y, rest_zt):
    _, width, height, _ = corr.shape
    own = height - 2 * RIM
    return pl.pallas_call(
        prolong_kernel,
        in_specs=[SMEM] + [VMEM] * 6,
        out_shape=jax.ShapeDtypeStruct(smooth.shape, F32),
        scratch_shapes=[
            pltpu.VMEM((3, height, LANES), F32),
            pltpu.VMEM((3, height, LANES), F32),
            pltpu.VMEM((5, height, LANES), F32),
            pltpu.VMEM((height, LANES), F32),
            pltpu.VMEM((2 * width, 2 * own, LANES), F32),
        ],
        compiler_params=params(),
        cost_estimate=cost(12),
        name="prolong",
    )(rest_x, corr, got_near, got_far, smooth, rest_y, rest_zt)


def gather(own, edges, prolonged):
    count = lax.axis_size("narrow")

    def ring(x, by):
        return lax.ppermute(x, "narrow", [(i, (i + by) % count) for i in range(count)])

    after = lax.optimization_barrier
    pair = swap_near(own, "narrow")
    low, high = ring(own, 2), ring(own, -2)
    def across(x, by):
        return lax.ppermute(x, "narrow", [(i, ((i + by) % count) ^ 1) for i in range(count)])

    pair_low, pair_high = across(own, 2), across(own, -2)
    far_edge, near_edge = edges
    first, second, near_edge = after((low, pair_high, near_edge))
    edges = far_edge, near_edge
    far_own, far_pair = ring(first, 2), ring(second, -2)
    result = prolonged(edges)
    return [own, pair_low, high, pair, low, pair_high, far_own, far_pair], result


def assemble_kernel(*refs):
    *blocks, out, sems = refs
    count = len(blocks)
    n = lax.axis_index("narrow")
    m = n + 1 - 2 * lax.rem(n, 2)
    own = blocks[0].shape[2]
    sources = [n, m - 2, n + 2, m, n - 2, m + 2, n - 4, m + 4]
    copies = []
    for k, (block, source) in enumerate(zip(blocks, sources)):
        start = pl.multiple_of(lax.rem(source + count, count) * own, SUB)
        copies.append(pltpu.make_async_copy(block, out.at[:, :, pl.ds(start, own), :], sems.at[k]))
        copies[-1].start()
    for copy in copies:
        copy.wait()


def assemble(blocks):
    three, width, own, lanes = blocks[0].shape
    return pl.pallas_call(
        assemble_kernel,
        in_specs=[ANY] * len(blocks),
        out_specs=ANY,
        out_shape=jax.ShapeDtypeStruct((three, width, own * len(blocks), lanes), F32),
        scratch_shapes=[pltpu.SemaphoreType.DMA((len(blocks),))],
        compiler_params=params(),
        cost_estimate=cost(1),
        name="assemble",
    )(*blocks)


def body(
    right_side,
    start_guess,
    reaction,
    coarse_reaction,
    rest_x,
    rest_y,
    rest_z,
    fine_bounds,
    coarse_bounds,
):
    x_weights = jnp.pad(rest_x, ((1, 1), (0, 0)))
    y_padded = jnp.pad(rest_y, ((RIM, RIM), (0, 0)))
    z_weights = rest_z.T
    from_hbm = [pltpu.with_memory_space_constraint(x, pltpu.HBM) for x in (start_guess, right_side, reaction)]
    got = swap_both(pack_y(*from_hbm), "narrow")
    r0p, s_win, *main = residual(start_guess, right_side, reaction)
    r_end, s_end, *sent = ends(start_guess, right_side, reaction, got, main)
    got = swap_both(sent, "wide")
    waiting = [pltpu.with_memory_space_constraint(x, pltpu.HBM) for x in (r0p, s_win, r_end, s_end)]
    own = inner(fine_bounds, *waiting)
    smooth, partial, *sent = smoothing(fine_bounds, x_weights, start_guess, own, got, sent, y_padded, z_weights)
    got = swap_both(sent, "narrow")
    q, coarse_win, *sent = rows(partial, *got, coarse_reaction)
    got = swap_both(sent, "wide")
    corr, own, *sent = coarse_solve(coarse_bounds, q, coarse_win, *got)
    edges = swap_both(sent, "wide")[::-1]
    blocks, solution_block = gather(
        own, edges, lambda edges: prolong(x_weights, corr, *edges, smooth, y_padded, z_weights)
    )
    return solution_block, assemble(blocks)


def solution(mesh):
    return jax.shard_map(
        body,
        mesh=mesh,
        in_specs=(
            P(None, "wide", "narrow", None),
            P(None, "wide", "narrow", None),
            P("wide", "narrow", None),
            P("wide", None, None),
            P(),
            P(),
            P(),
            P(),
            P(),
        ),
        out_specs=(P(None, "wide", "narrow", None), P(None, "wide", None, None)),
        check_vma=False,
    )
```

```python
import jax
import jax.numpy as jnp
from jax import lax
from jax.experimental import pallas as pl
from jax.experimental.pallas import tpu as pltpu
from jax.sharding import PartitionSpec as P

F32 = jnp.float32
LANES = 128
SUB = 8
RIM = 4
PAD = 8
MIB = 1024 * 1024
BYTES_PER_US = 3_690_000


def params(mib=24):
    return pltpu.CompilerParams(vmem_limit_bytes=mib * MIB)


def cost(us):
    return pl.CostEstimate(flops=0, bytes_accessed=int(us * BYTES_PER_US), transcendentals=0)


def swap_near(x, axis):
    count = lax.axis_size(axis)
    return lax.ppermute(x, axis, [(i, i ^ 1) for i in range(count)])


def swap_far(x, axis):
    count = lax.axis_size(axis)
    up = [(i, i + 1) for i in range(1, count - 1, 2)]
    return lax.ppermute(x, axis, up + [(j, i) for i, j in up])


def swap_both(pair, axis):
    return [swap_near(pair[0], axis), swap_far(pair[1], axis)]


def is_even(axis):
    return lax.rem(lax.axis_index(axis), 2) == 0


def lane_index():
    return lax.broadcasted_iota(jnp.int32, (SUB, LANES), 1)


def z_next(parts, last):
    rolled = [pltpu.roll(part, LANES - 1, 1) for part in parts]
    beyond = rolled[1:] + [jnp.zeros_like(parts[0])]
    return [jnp.where(last, b, r) for r, b in zip(rolled, beyond)]


def z_before(parts, first):
    rolled = [pltpu.roll(part, 1, 1) for part in parts]
    beyond = [jnp.zeros_like(parts[0])] + rolled[:-1]
    return [jnp.where(first, b, r) for r, b in zip(rolled, beyond)]


def each(fn, *lists):
    return [fn(*items) for items in zip(*lists)]


def add(a, b):
    return each(lambda p, q: p + q, a, b)


def sub(a, b):
    return each(lambda p, q: p - q, a, b)


def eighth(a):
    return each(lambda p: 0.125 * p, a)


class Plane:
    def __init__(self, load):
        self.v = [load(c, 0) for c in range(3)]
        above = [load(c, 1) for c in range(3)]
        below = [load(c, -1) for c in range(3)]
        self.along_y = [add(above[c], below[c]) for c in range(3)]
        self.dy = [eighth(sub(above[c], below[c])) for c in range(3)]


def applied(before, plane, after, diagonal, edges):
    first, last = edges
    v, dy = plane.v, plane.dy

    def difference(pick):
        if before is None:
            return pick(after)
        if after is None:
            return each(lambda p: -p, pick(before))
        return sub(pick(after), pick(before))

    slope = [
        eighth(difference(lambda q: q.v[2])),
        dy[2],
        add(eighth(difference(lambda q: q.v[0])), dy[1]),
    ]
    cross = [difference(lambda q: q.dy[1]), difference(lambda q: q.dy[0]), None]
    out = []
    for c in range(3):
        near = plane.along_y[c]
        for other in (before, after):
            if other is not None:
                near = add(near, other.v[c])
        total = each(lambda d, p, q: d * p - q, diagonal, v[c], near)
        if cross[c] is not None:
            total = add(total, cross[c])
        total = add(total, z_next(sub(slope[c], v[c]), last))
        out.append(sub(total, z_before(add(slope[c], v[c]), first)))
    return out


def shares(load, edges):
    first, last = edges
    plane = Plane(load)
    v, dy = plane.v, plane.dy
    along_z = [sub(z_next(v[c], last), z_before(v[c], first)) for c in (0, 2)]
    slope = [add(dy[1], eighth(along_z[1])), dy[0], eighth(along_z[0])]
    return [add(v[c], slope[c]) for c in range(3)], [sub(v[c], slope[c]) for c in range(3)]


def edge_masks():
    lane = lane_index()
    return lane == 0, lane == LANES - 1


def inside_rows(start, own, axis):
    row = start + lax.broadcasted_iota(jnp.int32, (SUB, LANES), 0)
    place = lax.axis_index(axis)
    low = jnp.where(place == 0, RIM, 0)
    high = jnp.where(place == lax.axis_size(axis) - 1, RIM + own, own + 2 * RIM)
    return (row >= low) & (row < high)


def pack_y_kernel(u_lo, u_hi, b_lo, b_hi, s_lo, s_hi, near, far):
    width = u_lo.shape[1]

    def pack(out, u, b, s, low):
        u_rows = slice(0, 3) if low else slice(5, 8)
        two = slice(0, 2) if low else slice(6, 8)
        for h in range(2):
            lanes = slice(h * LANES, (h + 1) * LANES)
            for x in range(width):
                for c in range(3):
                    k = c * width + x
                    out[h, 3 * k : 3 * k + 3, :] = u[c, x, u_rows, lanes]
                    base = 9 * width + 2 * k
                    out[h, base : base + 2, :] = b[c, x, two, lanes]
            out[h, 15 * width :, :] = jnp.concatenate([s[x, two, lanes] for x in range(width)], axis=0)

    even = is_even("narrow")

    @pl.when(even)
    def _():
        pack(near, u_hi, b_hi, s_hi, False)
        pack(far, u_lo, b_lo, s_lo, True)

    @pl.when(jnp.logical_not(even))
    def _():
        pack(near, u_lo, b_lo, s_lo, True)
        pack(far, u_hi, b_hi, s_hi, False)


def pack_y(u, b, s):
    _, width, height, depth = u.shape
    last = height // SUB - 1
    block = pl.BlockSpec((3, width, SUB, depth), lambda i: (0, 0, 0, 0))
    block_last = pl.BlockSpec((3, width, SUB, depth), lambda i: (0, 0, last, 0))
    plane = pl.BlockSpec((width, SUB, depth), lambda i: (0, 0, 0))
    plane_last = pl.BlockSpec((width, SUB, depth), lambda i: (0, last, 0))
    rows = 17 * width
    out = jax.ShapeDtypeStruct((2, rows, LANES), F32)
    whole = pl.BlockSpec((2, rows, LANES), lambda i: (0, 0, 0))
    return pl.pallas_call(
        pack_y_kernel,
        grid=(1,),
        in_specs=[block, block_last, block, block_last, plane, plane_last],
        out_specs=[whole, whole],
        out_shape=[out, out],
        compiler_params=params(),
        cost_estimate=cost(1),
        name="pack_y",
    )(u, u, b, b, s, s)


def residual_kernel(u, b, s, r0, s_out, near, far, ue):
    _, width, height, _ = u.shape
    for h in range(2):
        lanes = slice(h * LANES, (h + 1) * LANES)
        for x in range(width):
            for c in range(3):
                ue[c, x, h, 0:PAD, :] = jnp.zeros((PAD, LANES), F32)
                ue[c, x, h, PAD + height :, :] = jnp.zeros((PAD, LANES), F32)

        def fill(t, carry, h=h, lanes=lanes):
            rows = pl.ds(pl.multiple_of(t * SUB, SUB), SUB)
            to = pl.ds(pl.multiple_of(PAD + t * SUB, SUB), SUB)
            for x in range(width):
                for c in range(3):
                    ue[c, x, h, to, :] = u[c, x, rows, lanes]
            return carry

        lax.fori_loop(0, height // SUB, fill, 0)

    edges = edge_masks()

    def step(t, carry):
        start = PAD + t * SUB
        rows = pl.ds(pl.multiple_of(t * SUB, SUB), SUB)
        to = pl.ds(RIM + t * SUB, SUB)

        def plane(x):
            return Plane(lambda c, dy: [ue[c, x, h, pl.ds(start + dy, SUB), :] for h in range(2)])

        before, here = None, plane(0)
        for x in range(width):
            after = plane(x + 1) if x + 1 < width else None
            au = applied(before, here, after, [6.0 + s[x, rows, h * LANES : (h + 1) * LANES] for h in range(2)], edges)
            for c in range(3):
                for h in range(2):
                    r0[c, x, h, to, :] = b[c, x, rows, h * LANES : (h + 1) * LANES] - au[c][h]
            for h in range(2):
                s_out[x, h, to, :] = s[x, rows, h * LANES : (h + 1) * LANES]
            before, here = here, after
        return carry

    lax.fori_loop(0, height // SUB, step, 0, unroll=2)
    own = slice(RIM, RIM + height)

    def pack(out, edge, second):
        for c in range(3):
            out[c] = r0[c, edge, :, own, :]
            out[3 + c] = r0[c, second, :, own, :]
            out[6 + c] = ue[c, edge, :, PAD : PAD + height, :]
        for h in range(2):
            out[9, h] = s[edge, :, h * LANES : (h + 1) * LANES]

    even_x = is_even("wide")

    @pl.when(even_x)
    def _():
        pack(near, width - 1, width - 2)
        pack(far, 0, 1)

    @pl.when(jnp.logical_not(even_x))
    def _():
        pack(near, 0, 1)
        pack(far, width - 1, width - 2)


def residual(u, b, s):
    _, width, height, _ = u.shape
    side = jax.ShapeDtypeStruct((10, 2, height, LANES), F32)
    return pl.pallas_call(
        residual_kernel,
        out_shape=[
            pltpu.HBM((3, width, 2, height + 2 * RIM, LANES), F32),
            pltpu.HBM((width, 2, height + 2 * RIM, LANES), F32),
            side,
            side,
        ],
        scratch_shapes=[pltpu.VMEM((3, width, 2, height + 2 * PAD, LANES), F32)],
        compiler_params=params(),
        cost_estimate=cost(3),
        name="residual",
    )(u, b, s)


def ends_kernel(
    u_lo, u_hi, b_lo, b_hi, s_lo, s_hi, got_near, got_far, main_near, main_far,
    r_end, s_end, near, far, ue, be, se, own,
):
    width = u_lo.shape[1]
    begin = (PAD + RIM, PAD - RIM)

    def place(e, u, b, s, halo):
        at = begin[e]
        low = e == 0
        three = slice(at - 3, at) if low else slice(at + SUB, at + SUB + 3)
        two = slice(at - 2, at) if low else slice(at + SUB, at + SUB + 2)
        for h in range(2):
            lanes = slice(h * LANES, (h + 1) * LANES)
            coefficient = halo[h, 15 * width :, :]
            for x in range(width):
                for c in range(3):
                    k = c * width + x
                    ue[e, c, x, h, at : at + SUB, :] = u[c, x, :, lanes]
                    be[e, c, x, h, at : at + SUB, :] = b[c, x, :, lanes]
                    ue[e, c, x, h, three, :] = halo[h, 3 * k : 3 * k + 3, :]
                    base = 9 * width + 2 * k
                    be[e, c, x, h, two, :] = halo[h, base : base + 2, :]
                se[e, x, h, at : at + SUB, :] = s[x, :, lanes]
                se[e, x, h, two, :] = coefficient[2 * x : 2 * x + 2, :]

    even = is_even("narrow")

    @pl.when(even)
    def _():
        place(0, u_lo, b_lo, s_lo, got_far)
        place(1, u_hi, b_hi, s_hi, got_near)

    @pl.when(jnp.logical_not(even))
    def _():
        place(0, u_lo, b_lo, s_lo, got_near)
        place(1, u_hi, b_hi, s_hi, got_far)

    edges = edge_masks()

    def step(e, carry):
        inside = inside_rows(e * own + 2 * RIM * e - SUB * e, own, "narrow")

        def plane(x):
            return Plane(lambda c, dy: [ue[e, c, x, h, pl.ds(PAD + dy, SUB), :] for h in range(2)])

        before, here = None, plane(0)
        tile = pl.ds(PAD, SUB)
        for x in range(width):
            after = plane(x + 1) if x + 1 < width else None
            au = applied(before, here, after, [6.0 + se[e, x, h, tile, :] for h in range(2)], edges)
            for c in range(3):
                for h in range(2):
                    r_end[e, c, x, h] = jnp.where(inside, be[e, c, x, h, tile, :] - au[c][h], 0.0)
            for h in range(2):
                s_end[e, x, h] = se[e, x, h, tile, :]
            before, here = here, after
        return carry

    lax.fori_loop(0, 2, step, 0, unroll=2)

    def pack(out, main, edge, second):
        for k in range(10):
            out[k, :, SUB:own, :] = main[k, :, RIM : own - RIM, :]
        for e in range(2):
            tile = slice(e * own, e * own + SUB)
            for h in range(2):
                for c in range(3):
                    out[c, h, tile, :] = r_end[e, c, edge, h]
                    out[3 + c, h, tile, :] = r_end[e, c, second, h]
                    out[6 + c, h, tile, :] = ue[e, c, edge, h, PAD : PAD + SUB, :]
                out[9, h, tile, :] = s_end[e, edge, h]

    even_x = is_even("wide")

    @pl.when(even_x)
    def _():
        pack(near, main_near, width - 1, width - 2)
        pack(far, main_far, 0, 1)

    @pl.when(jnp.logical_not(even_x))
    def _():
        pack(near, main_near, 0, 1)
        pack(far, main_far, width - 1, width - 2)


def ends(u, b, s, got, main):
    _, width, height, depth = u.shape
    last = height // SUB - 1
    block = pl.BlockSpec((3, width, SUB, depth), lambda i: (0, 0, 0, 0))
    block_last = pl.BlockSpec((3, width, SUB, depth), lambda i: (0, 0, last, 0))
    plane = pl.BlockSpec((width, SUB, depth), lambda i: (0, 0, 0))
    plane_last = pl.BlockSpec((width, SUB, depth), lambda i: (0, last, 0))
    shapes = [(2, 3, width, 2, SUB, LANES), (2, width, 2, SUB, LANES)] + [(10, 2, height + 2 * RIM, LANES)] * 2

    def whole(shape):
        return pl.BlockSpec(shape, lambda i: (0,) * len(shape))

    def field(*lead):
        return pltpu.VMEM((2, *lead, 2, 3 * SUB, LANES), F32)

    def kernel(*refs):
        return ends_kernel(*refs, height)

    return pl.pallas_call(
        kernel,
        grid=(1,),
        in_specs=[block, block_last, block, block_last, plane, plane_last] + [whole(x.shape) for x in (*got, *main)],
        out_specs=[whole(shape) for shape in shapes],
        out_shape=[pltpu.HBM(shape, F32) for shape in shapes[:2]]
        + [jax.ShapeDtypeStruct(shape, F32) for shape in shapes[2:]],
        scratch_shapes=[field(3, width), field(3, width), field(width)],
        compiler_params=params(),
        cost_estimate=cost(40),
        name="ends",
    )(u, u, b, b, s, s, *got, *main)


def full(value):
    return jnp.full((SUB, LANES), value, F32)


def chebyshev_numbers(bounds, steps):
    low, high = full(bounds[0]), full(bounds[1])
    middle = (high + low) / 2.0
    radius = (high - low) / 2.0
    stretch = middle / radius
    rho = 1.0 / stretch
    factors = []
    for _ in range(steps - 1):
        rho_next = 1.0 / (2.0 * stretch - rho)
        factors.append((rho_next * rho, 2.0 * rho_next / radius))
        rho = rho_next
    return 1.0 / middle, factors


def z_matrix(rest_zt):
    shape = (2 * LANES, LANES)
    offset = lax.broadcasted_iota(jnp.int32, shape, 0) - 2 * lax.broadcasted_iota(jnp.int32, shape, 1) + 2
    out = jnp.zeros(shape, F32)
    for a in range(5):
        out = out + jnp.where(offset == a, rest_zt[a : a + 1, :], 0.0)
    return out


def y_weights(rest_y, a, rows, own):
    start = pl.multiple_of(lax.axis_index("narrow") * own, SUB)
    return jnp.broadcast_to(rest_y[pl.ds(start, rows), a : a + 1], (rows, LANES))


def field_shape(height, *lead):
    return (*lead, 2, height + 2 * (RIM + PAD), LANES)


def start_copies(moves, sems):
    copies = [pltpu.make_async_copy(source, to, sems.at[k]) for k, (source, to) in enumerate(moves)]
    for copy in copies:
        copy.start()
    return copies


def inner_kernel(bounds, r0p, s_win, r_end, s_end, r0, s_ext, d1, r1, r2, sems):
    _, width, _, rows, _ = r0p.shape
    height = rows - 2 * RIM
    middle, to_middle = pl.ds(SUB, height - SUB), pl.ds(PAD + SUB, height - SUB)
    to_tile = [pl.ds(PAD, SUB), pl.ds(PAD + height, SUB)]
    moves = [
        (r0p.at[:, :, :, middle, :], r0.at[:, :, :, to_middle, :]),
        (s_win.at[:, :, middle, :], s_ext.at[:, :, to_middle, :]),
    ]
    for e in range(2):
        moves.append((r_end.at[e], r0.at[:, :, :, to_tile[e], :]))
        moves.append((s_end.at[e], s_ext.at[:, :, to_tile[e], :]))
    for copy in start_copies(moves, sems):
        copy.wait()
    edges = edge_masks()
    inverse, factors = chebyshev_numbers(bounds, 2)
    factor_d = factors[0][0] * inverse
    factor_r = factors[0][1]

    def first_step(t, carry):
        start = PAD + t * SUB
        rows = pl.ds(start, SUB)
        inside = inside_rows(t * SUB, height, "narrow")

        def plane(x):
            return Plane(lambda c, dy: [r0[c, x, h, pl.ds(start + dy, SUB), :] for h in range(2)])

        before, here = plane(1), plane(2)
        for x in range(2, width - 2):
            after = plane(x + 1)
            diagonal = [6.0 + s_ext[x, h, rows, :] for h in range(2)]
            ar = applied(before, here, after, diagonal, edges)
            for c in range(3):
                for h in range(2):
                    old = here.v[c][h]
                    new = old - inverse * ar[c][h]
                    d1[c, x - 2, h, rows, :] = jnp.where(inside, factor_d * old + factor_r * new, 0.0)
                    r1[c, x - 2, h, rows, :] = new
            before, here = here, after
        return carry

    lax.fori_loop(0, (height + 2 * RIM) // SUB, first_step, 0, unroll=9)

    def second_step(t, carry):
        start = PAD + RIM + t * SUB
        rows = pl.ds(start, SUB)
        to = pl.ds(pl.multiple_of(t * SUB, SUB), SUB)

        def plane(x):
            return Plane(lambda c, dy: [d1[c, x - 2, h, pl.ds(start + dy, SUB), :] for h in range(2)])

        before, here = plane(2), plane(3)
        for x in range(3, width - 3):
            after = plane(x + 1)
            ad = applied(before, here, after, [6.0 + s_ext[x, h, rows, :] for h in range(2)], edges)
            for c in range(3):
                for h in range(2):
                    r2[c, x - 3, h, to, :] = r1[c, x - 2, h, rows, :] - ad[c][h]
            before, here = here, after
        return carry

    lax.fori_loop(0, height // SUB, second_step, 0, unroll=4)


def inner(bounds, r0p, s_win, r_end, s_end):
    _, width, _, rows, _ = r0p.shape
    height = rows - 2 * RIM
    shapes = [field_shape(height, *lead) for lead in ((3, width), (width,), (3, width - 4), (3, width - 4))]
    shapes.append((3, width - 6, 2, height, LANES))
    return pl.pallas_call(
        inner_kernel,
        in_specs=[SMEM] + [ANY] * 4,
        out_shape=[jax.ShapeDtypeStruct(shape, F32) for shape in shapes],
        scratch_shapes=[pltpu.SemaphoreType.DMA((6,))],
        compiler_params=params(),
        cost_estimate=cost(5),
        name="inner",
    )(bounds, r0p, s_win, r_end, s_end)


def smooth_kernel(
    bounds, rest_x, guess, r0_own, s_ext, d1_own, r1_own, r2_own, got_near, got_far, sent_near, sent_far, rest_y, rest_zt,
    smooth, partial, near, far, left, right, u_left, u_right, r0_rim, d1_rim, r1_rim, r2_rim, t_pad, zr, u, sems,
):
    _, width, height, _ = u.shape
    tiles = (height + 2 * RIM) // SUB
    window = slice(PAD, PAD + height + 2 * RIM)
    even_x = is_even("wide")
    (guess_copy,) = start_copies([(guess, u)], sems)
    zr[0], zr[1] = split(z_matrix(rest_zt))

    def place(from_left, from_right, mine_left, mine_right):
        for k in range(10):
            left[k, :, window, :] = from_left[k]
            right[k, :, window, :] = from_right[k]
        for c in range(3):
            u_left[c, :, window, :] = mine_left[6 + c]
            u_right[c, :, window, :] = mine_right[6 + c]

    @pl.when(even_x)
    def _():
        place(got_far, got_near, sent_far, sent_near)

    @pl.when(jnp.logical_not(even_x))
    def _():
        place(got_near, got_far, sent_near, sent_far)

    def rim(own_ref, first, last, rim_ref, low):
        def pick(c, x):
            if first <= x < last:
                return own_ref.at[c, x - first]
            return rim_ref.at[c, x - low if x < first else x - low - (last - first)]

        return pick

    r0 = rim(r0_own.at[:, 1 : width - 1], 1, width - 1, r0_rim, -2)
    d1 = rim(d1_own, 2, width - 2, d1_rim, -1)
    r1 = rim(r1_own, 2, width - 2, r1_rim, 0)
    r2 = rim(r2_own, 3, width - 3, r2_rim, 0)

    edges = edge_masks()
    place_x = lax.axis_index("wide")
    has_left = place_x > 0
    has_right = place_x < lax.axis_size("wide") - 1
    inverse, factors = chebyshev_numbers(bounds, 2)
    factor_d = factors[0][0] * inverse
    factor_r = factors[0][1]

    def fix(t, carry):
        start = PAD + t * SUB
        rows = pl.ds(start, SUB)
        inside = inside_rows(t * SUB, height, "narrow")

        def of(ref, first):
            return shares(lambda c, dy: [ref[first + c, h, pl.ds(start + dy, SUB), :] for h in range(2)], edges)

        out_left, _ = of(left, 6)
        _, in_left = of(u_left, 0)
        in_right, _ = of(u_right, 0)
        _, out_right = of(right, 6)
        inside_left = inside & has_left
        inside_right = inside & has_right
        for c in range(3):
            for h in range(2):
                r0(c, -2)[h, rows, :] = left[3 + c, h, rows, :]
                r0(c, -1)[h, rows, :] = jnp.where(
                    inside_left, left[c, h, rows, :] + in_left[c][h], 0.0
                )
                r0(c, 0)[h, rows, :] = jnp.where(
                    inside, r0_own[c, 0, h, rows, :] + out_left[c][h], 0.0
                )
                r0(c, width - 1)[h, rows, :] = jnp.where(
                    inside, r0_own[c, width - 1, h, rows, :] + out_right[c][h], 0.0
                )
                r0(c, width)[h, rows, :] = jnp.where(
                    inside_right, right[c, h, rows, :] + in_right[c][h], 0.0
                )
                r0(c, width + 1)[h, rows, :] = right[3 + c, h, rows, :]
        return carry

    lax.fori_loop(0, tiles, fix, 0, unroll=9)

    def first_step(t, carry):
        start = PAD + t * SUB
        rows = pl.ds(start, SUB)
        inside = inside_rows(t * SUB, height, "narrow")

        def plane(x):
            return Plane(lambda c, dy: [r0(c, x)[h, pl.ds(start + dy, SUB), :] for h in range(2)])

        for first in (-1, width - 2):
            before, here = plane(first - 1), plane(first)
            for x in range(first, first + 3):
                after = plane(x + 1)
                keep = inside & has_left if x < 0 else inside & has_right if x == width else inside
                source = left.at[9] if x < 0 else right.at[9] if x == width else s_ext.at[x]
                diagonal = [6.0 + source[h, rows, :] for h in range(2)]
                ar = applied(before, here, after, diagonal, edges)
                for c in range(3):
                    for h in range(2):
                        old = here.v[c][h]
                        new = old - inverse * ar[c][h]
                        d1(c, x)[h, rows, :] = jnp.where(keep, factor_d * old + factor_r * new, 0.0)
                        if 0 <= x < width:
                            r1(c, x)[h, rows, :] = new
                before, here = here, after
        return carry

    lax.fori_loop(0, tiles, first_step, 0, unroll=9)

    def second_step(t, carry):
        start = PAD + RIM + t * SUB
        rows = pl.ds(start, SUB)
        to = pl.ds(pl.multiple_of(t * SUB, SUB), SUB)

        def plane(x):
            return Plane(lambda c, dy: [d1(c, x)[h, pl.ds(start + dy, SUB), :] for h in range(2)])

        for first in (0, width - 3):
            before, here = plane(first - 1), plane(first)
            for x in range(first, first + 3):
                after = plane(x + 1)
                diagonal = [6.0 + s_ext[x, h, rows, :] for h in range(2)]
                ad = applied(before, here, after, diagonal, edges)
                for c in range(3):
                    for h in range(2):
                        r2(c, x)[h, to, :] = r1(c, x)[h, rows, :] - ad[c][h]
                before, here = here, after
        for x in range(width):
            for c in range(3):
                for h in range(2):
                    lanes = slice(h * LANES, (h + 1) * LANES)
                    step = inverse * r0(c, x)[h, rows, :] + d1(c, x)[h, rows, :]
                    smooth[c, x, to, lanes] = u[c, x, to, lanes] + step
        return carry

    guess_copy.wait()
    lax.fori_loop(0, height // SUB, second_step, 0, unroll=4)

    coarse_width = width // 2
    coarse_height = height // 2
    coarse_rows = coarse_height + 2 * RIM
    first_weight = place_x * coarse_width
    lead = 2 * RIM + 2
    zr_halves = zr[0], zr[1]
    for c in range(3):
        for i in range(-1, coarse_width + 1):
            k = c * (coarse_width + 2) + i + 1
            terms = [(a, 2 * i - 2 + a) for a in range(5) if 0 <= 2 * i - 2 + a < width]
            halves = []
            for h in range(2):
                total = None
                for a, x in terms:
                    piece = rest_x[first_weight + i + 1, a] * r2(c, x)[h]
                    total = piece if total is None else total + piece
                halves.append(total)
            joined = jnp.concatenate(halves, axis=1)
            t_pad[k, 0:lead, :] = jnp.zeros((lead, LANES), F32)
            t_pad[k, lead + height :, :] = jnp.zeros((t_pad.shape[1] - lead - height, LANES), F32)
            t_pad[k, lead : lead + height, :] = product(joined, zr_halves, 0)
    weights = [y_weights(rest_y, a, coarse_rows, coarse_height) for a in range(5)]
    even_y = is_even("narrow")
    for c in range(3):
        for i in range(coarse_width + 2):
            k = c * (coarse_width + 2) + i
            total = None
            for a in range(5):
                piece = weights[a] * t_pad[k, pl.ds(a, coarse_rows, stride=2), :]
                total = piece if total is None else total + piece
            partial[c, i] = total

    def send(out, first):
        for c in range(3):
            for i in range(coarse_width + 2):
                k = 5 * (c * (coarse_width + 2) + i)
                out[k : k + 5, :] = partial[c, i, first : first + 5, :]

    @pl.when(even_y)
    def _():
        send(near, coarse_rows - 8)
        send(far, 3)

    @pl.when(jnp.logical_not(even_y))
    def _():
        send(near, 3)
        send(far, coarse_rows - 8)


def split(x):
    high = x.astype(jnp.bfloat16)
    return high, (x - high.astype(F32)).astype(jnp.bfloat16)


def product(x, halves, contract):
    high, low = split(x)
    dims = (((1,), (contract,)), ((), ()))

    def dot(p, q):
        return lax.dot_general(p, q, dims, preferred_element_type=F32)

    return dot(high, halves[0]) + (dot(high, halves[1]) + dot(low, halves[0]))


SMEM = pl.BlockSpec(memory_space=pltpu.SMEM)
VMEM = pl.BlockSpec(memory_space=pltpu.VMEM)
ANY = pl.BlockSpec(memory_space=pl.ANY)


def smoothing(bounds, rest_x, u, own, got, sent, rest_y, rest_zt):
    _, width, height, depth = u.shape
    planes = 3 * (width // 2 + 2)
    coarse_rows = height // 2 + 2 * RIM
    tile = jax.ShapeDtypeStruct((-(-5 * planes // SUB) * SUB, LANES), F32)

    def field(*lead):
        return pltpu.VMEM(field_shape(height, *lead), F32)

    return pl.pallas_call(
        smooth_kernel,
        in_specs=[SMEM, SMEM, ANY] + [VMEM] * 11,
        out_shape=[
            jax.ShapeDtypeStruct((3, width, height, depth), F32),
            jax.ShapeDtypeStruct((3, width // 2 + 2, coarse_rows, LANES), F32),
            tile,
            tile,
        ],
        scratch_shapes=[
            field(10),
            field(10),
            field(3),
            field(3),
            field(3, 6),
            field(3, 6),
            field(3, 4),
            pltpu.VMEM((3, 6, 2, height, LANES), F32),
            pltpu.VMEM((planes, 2 * coarse_rows + 2 * SUB, LANES), F32),
            pltpu.VMEM((2, 2 * LANES, LANES), jnp.bfloat16),
            pltpu.VMEM((3, width, height, depth), F32),
            pltpu.SemaphoreType.DMA((1,)),
        ],
        compiler_params=params(),
        cost_estimate=cost(10),
        name="smoothing",
    )(bounds, rest_x, u, *own, *got, *sent, rest_y, rest_zt)


def rows_kernel(partial, got_near, got_far, s, q, s_win, near, far):
    _, planes, rows, _ = partial.shape
    own = rows - 2 * RIM
    coarse_width = planes - 2
    n = lax.axis_index("narrow")
    even_y = is_even("narrow")
    q[...] = partial[...]

    def join(low, high):
        spare = jnp.zeros((SUB - 5, LANES), F32)
        for c in range(3):
            for i in range(planes):
                k = 5 * (c * planes + i)
                q[c, i, 0:SUB, :] = partial[c, i, 0:SUB, :] + jnp.concatenate([low[k : k + 5, :], spare], axis=0)
                q[c, i, rows - SUB :, :] = partial[c, i, rows - SUB :, :] + jnp.concatenate(
                    [spare, high[k : k + 5, :]], axis=0
                )

    @pl.when(even_y)
    def _():
        join(got_far, got_near)

    @pl.when(jnp.logical_not(even_y))
    def _():
        join(got_near, got_far)

    total = s.shape[1]
    start = pl.multiple_of(n * own, SUB)
    before = pl.multiple_of(jnp.maximum(start - SUB, 0), SUB)
    after = pl.multiple_of(jnp.minimum(start + own, total - SUB), SUB)
    for x in range(coarse_width):
        s_win[x] = jnp.concatenate(
            [
                s[x, pl.ds(before, SUB), :][SUB - RIM :, :],
                s[x, pl.ds(start, own), :],
                s[x, pl.ds(after, SUB), :][0:RIM, :],
            ],
            axis=0,
        )

    def pack(out, to_left):
        first = 0 if to_left else 2
        for c in range(3):
            for k in range(coarse_width):
                out[c * coarse_width + k] = q[c, first + k]
        edge = 0 if to_left else coarse_width - 2
        for k in range(2):
            out[3 * coarse_width + k] = s_win[edge + k]

    even_x = is_even("wide")

    @pl.when(even_x)
    def _():
        pack(near, False)
        pack(far, True)

    @pl.when(jnp.logical_not(even_x))
    def _():
        pack(near, True)
        pack(far, False)


def rows(partial, got_near, got_far, s):
    _, planes, height, _ = partial.shape
    width = planes - 2
    side = jax.ShapeDtypeStruct((3 * width + 2, height, LANES), F32)
    return pl.pallas_call(
        rows_kernel,
        out_shape=[
            jax.ShapeDtypeStruct(partial.shape, F32),
            jax.ShapeDtypeStruct((width, height, LANES), F32),
            side,
            side,
        ],
        compiler_params=params(),
        cost_estimate=cost(1),
        name="coarse_rows",
    )(partial, got_near, got_far, s)


def coarse_kernel(bounds, q, s_win, got_near, got_far, out, own_out, near, far, left, right, r, d, total, sc):
    _, planes, height, _ = q.shape
    width = planes - 2
    own = height - 2 * RIM
    tiles = height // SUB
    window = slice(PAD, PAD + height)
    even_x = is_even("wide")
    place_x = lax.axis_index("wide")
    has_left = place_x > 0
    has_right = place_x < lax.axis_size("wide") - 1
    inverse, factors = chebyshev_numbers(bounds, 4)
    edges = edge_masks()
    reach = 3

    def place(from_left, from_right):
        left[...] = from_left[...]
        right[...] = from_right[...]

    @pl.when(even_x)
    def _():
        place(got_far, got_near)

    @pl.when(jnp.logical_not(even_x))
    def _():
        place(got_near, got_far)

    for k in range(2):
        sc[k] = left[3 * width + k]
        sc[width + 2 + k] = right[3 * width + k]
    for x in range(width):
        sc[x + 2] = s_win[x]

    def start_rows(t, carry):
        rows = pl.ds(pl.multiple_of(t * SUB, SUB), SUB)
        to = pl.ds(pl.multiple_of(PAD + t * SUB, SUB), SUB)
        for c in range(3):
            for i in range(-reach, width + reach):
                value = None
                if -1 <= i <= width:
                    value = q[c, i + 1, rows, :]
                if i <= 0:
                    other = left[c * width + i + reach, rows, :]
                    value = other if value is None else value + other
                if i >= width - 1:
                    other = right[c * width + i - width + 1, rows, :]
                    value = other if value is None else value + other
                r[c, i + reach, to, :] = value
                first = inverse * value
                d[c, i + reach, to, :] = first
                if 0 <= i < width:
                    total[c, i, to, :] = first
        return carry

    lax.fori_loop(0, tiles, start_rows, 0, unroll=5)

    for k in range(3):
        factor_d, factor_r = factors[k]
        rim = reach - 1 - k

        def residual_step(t, carry, rim=rim):
            start = PAD + t * SUB
            rows = pl.ds(start, SUB)
            inside = inside_rows(t * SUB, own, "narrow")

            def plane(x):
                return Plane(lambda c, dy: [d[c, x + reach, pl.ds(start + dy, SUB), :]])

            before, here = plane(-rim - 1), plane(-rim)
            for x in range(-rim, width + rim):
                after = plane(x + 1)
                keep = inside & has_left if x < 0 else inside & has_right if x >= width else inside
                ad = applied(before, here, after, [6.0 + sc[x + 2, pl.ds(t * SUB, SUB), :]], edges)
                for c in range(3):
                    new = r[c, x + reach, rows, :] - ad[c][0]
                    r[c, x + reach, rows, :] = jnp.where(keep, new, 0.0)
                before, here = here, after
            return carry

        lax.fori_loop(0, tiles, residual_step, 0, unroll=5)

        def direction_step(t, carry, rim=rim, factor_d=factor_d, factor_r=factor_r):
            rows = pl.ds(pl.multiple_of(PAD + t * SUB, SUB), SUB)
            for c in range(3):
                for x in range(-rim, width + rim):
                    new = factor_d * d[c, x + reach, rows, :] + factor_r * r[c, x + reach, rows, :]
                    d[c, x + reach, rows, :] = new
                    if 0 <= x < width:
                        total[c, x, rows, :] = total[c, x, rows, :] + new
            return carry

        lax.fori_loop(0, tiles, direction_step, 0, unroll=5)

    for c in range(3):
        for x in range(width):
            out[c, x] = total[c, x, window, :]
            own_out[c, x] = total[c, x, PAD + RIM : PAD + RIM + own, :]

    def send(ref, x):
        for c in range(3):
            ref[c] = total[c, x, window, :]

    @pl.when(even_x)
    def _():
        send(near, width - 1)
        send(far, 0)

    @pl.when(jnp.logical_not(even_x))
    def _():
        send(near, 0)
        send(far, width - 1)


def coarse_solve(bounds, q, s_win, got_near, got_far):
    _, planes, height, _ = q.shape
    width = planes - 2
    side = (3 * width + 2, height, LANES)
    edge = jax.ShapeDtypeStruct((3, height, LANES), F32)

    def field(count):
        return pltpu.VMEM((3, count, height + 2 * PAD, LANES), F32)

    return pl.pallas_call(
        coarse_kernel,
        in_specs=[SMEM] + [VMEM] * 4,
        out_shape=[
            jax.ShapeDtypeStruct((3, width, height, LANES), F32),
            jax.ShapeDtypeStruct((3, width, height - 2 * RIM, LANES), F32),
            edge,
            edge,
        ],
        scratch_shapes=[
            pltpu.VMEM(side, F32),
            pltpu.VMEM(side, F32),
            field(width + 6),
            field(width + 6),
            field(width),
            pltpu.VMEM((width + 4, height, LANES), F32),
        ],
        compiler_params=params(),
        cost_estimate=cost(3),
        name="coarse_solve",
    )(bounds, q, s_win, got_near, got_far)


def prolong_kernel(rest_x, corr, got_far, got_near, smooth, rest_y, rest_zt, out, left, right, wy, col, grown):
    _, width, height, _ = corr.shape
    own = height - 2 * RIM
    fine_width = 2 * width
    even_x = is_even("wide")
    first_weight = lax.axis_index("wide") * width
    zr = split(z_matrix(rest_zt))
    for a in range(5):
        wy[a] = y_weights(rest_y, a, height, own)

    def place(from_left, from_right):
        left[...] = from_left[...]
        right[...] = from_right[...]

    @pl.when(even_x)
    def _():
        place(got_far, got_near)

    @pl.when(jnp.logical_not(even_x))
    def _():
        place(got_near, got_far)

    def row(c, i):
        return left[c] if i < 0 else right[c] if i == width else corr[c, i]

    for c in range(3):
        for x in range(fine_width):
            total = None
            for a in range(x % 2, 5, 2):
                i = (x + 2 - a) // 2
                piece = rest_x[first_weight + i + 1, a] * row(c, i)
                total = piece if total is None else total + piece
            col[...] = total

            def at(a, shift):
                rows = pl.ds(RIM + shift, own)
                return wy[a, rows, :] * col[rows, :]

            grown[x, pl.ds(0, own, stride=2), :] = at(0, 1) + at(2, 0) + at(4, -1)
            grown[x, pl.ds(1, own, stride=2), :] = at(1, 1) + at(3, 0)
        flat = grown[...].reshape(fine_width * 2 * own, LANES)
        wide = product(flat, zr, 1)
        out[c] = smooth[c] + wide.reshape(fine_width, 2 * own, 2 * LANES)


def prolong(rest_x, corr, got_near, got_far, smooth, rest_y, rest_zt):
    _, width, height, _ = corr.shape
    own = height - 2 * RIM
    return pl.pallas_call(
        prolong_kernel,
        in_specs=[SMEM] + [VMEM] * 6,
        out_shape=jax.ShapeDtypeStruct(smooth.shape, F32),
        scratch_shapes=[
            pltpu.VMEM((3, height, LANES), F32),
            pltpu.VMEM((3, height, LANES), F32),
            pltpu.VMEM((5, height, LANES), F32),
            pltpu.VMEM((height, LANES), F32),
            pltpu.VMEM((2 * width, 2 * own, LANES), F32),
        ],
        compiler_params=params(),
        cost_estimate=cost(12),
        name="prolong",
    )(rest_x, corr, got_near, got_far, smooth, rest_y, rest_zt)


def gather(own, edges, prolonged):
    count = lax.axis_size("narrow")

    def ring(x, by):
        return lax.ppermute(x, "narrow", [(i, (i + by) % count) for i in range(count)])

    after = lax.optimization_barrier
    pair = swap_near(own, "narrow")
    low, high = ring(own, 2), ring(own, -2)
    def across(x, by):
        return lax.ppermute(x, "narrow", [(i, ((i + by) % count) ^ 1) for i in range(count)])

    pair_low, pair_high = across(own, 2), across(own, -2)
    far_edge, near_edge = edges
    first, second, near_edge = after((low, pair_high, near_edge))
    edges = far_edge, near_edge
    far_own, far_pair = ring(first, 2), ring(second, -2)
    result = prolonged(edges)
    return [own, pair_low, high, pair, low, pair_high, far_own, far_pair], result


def assemble_kernel(*refs):
    *blocks, out, sems = refs
    count = len(blocks)
    n = lax.axis_index("narrow")
    m = n + 1 - 2 * lax.rem(n, 2)
    own = blocks[0].shape[2]
    sources = [n, m - 2, n + 2, m, n - 2, m + 2, n - 4, m + 4]
    copies = []
    for k, (block, source) in enumerate(zip(blocks, sources)):
        start = pl.multiple_of(lax.rem(source + count, count) * own, SUB)
        copies.append(pltpu.make_async_copy(block, out.at[:, :, pl.ds(start, own), :], sems.at[k]))
        copies[-1].start()
    for copy in copies:
        copy.wait()


def assemble(blocks):
    three, width, own, lanes = blocks[0].shape
    return pl.pallas_call(
        assemble_kernel,
        in_specs=[ANY] * len(blocks),
        out_specs=ANY,
        out_shape=jax.ShapeDtypeStruct((three, width, own * len(blocks), lanes), F32),
        scratch_shapes=[pltpu.SemaphoreType.DMA((len(blocks),))],
        compiler_params=params(),
        cost_estimate=cost(1),
        name="assemble",
    )(*blocks)


def body(
    right_side,
    start_guess,
    reaction,
    coarse_reaction,
    rest_x,
    rest_y,
    rest_z,
    fine_bounds,
    coarse_bounds,
):
    x_weights = jnp.pad(rest_x, ((1, 1), (0, 0)))
    y_padded = jnp.pad(rest_y, ((RIM, RIM), (0, 0)))
    z_weights = rest_z.T
    from_hbm = [pltpu.with_memory_space_constraint(x, pltpu.HBM) for x in (start_guess, right_side, reaction)]
    got = swap_both(pack_y(*from_hbm), "narrow")
    r0p, s_win, *main = residual(start_guess, right_side, reaction)
    r_end, s_end, *sent = ends(start_guess, right_side, reaction, got, main)
    got = swap_both(sent, "wide")
    waiting = [pltpu.with_memory_space_constraint(x, pltpu.HBM) for x in (r0p, s_win, r_end, s_end)]
    own = inner(fine_bounds, *waiting)
    smooth, partial, *sent = smoothing(fine_bounds, x_weights, start_guess, own, got, sent, y_padded, z_weights)
    got = swap_both(sent, "narrow")
    q, coarse_win, *sent = rows(partial, *got, coarse_reaction)
    got = swap_both(sent, "wide")
    corr, own, *sent = coarse_solve(coarse_bounds, q, coarse_win, *got)
    edges = swap_both(sent, "wide")[::-1]
    blocks, solution_block = gather(
        own, edges, lambda edges: prolong(x_weights, corr, *edges, smooth, y_padded, z_weights)
    )
    return solution_block, assemble(blocks)


def solution(mesh):
    return jax.shard_map(
        body,
        mesh=mesh,
        in_specs=(
            P(None, "wide", "narrow", None),
            P(None, "wide", "narrow", None),
            P("wide", "narrow", None),
            P("wide", None, None),
            P(),
            P(),
            P(),
            P(),
            P(),
        ),
        out_specs=(P(None, "wide", "narrow", None), P(None, "wide", None, None)),
        check_vma=False,
    )
```
